32 devices in a mesh: box: 8 (over z, y), level: 4 (over x, core).
Axes of the slice: x: 2, y: 2, z: 4, core: 2. Of those that a mesh axis runs over, the one named last changes fastest.
Arguments:
- rhs_field: float32 [4, 128, 128], P(None, 'box'), may hold values from -6 to 6
- self_coef: float32 [128, 128], P('box'), may hold values from 2 to 4
- expand: bfloat16 [128, 256, 128], P('box'), may hold values from -0.5 to 0.5
- near_ops: bfloat16 [26, 128, 128], replicated, may hold values from -0.109375 to 0.109375
- class_ops: bfloat16 [8, 256, 256], P('box', 'level'), may hold values from -0.1875 to 0.1875
- near_src: int32 [128, 26], P('box'), may hold values from 0 to 47
- send_rows: int32 [8, 8, 2], P('box'), may hold values from 0 to 15
- list_slot: int32 [128, 4], P('box'), may hold values from 0 to 15
- list_class: int32 [128, 4], P('box'), may hold values from 0 to 7, all different within a row
Outputs:
- solution: float32 [4, 128, 128], P(None, 'box')
The draws below stay inside these ranges and needn't reach their ends.
Inputs may be any that keep to these rules, and one draw needn't show every extreme that they name: `near_src`: the near-field neighbours of a box lie among the boxes of the index of box before it, its own and the one after it, counted in that order. `send_rows`: each entry is a box of the sending index. `list_slot`: entry q * 2 + j names the j-th row sent by index q of box. `list_class`: the classes of one box's list are distinct.
All inputs are finite; a program needn't handle non-finite values.
Results may differ from the reference program's by a relative error of at most 0.004.
Values may be sent and summed in bfloat16 or wider, within the bound.
No kernel may reach another device: no remote copies, remote signals or barrier semaphores. Data moves between devices by JAX's collectives and lax.ppermute only.
A program may use at most 64 MiB of HBM per device.

```python
import jax
import jax.numpy as jnp
from jax import lax

P_SIZE = 256
PAN = 128
RHS = 4
BOX_DEV = 16
CAP = 2
NNEAR = 26
NBOX = 128
NCLASS = 8
LIST = 4
N_BOX = 8


def plant(entries, rng, least, top_value):
    index_at = [jax.random.randint(jax.random.fold_in(rng, axis), (), 0, length) for axis, length in enumerate(entries.shape)]
    main_axis = entries.shape.index(max(entries.shape))
    next_to = index_at[:main_axis] + [(index_at[main_axis] + 1) % entries.shape[main_axis]] + index_at[main_axis + 1:]
    return entries.at[tuple(index_at)].set(least).at[tuple(next_to)].set(top_value)


def steps_of(key, extent, pieces, smallest, largest):
    factor_of = 1.0
    for position, shards_of in pieces:
        draws = jax.random.uniform(jax.random.fold_in(jax.random.fold_in(key, 6), position), (shards_of,), jnp.float32, smallest / len(pieces), largest / len(pieces))
        factor_of = factor_of * jnp.repeat(jnp.exp(draws), extent[position] // shards_of).reshape((-1,) + (1,) * (len(extent) - 1 - position))
    return factor_of


def choose_distinct(own_key, rows, amount, top, lift):
    order = jax.random.permutation(jax.random.fold_in(own_key, 1), amount)
    pull = order
    for power in range(3):
        pull = pull * pull // amount
    pull = pull * lift // amount
    tickets = jax.random.randint(jax.random.fold_in(own_key, 2), (rows, amount), 0, 4096) + pull
    fixed_rows = jax.random.permutation(jax.random.fold_in(own_key, 3), rows)[jnp.arange(amount) % rows]
    tickets = jnp.where(jnp.arange(rows)[:, None] == fixed_rows[None, :], 1 << 14, tickets)
    merit = tickets * amount + jnp.arange(amount)
    return lax.top_k(merit.astype(jnp.int32), top)[1].astype(jnp.int32)


def gaussian(own_key, extent, width, limit, shards=(), kind=jnp.bfloat16):
    drawn = width * jax.random.normal(own_key, extent, jnp.float32)
    if shards:
        drawn = drawn * steps_of(own_key, extent, shards, -0.22, 0.18)
    return jnp.clip(drawn, -limit, limit).astype(kind)


def setup_inputs(seed: int = 0) -> dict:
    streams_of = jax.random.split(jax.random.key(seed), 10)
    rhs_field = gaussian(streams_of[0], (RHS, NBOX, PAN), 1.0, 6.0, ((1, 8),), jnp.float32)
    self_coef = jnp.clip(2.0 + 2.0 * jax.random.uniform(streams_of[1], (NBOX, PAN), jnp.float32) ** steps_of(streams_of[1], (NBOX, PAN), ((0, 8),), -0.2, 0.2), 2.0, 4.0)
    expand = gaussian(streams_of[2], (NBOX, P_SIZE, PAN), PAN ** -0.5, 0.5, ((0, 8),))
    near_ops = gaussian(streams_of[3], (NNEAR, PAN, PAN), (PAN * NNEAR) ** -0.5, 0.109375)
    class_ops = gaussian(streams_of[4], (NCLASS, P_SIZE, P_SIZE), (P_SIZE * LIST) ** -0.5, 0.1875, ((0, 8), (1, 4)))
    near_src = plant(jax.random.randint(streams_of[5], (NBOX, NNEAR), 0, 3 * BOX_DEV), jax.random.fold_in(streams_of[5], 1), 0, (3 * BOX_DEV) - 1).astype(jnp.int32)
    send_rows = plant(jax.random.randint(streams_of[6], (N_BOX, N_BOX, CAP), 0, BOX_DEV), jax.random.fold_in(streams_of[6], 1), 0, BOX_DEV - 1).astype(jnp.int32)
    list_slot = plant(jax.random.randint(streams_of[7], (NBOX, LIST), 0, N_BOX * CAP), jax.random.fold_in(streams_of[7], 1), 0, (N_BOX * CAP) - 1).astype(jnp.int32)
    list_class = choose_distinct(streams_of[8], NBOX, NCLASS, LIST, 0)
    return {"rhs_field": rhs_field, "self_coef": self_coef, "expand": expand, "near_ops": near_ops, "class_ops": class_ops, "near_src": near_src, "send_rows": send_rows, "list_slot": list_slot, "list_class": list_class}


def build_table(send_rows, list_slot, list_class):
    owner = jnp.arange(NBOX, dtype=jnp.int32) // BOX_DEV
    sender = (list_slot // CAP).astype(jnp.int32)
    place = (list_slot % CAP).astype(jnp.int32)
    global_src = sender * BOX_DEV + send_rows[sender, owner[:, None], place]
    table = jnp.full((NBOX, NCLASS), -1, jnp.int32)
    targets = jnp.broadcast_to(jnp.arange(NBOX, dtype=jnp.int32)[:, None], list_class.shape)
    return table.at[targets, list_class].set(global_src.astype(jnp.int32))

def apply_matrix(field, self_coef, expand, near_ops, class_ops, near_src, table):
    field_half = field.astype(jnp.bfloat16)
    expand_wide = expand.astype(jnp.float32)
    multipoles = jnp.einsum('tpk,rtk->trp', expand_wide, field_half.astype(jnp.float32)).astype(jnp.bfloat16)

    def add_class(number, totals):
        picked = table[:, number]
        sources = jnp.where((picked >= 0)[:, None, None], multipoles[jnp.maximum(picked, 0)], jnp.zeros((), jnp.bfloat16))
        return totals + jnp.einsum('qp,trp->trq', class_ops[number].astype(jnp.float32), sources.astype(jnp.float32))
    local_full = lax.fori_loop(0, NCLASS, add_class, jnp.zeros((NBOX, RHS, P_SIZE), jnp.float32))
    local_half = local_full.astype(jnp.bfloat16)
    far_part = jnp.einsum('tpk,trp->rtk', expand_wide, local_half.astype(jnp.float32))
    owner_start = jnp.arange(NBOX, dtype=jnp.int32) // BOX_DEV * BOX_DEV - BOX_DEV
    near_global = owner_start[:, None] + near_src
    valid = (near_global >= 0) & (near_global < NBOX)
    safe = jnp.clip(near_global, 0, NBOX - 1).astype(jnp.int32)

    def add_near(number, totals):
        chosen = field_half[:, safe[:, number]]
        chosen = jnp.where(valid[:, number][None, :, None], chosen, jnp.zeros((), jnp.bfloat16))
        return totals + jnp.einsum('ij,rtj->rti', near_ops[number].astype(jnp.float32), chosen.astype(jnp.float32))
    near_part = lax.fori_loop(0, NNEAR, add_near, jnp.zeros((RHS, NBOX, PAN), jnp.float32))
    return self_coef[None] * field + near_part + far_part

def inner(first, second):
    return lax.optimization_barrier(jnp.sum(first * second, axis=(1, 2)))

def spread(values, field):
    return values[:, None, None] * field

def reference(rhs_field, self_coef, expand, near_ops, class_ops, near_src, send_rows, list_slot, list_class):
    table = build_table(send_rows, list_slot, list_class)
    beta = jnp.sqrt(inner(rhs_field, rhs_field))
    first = rhs_field / beta[:, None, None]
    image = apply_matrix(first, self_coef, expand, near_ops, class_ops, near_src, table)
    h_one_one = inner(first, image)
    image = image - spread(h_one_one, first)
    h_two_one = jnp.sqrt(inner(image, image))
    second = image / h_two_one[:, None, None]
    image = apply_matrix(second, self_coef, expand, near_ops, class_ops, near_src, table)
    h_one_two = inner(first, image)
    h_two_two = inner(second, image)
    image = image - spread(h_one_two, first) - spread(h_two_two, second)
    h_three_two = jnp.sqrt(inner(image, image))
    gram_aa = h_one_one * h_one_one + h_two_one * h_two_one
    gram_ab = h_one_one * h_one_two + h_two_one * h_two_two
    gram_bb = h_one_two * h_one_two + h_two_two * h_two_two + h_three_two * h_three_two
    right_a = beta * h_one_one
    right_b = beta * h_one_two
    determinant = gram_aa * gram_bb - gram_ab * gram_ab
    coef_a = (gram_bb * right_a - gram_ab * right_b) / determinant
    coef_b = (gram_aa * right_b - gram_ab * right_a) / determinant
    return spread(coef_a, first) + spread(coef_b, second)
```

```python
import functools

import jax
import jax.numpy as jnp
from jax import lax
from jax.experimental import pallas as pl
from jax.experimental.pallas import tpu as pltpu
from jax.sharding import Mesh, PartitionSpec as P

SHIFT = 3.0
LANES = 128
HALF = jnp.bfloat16
FULL = jnp.float32
LIMIT = 48 * 1024 * 1024


def each(count, body):
    if count <= 32:
        for number in range(count):
            body(number)
    else:
        lax.fori_loop(0, count, lambda number, state: (body(number), state)[1], 0)


def fold(count, body, state):
    if count <= 32:
        for number in range(count):
            state = body(number, state)
        return state
    return lax.fori_loop(0, count, body, state)


def dot_nt(left, right):
    return lax.dot_general(left, right, (((1,), (1,)), ((), ())), preferred_element_type=FULL)


def dot_nn(left, right):
    return lax.dot_general(left, right, (((1,), (0,)), ((), ())), preferred_element_type=FULL)


def own_rows(values, result, box, boxes):
    row = lax.broadcasted_iota(jnp.int32, result.shape, 0)
    return jnp.where(row % boxes == box, values, result)


def multipoles_of(field, expand_ref):
    boxes, terms, _ = expand_ref.shape
    result = jnp.zeros((field.shape[0], terms), FULL)
    for box in range(boxes):
        result = own_rows(dot_nt(field, expand_ref[box]), result, box, boxes)
    return result


def put_rows(multipoles, send_ref, rows_ref, picked_ref, boxes):
    rows_ref[...] = multipoles
    picked_ref[...] = jnp.zeros(picked_ref.shape, picked_ref.dtype)
    width, cap = multipoles.shape[0] // boxes, send_ref.shape[2]
    parts = multipoles.shape[1] // LANES

    def put(target):
        for turn in range(cap):
            row = send_ref[0, target, turn]
            for rhs in range(width):
                chosen = rows_ref[pl.ds(rhs * boxes + row, 1), :]
                for part in range(parts):
                    place = (part * width + rhs) * cap + turn
                    picked_ref[target, place : place + 1, :] = chosen[:, part * LANES : (part + 1) * LANES]

    each(send_ref.shape[1], put)


def far_of(local, expand_ref, offset):
    boxes, _, panels = expand_ref.shape
    result = jnp.zeros((local.shape[0], panels), FULL)
    for box in range(boxes):
        rows = expand_ref[box, pl.ds(offset, local.shape[1]), :]
        result = own_rows(dot_nn(local, rows), result, box, boxes)
    return result


def near_of(near_ref, source_ref, extended, boxes, width):
    classes = near_ref.shape[0]
    spots = lax.broadcasted_iota(jnp.int32, (boxes, extended.shape[0]), 1)
    chosen = [
        jnp.where(source_ref[:, number : number + 1] == spots, 1.0, 0.0).astype(HALF)
        for number in range(classes)
    ]
    picked = dot_nn(jnp.concatenate(chosen, axis=0), extended).astype(HALF)
    result = jnp.zeros((width * boxes, near_ref.shape[1]), FULL)
    for number in range(classes):
        rows = picked[number * boxes : (number + 1) * boxes]
        stacked = jnp.concatenate(
            [rows[:, rhs * LANES : (rhs + 1) * LANES] for rhs in range(width)], axis=0
        )
        result = result + dot_nt(stacked, near_ref[number])
    return result


def local_of(bands, slot_ref, class_ref, received, width, cap, offset, band):
    boxes = slot_ref.shape[0]
    area = received.shape[0] // bands[0].shape[0]
    slots = slot_ref[...]
    places = (slots // cap) * area + slots % cap
    labels = class_ref[...]
    parts = bands[0].shape[1] * LANES
    halves = 2
    spots = lax.broadcasted_iota(jnp.int32, (boxes, received.shape[0]), 1)

    def add(number, totals):
        place = jnp.max(jnp.where(labels == number, places + 1, 0), axis=1, keepdims=True) - 1
        totals = list(totals)
        for part in range(halves):
            stacked = []
            for rhs in range(width):
                shift = (part * width + rhs) * cap
                chosen = jnp.where((place >= 0) & (place + shift == spots), 1.0, 0.0).astype(HALF)
                stacked.append(dot_nn(chosen, received).astype(HALF))
            source = jnp.concatenate(stacked, axis=0)
            for which, ref in enumerate(bands):
                rows = ref[number, offset + part * band : offset + (part + 1) * band, :]
                totals[which] = totals[which] + dot_nt(source, rows)
        return tuple(totals)

    empty = tuple(jnp.zeros((width * boxes, band), FULL) for _ in bands)
    return fold(bands[0].shape[0], add, empty)


def extended_of(pieces, index, count, boxes):
    low = jnp.where(index > 0, pieces[0], jnp.zeros_like(pieces[0]))
    high = jnp.where(index < count - 1, pieces[2], jnp.zeros_like(pieces[2]))
    width = low.shape[0] // boxes
    columns = [
        jnp.concatenate([piece[rhs * boxes : (rhs + 1) * boxes] for piece in (low, pieces[1], high)], axis=0)
        for rhs in range(width)
    ]
    return jnp.concatenate(columns, axis=1).astype(HALF)


def paired(own, other, core):
    return jnp.where(core == 0, jnp.concatenate([own, other], axis=1), jnp.concatenate([other, own], axis=1))


def first_kernel(width, rhs_ref, expand_ref, class_ref, send_ref, out_ref, rows_ref, picked_ref):
    boxes, panels = expand_ref.shape[0], expand_ref.shape[2]
    core = lax.axis_index("core")
    field = rhs_ref[pl.ds(core * width, width)].reshape(width * boxes, panels).astype(HALF)
    band = class_ref.shape[1]
    put_rows(multipoles_of(field, expand_ref), send_ref, rows_ref, picked_ref, boxes)
    operators = jnp.concatenate([class_ref[0][:, :LANES], class_ref[0][:, LANES:]], axis=0)
    low = 2 * band
    high = low + width * boxes

    def put(target):
        out_ref[target, :low, :] = operators
        out_ref[target, low:high, :] = field
        out_ref[target, high:, :] = picked_ref[target].astype(HALF)

    each(out_ref.shape[0], put)


def second_kernel(
    width,
    own_ref,
    other_ref,
    rhs_ref,
    self_ref,
    expand_ref,
    near_ref,
    source_ref,
    slot_ref,
    class_ref,
    send_ref,
    out_ref,
    rows_ref,
    picked_ref,
):
    boxes, terms, panels = expand_ref.shape
    count = own_ref.shape[0]
    core, side, index = lax.axis_index("core"), lax.axis_index("side"), lax.axis_index("box")
    low = 2 * (terms // 4)
    high = low + width * boxes
    pieces = [
        own_ref[jnp.clip(index + step, 0, count - 1), low:high, :] for step in (-1, 0, 1)
    ]
    extended = extended_of(pieces, index, count, boxes)
    near = near_of(near_ref, source_ref, extended, boxes, width)
    area = own_ref.shape[1] - high
    received = own_ref[:, high:, :].reshape(count * area, LANES)
    own, other = local_of(
        (own_ref, other_ref), slot_ref, class_ref, received, width, send_ref.shape[2], 0, terms // 4
    )
    local = paired(own, other, core).astype(HALF)
    far = far_of(local, expand_ref, side * (terms // 2))
    field = rhs_ref[pl.ds(core * width, width)]
    diagonal = ((self_ref[...] - SHIFT)[None] * field).reshape(width * boxes, panels)
    image = far + jnp.where(side == 0, near + diagonal, 0.0)
    half = image.astype(HALF)
    put_rows(multipoles_of(half, expand_ref), send_ref, rows_ref, picked_ref, boxes)
    rows = width * boxes

    def put(target):
        block = picked_ref[target].astype(HALF)
        for part in range(2):
            out_ref[2 * target + part, :rows, :] = half
            out_ref[2 * target + part, rows:, :] = block

    each(count, put)


def third_kernel(
    width,
    own_ref,
    other_ref,
    parts_ref,
    self_ref,
    expand_ref,
    near_ref,
    source_ref,
    slot_ref,
    class_ref,
    send_ref,
    far_ref,
    rest_ref,
    field_ref,
):
    boxes, terms, panels = expand_ref.shape
    count = own_ref.shape[0]
    core, side, index = lax.axis_index("core"), lax.axis_index("side"), lax.axis_index("box")
    rows = width * boxes

    def joined(place):
        return parts_ref[2 * place, :rows, :].astype(FULL) + parts_ref[2 * place + 1, :rows, :].astype(FULL)

    pieces = [joined(jnp.clip(index + step, 0, count - 1)) for step in (-1, 0, 1)]
    extended = extended_of(pieces, index, count, boxes)
    near = near_of(near_ref, source_ref, extended, boxes, width)
    area = parts_ref.shape[1] - rows
    blocks = parts_ref[:, rows:, :].reshape(count, 2, area, LANES).astype(FULL)
    received = (blocks[:, 0] + blocks[:, 1]).astype(HALF).reshape(count * area, LANES)
    own, other = local_of(
        (own_ref, other_ref), slot_ref, class_ref, received, width, send_ref.shape[2], 0, terms // 4
    )
    local = paired(own, other, core).astype(HALF)
    far_ref[...] = far_of(local, expand_ref, side * (terms // 2))
    field = pieces[1]
    diagonal = ((self_ref[...] - SHIFT)[None] * field.reshape(width, boxes, panels)).reshape(rows, panels)
    rest_ref[...] = near + diagonal
    field_ref[...] = field


def fourth_kernel(width, rest_ref, far_ref, other_ref, field_ref, rhs_ref, out_ref):
    core = lax.axis_index("core")
    rows, panels = field_ref.shape
    boxes = rows // width
    last = rest_ref[...] + (far_ref[...] + other_ref[...])
    field = field_ref[...]
    right = rhs_ref[pl.ds(core * width, width)].reshape(rows, panels)
    spots = lax.broadcasted_iota(jnp.int32, (8, panels), 0)
    lanes = lax.broadcasted_iota(jnp.int32, (8, panels), 1)
    result = jnp.zeros((8, panels), FULL)
    pairs = ((right, right), (right, field), (field, field), (right, last), (field, last), (last, last))
    for number, (one, two) in enumerate(pairs):
        product = one * two
        for rhs in range(width):
            total = jnp.sum(product[rhs * boxes : (rhs + 1) * boxes])
            mine = (spots == number) & (lanes // (panels // width) == rhs)
            result = jnp.where(mine, total, result)

    def put(target):
        out_ref[target] = result

    each(out_ref.shape[0], put)


def last_kernel(width, sums_ref, field_ref, other_ref, rhs_ref, out_ref):
    core = lax.axis_index("core")
    rows, panels = field_ref.shape
    boxes = rows // width
    fields = (field_ref[...], other_ref[...])
    part = panels // width
    lanes = lax.broadcasted_iota(jnp.int32, (1, panels), 1)
    for group in range(2):
        total = fold(
            sums_ref.shape[0] // 2,
            lambda number, state: state + sums_ref[2 * number + group],
            jnp.zeros(sums_ref.shape[1:], FULL),
        )
        rr, ru, uu, rw, uw, ww = (total[number : number + 1] for number in range(6))
        slope = ru / rr
        norm = uu - slope * ru
        first_row = rw - slope * ru
        scale = lax.rsqrt(rr * norm)
        h11 = slope + SHIFT
        h21 = jnp.sqrt(norm / rr)
        h12 = first_row * scale
        h22 = (uw - slope * uu - slope * first_row) / norm
        image = (ww - 2.0 * slope * uw + slope * slope * uu) / norm
        gram_aa = h11 * h11 + h21 * h21
        gram_ab = h11 * h12 + h21 * (h22 + SHIFT)
        gram_bb = image + 2.0 * SHIFT * h22 + SHIFT * SHIFT
        beta = jnp.sqrt(rr)
        right_a, right_b = beta * h11, beta * h12
        determinant = gram_aa * gram_bb - gram_ab * gram_ab
        coef_a = (gram_bb * right_a - gram_ab * right_b) / determinant
        coef_b = (gram_aa * right_b - gram_ab * right_a) / determinant
        weight = coef_b * lax.rsqrt(norm)
        first = coef_a / beta - weight * slope
        chosen = jnp.where(core == group, fields[0], fields[1])
        for rhs in range(width):
            def wide(value):
                inside = jnp.where(lanes // part == rhs, value, 0.0)
                spread = inside
                for step in range(1, width):
                    spread = spread + pltpu.roll(inside, step * part, 1)
                return spread

            place = group * width + rhs
            out_ref[place] = wide(first) * rhs_ref[place] + wide(weight) * chosen[rhs * boxes : (rhs + 1) * boxes]


def call(kernel, outs, *args, scalars=(), scratch=()):
    vmem = pl.BlockSpec(memory_space=pltpu.VMEM)
    smem = pl.BlockSpec(memory_space=pltpu.SMEM)
    many = isinstance(outs, list)
    return pl.pallas_call(
        kernel,
        out_shape=outs,
        in_specs=[smem if number in scalars else vmem for number in range(len(args))],
        out_specs=[vmem] * len(outs) if many else vmem,
        scratch_shapes=list(scratch),
        compiler_params=pltpu.CompilerParams(vmem_limit_bytes=LIMIT),
    )(*args)


def per_device(
    rhs_field, self_coef, expand, near_ops, class_ops, near_src, send_rows, list_slot, list_class
):
    count = lax.axis_size("box")
    boxes, terms, panels = expand.shape
    width = rhs_field.shape[0] // 2
    rows = width * boxes
    band = class_ops.shape[1]
    cap = send_rows.shape[2]
    area = -(-(cap * width * (terms // LANES)) // 16) * 16
    scratch = [pltpu.VMEM((rows, terms), FULL), pltpu.VMEM((count, area, LANES), FULL)]
    swap = [(0, 1), (1, 0)]

    slots = call(
        functools.partial(first_kernel, width),
        jax.ShapeDtypeStruct((count, 2 * band + rows + area, LANES), HALF),
        rhs_field, expand, class_ops, send_rows,
        scalars=(3,), scratch=scratch,
    )
    own = lax.all_to_all(slots, "box", 0, 0, tiled=True)
    other = lax.ppermute(own, "core", swap)
    parts = call(
        functools.partial(second_kernel, width),
        jax.ShapeDtypeStruct((2 * count, rows + area, LANES), HALF),
        own, other, rhs_field, self_coef, expand, near_ops, near_src, list_slot, list_class, send_rows,
        scalars=(9,), scratch=scratch,
    )
    parts = lax.all_to_all(parts, ("box", "side"), 0, 0, tiled=True)
    block = jax.ShapeDtypeStruct((rows, panels), FULL)
    far, rest, field = call(
        functools.partial(third_kernel, width),
        [block, block, block],
        own, other, parts, self_coef, expand, near_ops, near_src, list_slot, list_class, send_rows,
        scalars=(9,),
    )
    far_other = lax.ppermute(far, "side", swap)
    field_other = lax.ppermute(field, "core", swap)
    sums = call(
        functools.partial(fourth_kernel, width),
        jax.ShapeDtypeStruct((2 * count, 8, panels), FULL),
        rest, far, far_other, field, rhs_field,
    )
    sums = lax.all_to_all(sums, ("box", "core"), 0, 0, tiled=True)
    return call(
        functools.partial(last_kernel, width),
        jax.ShapeDtypeStruct(rhs_field.shape, FULL),
        sums, field, field_other, rhs_field,
    )


def solution(mesh):
    count, levels = mesh.devices.shape
    finer = Mesh(mesh.devices.reshape(count, levels // 2, 2), ("box", "side", "core"))
    return jax.shard_map(
        per_device,
        mesh=finer,
        in_specs=(
            P(None, "box", None),
            P("box", None),
            P("box", None, None),
            P(),
            P("box", ("side", "core"), None),
            P("box", None),
            P("box", None, None),
            P("box", None),
            P("box", None),
        ),
        out_specs=P(None, "box", None),
        check_vma=False,
    )
```

```python
import functools

import jax
import jax.numpy as jnp
from jax import lax
from jax.experimental import pallas as pl
from jax.experimental.pallas import tpu as pltpu
from jax.sharding import Mesh, PartitionSpec as P

SHIFT = 3.0
LANES = 128
HALF = jnp.bfloat16
FULL = jnp.float32
SLOT = pltpu.VMEM


def each(count, body):
    if count <= 32:
        for number in range(count):
            body(number)
    else:
        lax.fori_loop(0, count, lambda number, state: (body(number), state)[1], 0)


def fold(count, body, state):
    if count <= 32:
        for number in range(count):
            state = body(number, state)
        return state
    return lax.fori_loop(0, count, body, state)


def dot_nt(left, right):
    return lax.dot_general(left, right, (((1,), (1,)), ((), ())), preferred_element_type=FULL)


def dot_nn(left, right):
    return lax.dot_general(left, right, (((1,), (0,)), ((), ())), preferred_element_type=FULL)


def own_rows(values, result, box, boxes):
    row = lax.broadcasted_iota(jnp.int32, result.shape, 0)
    return jnp.where(row % boxes == box, values, result)


def multipoles_of(field, expand_ref):
    boxes, terms, _ = expand_ref.shape
    result = jnp.zeros((field.shape[0], terms), FULL)
    for box in range(boxes):
        result = own_rows(dot_nt(field, expand_ref[box]), result, box, boxes)
    return result


def send_table(send_ref, out_ref, boxes, width, parts):
    cap, targets = send_ref.shape
    area = out_ref.shape[0] // targets
    row = lax.broadcasted_iota(jnp.int32, (area, out_ref.shape[1]), 0)
    column = lax.broadcasted_iota(jnp.int32, (area, out_ref.shape[1]), 1)
    start = jnp.where(row < cap * width * parts, (row // cap) * boxes, -boxes)

    def put(target):
        place = start
        for turn in range(cap):
            place = jnp.where(row % cap == turn, start + send_ref[turn, target], place)
        begin = target * area if isinstance(target, int) else pl.multiple_of(target * area, area)
        out_ref[pl.ds(begin, area), :] = jnp.where(place == column, 1.0, 0.0)

    each(targets, put)


def sent_of(multipoles, table):
    half = multipoles.astype(HALF)
    parts = half.shape[1] // LANES
    stacked = jnp.concatenate([half[:, part * LANES : (part + 1) * LANES] for part in range(parts)], axis=0)
    return dot_nn(table, stacked)


def far_of(local, expand_ref, offset):
    boxes, _, panels = expand_ref.shape
    result = jnp.zeros((local.shape[0], panels), FULL)
    for box in range(boxes):
        rows = expand_ref[box, pl.ds(offset, local.shape[1]), :]
        result = own_rows(dot_nn(local, rows), result, box, boxes)
    return result


def near_of(near_ref, chosen_ref, extended, boxes, width):
    picked = dot_nn(chosen_ref[...], extended).astype(HALF)
    result = jnp.zeros((width * boxes, near_ref.shape[1]), FULL)
    for number in range(near_ref.shape[0]):
        rows = picked[number * boxes : (number + 1) * boxes]
        stacked = jnp.concatenate(
            [rows[:, rhs * LANES : (rhs + 1) * LANES] for rhs in range(width)], axis=0
        )
        result = result + dot_nt(stacked, near_ref[number])
    return result


def local_of(bands, table_ref, received, width, boxes, band):
    classes = bands[0].shape[0]
    parts = table_ref.shape[0] // width
    group = min(classes, 8)

    def add(number, total):
        begin = number * group * boxes
        if not isinstance(begin, int):
            begin = pl.multiple_of(begin, group * boxes)
        sources = [
            dot_nn(table_ref[place, pl.ds(begin, group * boxes), :], received).astype(HALF)
            for place in range(parts * width)
        ]
        for turn in range(group):
            rows = slice(turn * boxes, (turn + 1) * boxes)
            left = jnp.concatenate(
                [
                    jnp.concatenate([sources[part * width + rhs][rows] for rhs in range(width)], axis=0)
                    for part in range(parts)
                ],
                axis=1,
            )
            right = jnp.concatenate(
                [
                    jnp.concatenate(
                        [ref[number * group + turn, part * band : (part + 1) * band, :] for part in range(parts)],
                        axis=1,
                    )
                    for ref in bands
                ],
                axis=0,
            )
            total = total + dot_nt(left, right)
        return total

    return fold(classes // group, add, jnp.zeros((width * boxes, len(bands) * band), FULL))


def extended_of(pieces, index, count, boxes):
    low = jnp.where(index > 0, pieces[0], jnp.zeros_like(pieces[0]))
    high = jnp.where(index < count - 1, pieces[2], jnp.zeros_like(pieces[2]))
    width = low.shape[0] // boxes
    columns = [
        jnp.concatenate([piece[rhs * boxes : (rhs + 1) * boxes] for piece in (low, pieces[1], high)], axis=0)
        for rhs in range(width)
    ]
    return jnp.concatenate(columns, axis=1).astype(HALF)


def fetch(pairs, signals):
    copies = [
        pltpu.make_async_copy(source, target, signals.at[number])
        for number, (source, target) in enumerate(pairs)
    ]
    for copy in copies:
        copy.start()
    return copies


def near_table(source_ref, chosen_ref):
    boxes, classes = source_ref.shape
    spots = lax.broadcasted_iota(jnp.int32, (boxes, chosen_ref.shape[1]), 1)
    for number in range(classes):
        match = source_ref[:, number : number + 1] == spots
        chosen_ref[number * boxes : (number + 1) * boxes, :] = jnp.where(match, 1.0, 0.0).astype(HALF)


def list_table(cap, slot_ref, label_ref, table_ref):
    boxes = slot_ref.shape[1]
    kinds = table_ref.shape[1] // boxes
    slots, labels = slot_ref[...], label_ref[...]
    area = table_ref.shape[2] // kinds
    places = (slots // cap) * area + slots % cap
    group = min(kinds, 8)

    def put(number):
        rows = [
            jnp.max(jnp.where(labels == number * group + turn, places + 1, 0), axis=0, keepdims=True) - 1
            for turn in range(group)
        ]
        place = jnp.concatenate(rows, axis=1)
        spot = lax.broadcasted_iota(jnp.int32, (table_ref.shape[2], group * boxes), 0)
        begin = number * group * boxes
        if not isinstance(begin, int):
            begin = pl.multiple_of(begin, group * boxes)
        for which in range(table_ref.shape[0]):
            match = (place >= 0) & (place + which * cap == spot)
            table_ref[which, pl.ds(begin, group * boxes), :] = jnp.where(match, 1.0, 0.0).T.astype(HALF)

    each(kinds // group, put)


def first_kernel(
    width,
    rhs_hbm,
    expand_hbm,
    class_hbm,
    send_hbm,
    near_hbm,
    source_hbm,
    slot_hbm,
    label_hbm,
    out_ref,
    picks_ref,
    expand_ref,
    near_ref,
    chosen_ref,
    table_ref,
    rhs_ref,
    class_ref,
    send_ref,
    wide_ref,
    source_ref,
    slot_ref,
    label_ref,
    signals,
):
    boxes, terms, panels = expand_ref.shape
    core = lax.axis_index("core")
    step = boxes // 4
    pairs = [
        (send_hbm, send_ref),
        (rhs_hbm.at[pl.ds(core * width, width)], rhs_ref),
        (class_hbm, class_ref),
        (source_hbm, source_ref),
        (slot_hbm, slot_ref),
        (label_hbm, label_ref),
    ]
    for quarter in range(4):
        part = pl.ds(quarter * step, step)
        pairs.append((expand_hbm.at[part], expand_ref.at[part]))
    pairs.append((near_hbm, near_ref))
    copies = fetch(pairs, signals)
    copies[0].wait()
    send_table(send_ref, wide_ref, boxes, width, terms // LANES)
    picks_ref[...] = wide_ref[...].astype(HALF)
    band = class_ref.shape[1]
    low = (terms // LANES) * band
    high = low + width * boxes
    copies[1].wait()
    copies[2].wait()
    field = rhs_ref[...].reshape(width * boxes, panels).astype(HALF)
    operators = jnp.concatenate(
        [class_ref[0][:, part * LANES : (part + 1) * LANES] for part in range(terms // LANES)], axis=0
    )

    def put(target):
        out_ref[target, :low, :] = operators
        out_ref[target, low:high, :] = field

    each(out_ref.shape[0], put)
    for copy in copies[3:6]:
        copy.wait()
    near_table(source_ref, chosen_ref)
    list_table(send_ref.shape[0], slot_ref, label_ref, table_ref)
    result = jnp.zeros((width * boxes, terms), FULL)
    for box in range(boxes):
        if box % step == 0:
            copies[6 + box // step].wait()
        result = own_rows(dot_nt(field, expand_ref[box]), result, box, boxes)
    sent = sent_of(result, picks_ref[...]).astype(HALF)
    out_ref[:, high:, :] = sent.reshape(out_ref.shape[0], -1, LANES)
    copies[10].wait()


def base_kernel(width, low, own_ref, rhs_ref, self_ref, near_ref, chosen_ref, out_ref):
    boxes, panels = self_ref.shape
    count = own_ref.shape[0]
    core, side, index = lax.axis_index("core"), lax.axis_index("side"), lax.axis_index("box")
    high = low + width * boxes
    pieces = [own_ref[jnp.clip(index + step, 0, count - 1), low:high, :] for step in (-1, 0, 1)]
    near = near_of(near_ref, chosen_ref, extended_of(pieces, index, count, boxes), boxes, width)
    field = rhs_ref[pl.ds(core * width, width)]
    diagonal = ((self_ref[...] - SHIFT)[None] * field).reshape(width * boxes, panels)
    out_ref[...] = jnp.where(side == 0, near + diagonal, 0.0)


def second_kernel(width, band, own_ref, other_ref, base_ref, expand_ref, table_ref, send_ref, out_ref):
    boxes, terms, panels = expand_ref.shape
    count = own_ref.shape[0]
    core, side = lax.axis_index("core"), lax.axis_index("side")
    rows = width * boxes
    high = (terms // LANES) * band + rows
    received = own_ref[:, high:, :].astype(FULL).reshape(-1, LANES).astype(HALF)
    total = local_of((own_ref, other_ref), table_ref, received, width, boxes, band)
    local = jnp.where(core == 0, total, pltpu.roll(total, band, 1)).astype(HALF)
    image = far_of(local, expand_ref, side * (terms // 2)) + base_ref[...]
    half = image.astype(HALF)
    sent = sent_of(multipoles_of(half, expand_ref), send_ref[...]).astype(HALF).reshape(count, -1, LANES)
    for part in range(2):
        out_ref[:, part, rows:, :] = sent

    def put(target):
        for part in range(2):
            out_ref[target, part, :rows, :] = half

    each(count, put)


def rest_kernel(width, parts_ref, self_ref, near_ref, chosen_ref, rest_ref, field_ref):
    boxes, panels = self_ref.shape
    count = parts_ref.shape[0]
    index = lax.axis_index("box")
    rows = width * boxes

    def joined(place):
        return parts_ref[place, 0, :rows, :].astype(FULL) + parts_ref[place, 1, :rows, :].astype(FULL)

    pieces = [joined(jnp.clip(index + step, 0, count - 1)) for step in (-1, 0, 1)]
    near = near_of(near_ref, chosen_ref, extended_of(pieces, index, count, boxes), boxes, width)
    field = pieces[1]
    diagonal = ((self_ref[...] - SHIFT)[None] * field.reshape(width, boxes, panels)).reshape(rows, panels)
    rest_ref[...] = near + diagonal
    field_ref[...] = field


def third_kernel(
    width,
    band,
    own_ref,
    other_ref,
    across_ref,
    corner_ref,
    parts_ref,
    expand_ref,
    table_ref,
    rest_ref,
    field_ref,
    rhs_ref,
    out_ref,
):
    boxes, terms, panels = expand_ref.shape
    core, side = lax.axis_index("core"), lax.axis_index("side")
    rows = width * boxes
    blocks = parts_ref[:, :, rows:, :].astype(FULL)
    received = (blocks[:, 0] + blocks[:, 1]).reshape(-1, LANES).astype(HALF)
    bands = (own_ref, other_ref, across_ref, corner_ref)
    total = local_of(bands, table_ref, received, width, boxes, band)
    halves = [total[:, : 2 * band], total[:, 2 * band :]]
    halves = [jnp.where(core == 0, half, pltpu.roll(half, band, 1)) for half in halves]
    local = jnp.concatenate(
        [jnp.where(side == 0, halves[0], halves[1]), jnp.where(side == 0, halves[1], halves[0])], axis=1
    ).astype(HALF)
    last = rest_ref[...] + far_of(local, expand_ref, 0)
    field = field_ref[...]
    right = rhs_ref[pl.ds(core * width, width)].reshape(rows, panels)
    spots = lax.broadcasted_iota(jnp.int32, (8, panels), 0)
    lanes = lax.broadcasted_iota(jnp.int32, (8, panels), 1)
    result = jnp.zeros((8, panels), FULL)
    pairs = ((right, right), (right, field), (field, field), (right, last), (field, last), (last, last))
    for number, (one, two) in enumerate(pairs):
        product = one * two
        for rhs in range(width):
            total = jnp.sum(product[rhs * boxes : (rhs + 1) * boxes])
            mine = (spots == number) & (lanes // (panels // width) == rhs)
            result = jnp.where(mine, total, result)

    def put(target):
        out_ref[target] = result

    each(out_ref.shape[0], put)


def last_kernel(width, sums_ref, field_ref, other_ref, rhs_ref, out_ref):
    core = lax.axis_index("core")
    rows, panels = field_ref.shape
    boxes = rows // width
    fields = (field_ref[...], other_ref[...])
    part = panels // width
    lanes = lax.broadcasted_iota(jnp.int32, (1, panels), 1)
    for group in range(2):
        total = fold(
            sums_ref.shape[0] // 2,
            lambda number, state: state + sums_ref[2 * number + group],
            jnp.zeros(sums_ref.shape[1:], FULL),
        )
        rr, ru, uu, rw, uw, ww = (total[number : number + 1] for number in range(6))
        slope = ru / rr
        norm = uu - slope * ru
        first_row = rw - slope * ru
        scale = lax.rsqrt(rr * norm)
        h11 = slope + SHIFT
        h21 = jnp.sqrt(norm / rr)
        h12 = first_row * scale
        h22 = (uw - slope * uu - slope * first_row) / norm
        image = (ww - 2.0 * slope * uw + slope * slope * uu) / norm
        gram_aa = h11 * h11 + h21 * h21
        gram_ab = h11 * h12 + h21 * (h22 + SHIFT)
        gram_bb = image + 2.0 * SHIFT * h22 + SHIFT * SHIFT
        beta = jnp.sqrt(rr)
        right_a, right_b = beta * h11, beta * h12
        determinant = gram_aa * gram_bb - gram_ab * gram_ab
        coef_a = (gram_bb * right_a - gram_ab * right_b) / determinant
        coef_b = (gram_aa * right_b - gram_ab * right_a) / determinant
        weight = coef_b * lax.rsqrt(norm)
        first = coef_a / beta - weight * slope
        chosen = jnp.where(core == group, fields[0], fields[1])
        for rhs in range(width):
            def wide(value):
                inside = jnp.where(lanes // part == rhs, value, 0.0)
                spread = inside
                for step in range(1, width):
                    spread = spread + pltpu.roll(inside, step * part, 1)
                return spread

            place = group * width + rhs
            out_ref[place] = wide(first) * rhs_ref[place] + wide(weight) * chosen[rhs * boxes : (rhs + 1) * boxes]


def call(kernel, outs, *args, fixed=0, scratch=(), flops=0, limit=16):
    vmem = pl.BlockSpec(memory_space=pltpu.VMEM)
    many = isinstance(outs, list)
    held = len(args) - fixed
    args = [
        value if number < held else pltpu.with_memory_space_constraint(value, pltpu.HBM)
        for number, value in enumerate(args)
    ]
    return pl.pallas_call(
        kernel,
        out_shape=outs,
        in_specs=[vmem] * held + [pl.BlockSpec(memory_space=pltpu.HBM)] * fixed,
        out_specs=[vmem] * len(outs) if many else vmem,
        scratch_shapes=list(scratch),
        compiler_params=pltpu.CompilerParams(vmem_limit_bytes=limit * 1024 * 1024),
        cost_estimate=pl.CostEstimate(flops=flops, bytes_accessed=0, transcendentals=0) if flops else None,
    )(*args)


def per_device(
    rhs_field, self_coef, expand, near_ops, class_ops, near_src, send_rows, list_slot, list_class
):
    count = lax.axis_size("box")
    boxes, terms, panels = expand.shape
    width = rhs_field.shape[0] // 2
    rows = width * boxes
    band = class_ops.shape[1]
    cap = send_rows.shape[2]
    parts = terms // LANES
    area = -(-(cap * width * parts) // 8) * 8
    low = parts * band
    swap = [(0, 1), (1, 0)]
    shape = jax.ShapeDtypeStruct
    send = jnp.swapaxes(send_rows, 1, 2)[0]
    slot, label = list_slot.T, list_class.T
    block = shape((rows, panels), FULL)
    kernel = functools.partial(call, limit=16 if count <= 16 else 56)

    slots, picks, kept, near, chosen, table = kernel(
        functools.partial(first_kernel, width),
        [
            shape((count, low + rows + area, LANES), HALF),
            shape((count * area, parts * rows), HALF),
            SLOT(expand.shape, HALF),
            SLOT(near_ops.shape, HALF),
            shape((near_ops.shape[0] * boxes, 3 * boxes), HALF),
            shape((width * parts, count * boxes, count * area), HALF),
        ],
        rhs_field, expand, class_ops, send, near_ops, near_src, slot, label,
        fixed=8,
        scratch=[
            pltpu.VMEM((width,) + rhs_field.shape[1:], FULL),
            pltpu.VMEM(class_ops.shape, HALF),
            pltpu.SMEM(send.shape, jnp.int32),
            pltpu.VMEM((count * area, parts * rows), FULL),
            pltpu.VMEM(near_src.shape, jnp.int32),
            pltpu.VMEM(slot.shape, jnp.int32),
            pltpu.VMEM(label.shape, jnp.int32),
            pltpu.SemaphoreType.DMA((11,)),
        ],
    )
    own = lax.all_to_all(slots, "box", 0, 0, tiled=True)
    bands = own[:, :low]
    other = lax.ppermute(bands, "core", swap)
    across = lax.ppermute(bands, "side", swap)
    corner = lax.ppermute(across, "core", swap)
    base = kernel(
        functools.partial(base_kernel, width, low), block,
        own, rhs_field, self_coef, near, chosen,
        flops=1_000_000_000,
    )
    images = kernel(
        functools.partial(second_kernel, width, band),
        shape((count, 2, rows + area, LANES), HALF),
        own, other, base, kept, table, picks,
    )
    images = images.reshape((2 * count,) + images.shape[2:])
    images = lax.all_to_all(images, ("box", "side"), 0, 0, tiled=True)
    images = images.reshape((count, 2) + images.shape[1:])
    rest, field = kernel(
        functools.partial(rest_kernel, width), [block, block],
        images, self_coef, near, chosen,
        flops=1_000_000_000,
    )
    field_other = lax.ppermute(field, "core", swap)
    sums = kernel(
        functools.partial(third_kernel, width, band),
        SLOT((2 * count, 8, panels), FULL),
        bands, other, across, corner, images, kept, table, rest, field, rhs_field,
    )
    sums = lax.all_to_all(sums, ("box", "core"), 0, 0, tiled=True)
    return kernel(
        functools.partial(last_kernel, width),
        shape(rhs_field.shape, FULL),
        sums, field, field_other, rhs_field,
    )


def solution(mesh):
    count, levels = mesh.devices.shape
    finer = Mesh(mesh.devices.reshape(count, levels // 2, 2), ("box", "side", "core"))
    return jax.shard_map(
        per_device,
        mesh=finer,
        in_specs=(
            P(None, "box", None),
            P("box", None),
            P("box", None, None),
            P(),
            P("box", ("side", "core"), None),
            P("box", None),
            P("box", None, None),
            P("box", None),
            P("box", None),
        ),
        out_specs=P(None, "box", None),
        check_vma=False,
    )
```

```python
import functools

import jax
import jax.numpy as jnp
from jax import lax
from jax.experimental import pallas as pl
from jax.experimental.pallas import tpu as pltpu
from jax.sharding import Mesh, PartitionSpec as P

SHIFT = 3.0
LANES = 128
HALF = jnp.bfloat16
FULL = jnp.float32
SLOT = pltpu.VMEM


def each(count, body):
    if count <= 32:
        for number in range(count):
            body(number)
    else:
        lax.fori_loop(0, count, lambda number, state: (body(number), state)[1], 0)


def fold(count, body, state):
    if count <= 32:
        for number in range(count):
            state = body(number, state)
        return state
    return lax.fori_loop(0, count, body, state)


def dot_nt(left, right):
    return lax.dot_general(left, right, (((1,), (1,)), ((), ())), preferred_element_type=FULL)


def dot_nn(left, right):
    return lax.dot_general(left, right, (((1,), (0,)), ((), ())), preferred_element_type=FULL)


def own_rows(values, result, box, boxes):
    row = lax.broadcasted_iota(jnp.int32, result.shape, 0)
    return jnp.where(row % boxes == box, values, result)


def multipoles_of(field, expand_ref):
    boxes, terms, _ = expand_ref.shape
    result = jnp.zeros((field.shape[0], terms), FULL)
    for box in range(boxes):
        result = own_rows(dot_nt(field, expand_ref[box]), result, box, boxes)
    return result


def send_table(send_ref, out_ref, boxes, width, parts):
    cap, targets = send_ref.shape
    area = out_ref.shape[0] // targets
    row = lax.broadcasted_iota(jnp.int32, (area, out_ref.shape[1]), 0)
    column = lax.broadcasted_iota(jnp.int32, (area, out_ref.shape[1]), 1)
    start = jnp.where(row < cap * width * parts, (row // cap) * boxes, -boxes)

    def put(target):
        place = start
        for turn in range(cap):
            place = jnp.where(row % cap == turn, start + send_ref[turn, target], place)
        begin = target * area if isinstance(target, int) else pl.multiple_of(target * area, area)
        out_ref[pl.ds(begin, area), :] = jnp.where(place == column, 1.0, 0.0)

    each(targets, put)


def sent_of(multipoles, table):
    half = multipoles.astype(HALF)
    parts = half.shape[1] // LANES
    stacked = jnp.concatenate([half[:, part * LANES : (part + 1) * LANES] for part in range(parts)], axis=0)
    return dot_nn(table, stacked)


def far_of(local, expand_ref, offset):
    boxes = expand_ref.shape[0]
    row = lax.broadcasted_iota(jnp.int32, local.shape, 0)
    left = [jnp.where(row % boxes == box, local, jnp.zeros_like(local)) for box in range(boxes)]
    right = [expand_ref[box, pl.ds(offset, local.shape[1]), :] for box in range(boxes)]
    return dot_nn(jnp.concatenate(left, axis=1), jnp.concatenate(right, axis=0))


def near_of(near_ref, chosen_ref, extended, boxes, width):
    picked = dot_nn(chosen_ref[...], extended).astype(HALF)
    classes = near_ref.shape[0]
    result = jnp.zeros((width * boxes, near_ref.shape[1]), FULL)
    for first in range(0, classes, 2):
        group = range(first, min(first + 2, classes))
        left = [
            jnp.concatenate(
                [
                    picked[number * boxes : (number + 1) * boxes, rhs * LANES : (rhs + 1) * LANES]
                    for number in group
                ],
                axis=1,
            )
            for rhs in range(width)
        ]
        right = [near_ref[number] for number in group]
        result = result + dot_nt(jnp.concatenate(left, axis=0), jnp.concatenate(right, axis=1))
    return result


def sources_of(blocks):
    count, area, panels = blocks.shape
    half = area // 2
    pairs = blocks.reshape(count // 2, 2, area, panels)
    low, high = pairs[:, 0], pairs[:, 1]
    row = lax.broadcasted_iota(jnp.int32, low.shape, 1)
    moved_low, moved_high = pltpu.roll(low, half, 1), pltpu.roll(high, half, 1)
    first = jnp.where(row < half, low, moved_high).reshape(-1, panels)
    second = jnp.where(row < half, moved_low, high).reshape(-1, panels)
    return jnp.concatenate([first, second], axis=1).astype(HALF)


def local_of(bands, table_ref, sources, band):
    classes = bands[0].shape[0]
    group = classes // table_ref.shape[0]
    parts = sources.shape[1] // LANES

    def add(number, total):
        images = []
        for turn in range(group):
            right = [
                jnp.concatenate(
                    [ref[number * group + turn, part * band : (part + 1) * band, :] for part in range(parts)],
                    axis=1,
                )
                for ref in bands
            ]
            images.append(dot_nt(sources, jnp.concatenate(right, axis=0)))
        images = jnp.concatenate(images, axis=0)
        upper = images.astype(HALF)
        lower = (images - upper.astype(FULL)).astype(HALF)
        table = table_ref[number]
        return total + (dot_nn(table, upper) + dot_nn(table, lower))

    return fold(table_ref.shape[0], add, jnp.zeros((table_ref.shape[1], len(bands) * band), FULL))


def extended_of(pieces, index, count, boxes):
    low = jnp.where(index > 0, pieces[0], jnp.zeros_like(pieces[0]))
    high = jnp.where(index < count - 1, pieces[2], jnp.zeros_like(pieces[2]))
    width = low.shape[0] // boxes
    columns = [
        jnp.concatenate([piece[rhs * boxes : (rhs + 1) * boxes] for piece in (low, pieces[1], high)], axis=0)
        for rhs in range(width)
    ]
    return jnp.concatenate(columns, axis=1).astype(HALF)


def fetch(pairs, signals):
    copies = [
        pltpu.make_async_copy(source, target, signals.at[number])
        for number, (source, target) in enumerate(pairs)
    ]
    for copy in copies:
        copy.start()
    return copies


def near_table(source_ref, chosen_ref):
    boxes, classes = source_ref.shape
    spots = lax.broadcasted_iota(jnp.int32, (boxes, chosen_ref.shape[1]), 1)
    for number in range(classes):
        match = source_ref[:, number : number + 1] == spots
        chosen_ref[number * boxes : (number + 1) * boxes, :] = jnp.where(match, 1.0, 0.0).astype(HALF)


def list_table(cap, width, kinds, slot_ref, label_ref, table_ref):
    boxes = slot_ref.shape[1]
    groups, rows, columns = table_ref.shape
    slots, labels = slot_ref[...], label_ref[...]
    places = (slots // cap) * (cap * width) + slots % cap
    group = kinds // groups
    received = columns // group

    def put(number):
        blocks = []
        for turn in range(group):
            place = jnp.max(jnp.where(labels == number * group + turn, places + 1, 0), axis=0, keepdims=True) - 1
            place = jnp.concatenate([jnp.where(place >= 0, place + rhs * cap, -1) for rhs in range(width)], axis=1)
            spot = lax.broadcasted_iota(jnp.int32, (received, rows), 0)
            blocks.append(jnp.where(place == spot, 1.0, 0.0))
        table_ref[number] = jnp.concatenate(blocks, axis=0).T.astype(HALF)

    each(groups, put)


def first_kernel(
    width,
    rhs_hbm,
    expand_hbm,
    class_hbm,
    send_hbm,
    near_hbm,
    source_hbm,
    slot_hbm,
    label_hbm,
    out_ref,
    picks_ref,
    expand_ref,
    near_ref,
    chosen_ref,
    table_ref,
    rhs_ref,
    class_ref,
    send_ref,
    wide_ref,
    source_ref,
    slot_ref,
    label_ref,
    signals,
):
    boxes, terms, panels = expand_ref.shape
    core, side = lax.axis_index("core"), lax.axis_index("side")
    step = boxes // 4
    pairs = [
        (send_hbm, send_ref),
        (rhs_hbm.at[pl.ds(core * width, width)], rhs_ref),
        (class_hbm, class_ref),
        (source_hbm, source_ref),
        (slot_hbm, slot_ref),
        (label_hbm, label_ref),
    ]
    for quarter in range(4):
        part = pl.ds(quarter * step, step)
        pairs.append((expand_hbm.at[part], expand_ref.at[part]))
    pairs.append((near_hbm, near_ref))
    copies = fetch(pairs, signals)
    copies[0].wait()
    send_table(send_ref, wide_ref, boxes, width, terms // LANES)
    picks_ref[...] = wide_ref[...].astype(HALF)
    band = class_ref.shape[1]
    low = (terms // LANES) * band
    high = low + width * (boxes // 2)
    copies[1].wait()
    copies[2].wait()
    shown = rhs_ref[:, pl.ds(side * (boxes // 2), boxes // 2), :].reshape(high - low, panels).astype(HALF)
    field = rhs_ref[...].reshape(width * boxes, panels).astype(HALF)
    operators = jnp.concatenate(
        [class_ref[0][:, part * LANES : (part + 1) * LANES] for part in range(terms // LANES)], axis=0
    )

    def put(target):
        out_ref[target, :low, :] = operators
        out_ref[target, low:high, :] = shown

    each(out_ref.shape[0], put)
    for copy in copies[3:6]:
        copy.wait()
    near_table(source_ref, chosen_ref)
    list_table(send_ref.shape[0], width, out_ref.shape[0], slot_ref, label_ref, table_ref)
    result = jnp.zeros((width * boxes, terms), FULL)
    for box in range(boxes):
        if box % step == 0:
            copies[6 + box // step].wait()
        result = own_rows(dot_nt(field, expand_ref[box]), result, box, boxes)
    sent = sent_of(result, picks_ref[...]).astype(HALF)
    out_ref[:, high:, :] = sent.reshape(out_ref.shape[0], -1, LANES)
    copies[10].wait()


def base_kernel(width, low, own_ref, rhs_ref, self_ref, near_ref, chosen_ref, out_ref):
    boxes, panels = self_ref.shape
    count = own_ref.shape[0]
    core, side, index = lax.axis_index("core"), lax.axis_index("side"), lax.axis_index("box")
    half = boxes // 2
    empty = jnp.zeros((half, panels), FULL)
    pieces = []
    for step in (-1, 0, 1):
        shown = own_ref[jnp.clip(index + step, 0, count - 1), low : low + width * half, :].astype(FULL)
        rows = []
        for rhs in range(width):
            part = shown[rhs * half : (rhs + 1) * half]
            rows += [jnp.where(side == 0, part, empty), jnp.where(side == 0, empty, part)]
        pieces.append(jnp.concatenate(rows, axis=0))
    near = near_of(near_ref, chosen_ref, extended_of(pieces, index, count, boxes), boxes, width)
    field = rhs_ref[pl.ds(core * width, width)]
    diagonal = ((self_ref[...] - SHIFT)[None] * field).reshape(width * boxes, panels)
    out_ref[...] = near + jnp.where(side == 0, diagonal, 0.0)


def second_kernel(width, band, own_ref, other_ref, base_ref, expand_ref, table_ref, send_ref, out_ref):
    boxes, terms, panels = expand_ref.shape
    count = own_ref.shape[0]
    core, side = lax.axis_index("core"), lax.axis_index("side")
    rows = width * boxes
    high = (terms // LANES) * band + rows // 2
    sources = sources_of(own_ref[:, high:, :].astype(FULL))
    total = local_of((own_ref, other_ref), table_ref, sources, band)
    local = jnp.where(core == 0, total, pltpu.roll(total, band, 1)).astype(HALF)
    image = far_of(local, expand_ref, side * (terms // 2)) + base_ref[...]
    half = image.astype(HALF)
    sent = sent_of(multipoles_of(half, expand_ref), send_ref[...]).astype(HALF).reshape(count, -1, LANES)
    for part in range(2):
        out_ref[:, part, rows:, :] = sent

    def put(target):
        for part in range(2):
            out_ref[target, part, :rows, :] = half

    each(count, put)


def rest_kernel(width, parts_ref, self_ref, near_ref, chosen_ref, rest_ref, field_ref):
    boxes, panels = self_ref.shape
    count = parts_ref.shape[0]
    index = lax.axis_index("box")
    rows = width * boxes

    def joined(place):
        return parts_ref[place, 0, :rows, :].astype(FULL) + parts_ref[place, 1, :rows, :].astype(FULL)

    pieces = [joined(jnp.clip(index + step, 0, count - 1)) for step in (-1, 0, 1)]
    near = near_of(near_ref, chosen_ref, extended_of(pieces, index, count, boxes), boxes, width)
    field = pieces[1]
    diagonal = ((self_ref[...] - SHIFT)[None] * field.reshape(width, boxes, panels)).reshape(rows, panels)
    rest_ref[...] = near + diagonal
    field_ref[...] = field


def third_kernel(
    width,
    band,
    own_ref,
    other_ref,
    across_ref,
    corner_ref,
    parts_ref,
    expand_ref,
    table_ref,
    rest_ref,
    field_ref,
    rhs_ref,
    out_ref,
):
    boxes, terms, panels = expand_ref.shape
    core, side = lax.axis_index("core"), lax.axis_index("side")
    rows = width * boxes
    blocks = parts_ref[:, :, rows:, :].astype(FULL)
    sources = sources_of(blocks[:, 0] + blocks[:, 1])
    bands = (own_ref, other_ref, across_ref, corner_ref)
    total = local_of(bands, table_ref, sources, band)
    halves = [total[:, : 2 * band], total[:, 2 * band :]]
    halves = [jnp.where(core == 0, half, pltpu.roll(half, band, 1)) for half in halves]
    local = jnp.concatenate(
        [jnp.where(side == 0, halves[0], halves[1]), jnp.where(side == 0, halves[1], halves[0])], axis=1
    ).astype(HALF)
    last = rest_ref[...] + far_of(local, expand_ref, 0)
    field = field_ref[...]
    right = rhs_ref[pl.ds(core * width, width)].reshape(rows, panels)
    spots = lax.broadcasted_iota(jnp.int32, (8, panels), 0)
    lanes = lax.broadcasted_iota(jnp.int32, (8, panels), 1)
    result = jnp.zeros((8, panels), FULL)
    pairs = ((right, right), (right, field), (field, field), (right, last), (field, last), (last, last))
    for number, (one, two) in enumerate(pairs):
        product = one * two
        for rhs in range(width):
            total = jnp.sum(product[rhs * boxes : (rhs + 1) * boxes])
            mine = (spots == number) & (lanes // (panels // width) == rhs)
            result = jnp.where(mine, total, result)

    def put(target):
        out_ref[target] = result

    each(out_ref.shape[0], put)


def last_kernel(width, sums_ref, field_ref, other_ref, rhs_ref, out_ref):
    core = lax.axis_index("core")
    rows, panels = field_ref.shape
    boxes = rows // width
    fields = (field_ref[...], other_ref[...])
    part = panels // width
    lanes = lax.broadcasted_iota(jnp.int32, (1, panels), 1)
    for group in range(2):
        total = fold(
            sums_ref.shape[0] // 2,
            lambda number, state: state + sums_ref[2 * number + group],
            jnp.zeros(sums_ref.shape[1:], FULL),
        )
        rr, ru, uu, rw, uw, ww = (total[number : number + 1] for number in range(6))
        slope = ru / rr
        norm = uu - slope * ru
        first_row = rw - slope * ru
        scale = lax.rsqrt(rr * norm)
        h11 = slope + SHIFT
        h21 = jnp.sqrt(norm / rr)
        h12 = first_row * scale
        h22 = (uw - slope * uu - slope * first_row) / norm
        image = (ww - 2.0 * slope * uw + slope * slope * uu) / norm
        gram_aa = h11 * h11 + h21 * h21
        gram_ab = h11 * h12 + h21 * (h22 + SHIFT)
        gram_bb = image + 2.0 * SHIFT * h22 + SHIFT * SHIFT
        beta = jnp.sqrt(rr)
        right_a, right_b = beta * h11, beta * h12
        determinant = gram_aa * gram_bb - gram_ab * gram_ab
        coef_a = (gram_bb * right_a - gram_ab * right_b) / determinant
        coef_b = (gram_aa * right_b - gram_ab * right_a) / determinant
        weight = coef_b * lax.rsqrt(norm)
        first = coef_a / beta - weight * slope
        chosen = jnp.where(core == group, fields[0], fields[1])
        for rhs in range(width):
            def wide(value):
                inside = jnp.where(lanes // part == rhs, value, 0.0)
                spread = inside
                for step in range(1, width):
                    spread = spread + pltpu.roll(inside, step * part, 1)
                return spread

            place = group * width + rhs
            out_ref[place] = wide(first) * rhs_ref[place] + wide(weight) * chosen[rhs * boxes : (rhs + 1) * boxes]


def call(kernel, outs, *args, fixed=0, scratch=(), flops=0, limit=16):
    vmem = pl.BlockSpec(memory_space=pltpu.VMEM)
    many = isinstance(outs, list)
    held = len(args) - fixed
    args = [
        value if number < held else pltpu.with_memory_space_constraint(value, pltpu.HBM)
        for number, value in enumerate(args)
    ]
    return pl.pallas_call(
        kernel,
        out_shape=outs,
        in_specs=[vmem] * held + [pl.BlockSpec(memory_space=pltpu.HBM)] * fixed,
        out_specs=[vmem] * len(outs) if many else vmem,
        scratch_shapes=list(scratch),
        compiler_params=pltpu.CompilerParams(vmem_limit_bytes=limit * 1024 * 1024),
        cost_estimate=pl.CostEstimate(flops=flops, bytes_accessed=0, transcendentals=0) if flops else None,
    )(*args)


def per_device(
    rhs_field, self_coef, expand, near_ops, class_ops, near_src, send_rows, list_slot, list_class
):
    count = lax.axis_size("box")
    boxes, terms, panels = expand.shape
    width = rhs_field.shape[0] // 2
    rows = width * boxes
    band = class_ops.shape[1]
    cap = send_rows.shape[2]
    parts = terms // LANES
    area = -(-(cap * width * parts) // 8) * 8
    low = parts * band
    swap = [(0, 1), (1, 0)]
    shape = jax.ShapeDtypeStruct
    send = jnp.swapaxes(send_rows, 1, 2)[0]
    slot, label = list_slot.T, list_class.T
    block = shape((rows, panels), FULL)
    kernel = functools.partial(call, limit=16 if count <= 16 else 56)

    slots, picks, kept, near, chosen, table = kernel(
        functools.partial(first_kernel, width),
        [
            shape((count, low + rows // 2 + area, LANES), HALF),
            shape((count * area, parts * rows), HALF),
            SLOT(expand.shape, HALF),
            SLOT(near_ops.shape, HALF),
            shape((near_ops.shape[0] * boxes, 3 * boxes), HALF),
            shape((-(-count // 8), rows, min(count, 8) * count * cap * width), HALF),
        ],
        rhs_field, expand, class_ops, send, near_ops, near_src, slot, label,
        fixed=8,
        scratch=[
            pltpu.VMEM((width,) + rhs_field.shape[1:], FULL),
            pltpu.VMEM(class_ops.shape, HALF),
            pltpu.SMEM(send.shape, jnp.int32),
            pltpu.VMEM((count * area, parts * rows), FULL),
            pltpu.VMEM(near_src.shape, jnp.int32),
            pltpu.VMEM(slot.shape, jnp.int32),
            pltpu.VMEM(label.shape, jnp.int32),
            pltpu.SemaphoreType.DMA((11,)),
        ],
    )
    own = lax.all_to_all(slots, "box", 0, 0, tiled=True)
    bands = own[:, :low]
    other = lax.ppermute(bands, "core", swap)
    across = lax.ppermute(bands, "side", swap)
    corner = lax.ppermute(across, "core", swap)
    base = kernel(
        functools.partial(base_kernel, width, low), block,
        own, rhs_field, self_coef, near, chosen,
        flops=1_000_000_000,
    )
    images = kernel(
        functools.partial(second_kernel, width, band),
        shape((count, 2, rows + area, LANES), HALF),
        own, other, base, kept, table, picks,
    )
    images = images.reshape((2 * count,) + images.shape[2:])
    images = lax.all_to_all(images, ("box", "side"), 0, 0, tiled=True)
    images = images.reshape((count, 2) + images.shape[1:])
    rest, field = kernel(
        functools.partial(rest_kernel, width), [block, block],
        images, self_coef, near, chosen,
        flops=1_000_000_000,
    )
    field_other = lax.ppermute(field, "core", swap)
    sums = kernel(
        functools.partial(third_kernel, width, band),
        SLOT((2 * count, 8, panels), FULL),
        bands, other, across, corner, images, kept, table, rest, field, rhs_field,
    )
    sums, field_other = lax.optimization_barrier((sums, field_other))
    sums = lax.all_to_all(sums, ("box", "core"), 0, 0, tiled=True)
    return kernel(
        functools.partial(last_kernel, width),
        shape(rhs_field.shape, FULL),
        sums, field, field_other, rhs_field,
    )


def solution(mesh):
    count, levels = mesh.devices.shape
    finer = Mesh(mesh.devices.reshape(count, levels // 2, 2), ("box", "side", "core"))
    return jax.shard_map(
        per_device,
        mesh=finer,
        in_specs=(
            P(None, "box", None),
            P("box", None),
            P("box", None, None),
            P(),
            P("box", ("side", "core"), None),
            P("box", None),
            P("box", None, None),
            P("box", None),
            P("box", None),
        ),
        out_specs=P(None, "box", None),
        check_vma=False,
    )
```

```python
import functools

import jax
import jax.numpy as jnp
from jax import lax
from jax.experimental import pallas as pl
from jax.experimental.pallas import tpu as pltpu
from jax.sharding import Mesh, PartitionSpec as P

SHIFT = 3.0
LANES = 128
HALF = jnp.bfloat16
FULL = jnp.float32
SLOT = pltpu.VMEM
FIRST = {8: (2, 4, 6, 0, 5, 1, 7, 3)}
SECOND = {16: (10, 3, 8, 6, 15, 4, 13, 14, 12, 11, 9, 7, 2, 1, 0, 5)}
THIRD = {16: (7, 9, 3, 14, 4, 12, 13, 10, 1, 8, 11, 2, 15, 6, 5, 0)}


def spot(order, member):
    if order is None:
        return member
    if isinstance(member, int):
        return order.index(member)
    result = jnp.zeros_like(member)
    for number, value in enumerate(order):
        result = jnp.where(member == value, number, result)
    return result


def exchange(value, axes, order):
    groups = None if order is None else [list(order)]
    return lax.all_to_all(value, axes, 0, 0, tiled=True, axis_index_groups=groups)


def each(count, body):
    if count <= 32:
        for number in range(count):
            body(number)
    else:
        lax.fori_loop(0, count, lambda number, state: (body(number), state)[1], 0)


def fold(count, body, state):
    if count <= 32:
        for number in range(count):
            state = body(number, state)
        return state
    return lax.fori_loop(0, count, body, state)


def dot_nt(left, right):
    return lax.dot_general(left, right, (((1,), (1,)), ((), ())), preferred_element_type=FULL)


def dot_nn(left, right):
    return lax.dot_general(left, right, (((1,), (0,)), ((), ())), preferred_element_type=FULL)


def own_rows(values, result, box, boxes):
    row = lax.broadcasted_iota(jnp.int32, result.shape, 0)
    return jnp.where(row % boxes == box, values, result)


def multipoles_of(field, expand_ref):
    boxes, terms, _ = expand_ref.shape
    result = jnp.zeros((field.shape[0], terms), FULL)
    for box in range(boxes):
        result = own_rows(dot_nt(field, expand_ref[box]), result, box, boxes)
    return result


def send_table(order, send_ref, out_ref, boxes, width, parts):
    cap, targets = send_ref.shape
    area = out_ref.shape[0] // targets
    row = lax.broadcasted_iota(jnp.int32, (area, out_ref.shape[1]), 0)
    column = lax.broadcasted_iota(jnp.int32, (area, out_ref.shape[1]), 1)
    start = jnp.where(row < cap * width * parts, (row // cap) * boxes, -boxes)

    def put(target):
        place = start
        for turn in range(cap):
            place = jnp.where(row % cap == turn, start + send_ref[turn, target], place)
        begin = spot(order, target) * area
        if not isinstance(target, int):
            begin = pl.multiple_of(begin, area)
        out_ref[pl.ds(begin, area), :] = jnp.where(place == column, 1.0, 0.0)

    each(targets, put)


def sent_of(multipoles, table):
    half = multipoles.astype(HALF)
    parts = half.shape[1] // LANES
    stacked = jnp.concatenate([half[:, part * LANES : (part + 1) * LANES] for part in range(parts)], axis=0)
    return dot_nn(table, stacked)


def far_of(local, expand_ref, offset):
    boxes = expand_ref.shape[0]
    row = lax.broadcasted_iota(jnp.int32, local.shape, 0)
    left = [jnp.where(row % boxes == box, local, jnp.zeros_like(local)) for box in range(boxes)]
    right = [expand_ref[box, pl.ds(offset, local.shape[1]), :] for box in range(boxes)]
    return dot_nn(jnp.concatenate(left, axis=1), jnp.concatenate(right, axis=0))


def near_of(near_ref, chosen_ref, extended, boxes, width):
    picked = dot_nn(chosen_ref[...], extended).astype(HALF)
    classes = near_ref.shape[0]
    result = jnp.zeros((width * boxes, near_ref.shape[1]), FULL)
    for first in range(0, classes, 2):
        group = range(first, min(first + 2, classes))
        left = [
            jnp.concatenate(
                [
                    picked[number * boxes : (number + 1) * boxes, rhs * LANES : (rhs + 1) * LANES]
                    for number in group
                ],
                axis=1,
            )
            for rhs in range(width)
        ]
        right = [near_ref[number] for number in group]
        result = result + dot_nt(jnp.concatenate(left, axis=0), jnp.concatenate(right, axis=1))
    return result


def sources_of(blocks):
    count, area, panels = blocks.shape
    half = area // 2
    pairs = blocks.reshape(count // 2, 2, area, panels)
    low, high = pairs[:, 0], pairs[:, 1]
    row = lax.broadcasted_iota(jnp.int32, low.shape, 1)
    moved_low, moved_high = pltpu.roll(low, half, 1), pltpu.roll(high, half, 1)
    first = jnp.where(row < half, low, moved_high).reshape(-1, panels)
    second = jnp.where(row < half, moved_low, high).reshape(-1, panels)
    return jnp.concatenate([first, second], axis=1).astype(HALF)


def local_of(order, bands, table_ref, sources, band):
    classes = bands[0].shape[0]
    group = classes // table_ref.shape[0]
    parts = sources.shape[1] // LANES

    def add(number, total):
        images = []
        for turn in range(group):
            right = [
                jnp.concatenate(
                    [
                        ref[spot(order, number * group + turn), part * band : (part + 1) * band, :]
                        for part in range(parts)
                    ],
                    axis=1,
                )
                for ref in bands
            ]
            images.append(dot_nt(sources, jnp.concatenate(right, axis=0)))
        images = jnp.concatenate(images, axis=0)
        upper = images.astype(HALF)
        lower = (images - upper.astype(FULL)).astype(HALF)
        table = table_ref[number]
        return total + (dot_nn(table, upper) + dot_nn(table, lower))

    return fold(table_ref.shape[0], add, jnp.zeros((table_ref.shape[1], len(bands) * band), FULL))


def extended_of(pieces, index, count, boxes):
    low = jnp.where(index > 0, pieces[0], jnp.zeros_like(pieces[0]))
    high = jnp.where(index < count - 1, pieces[2], jnp.zeros_like(pieces[2]))
    width = low.shape[0] // boxes
    columns = [
        jnp.concatenate([piece[rhs * boxes : (rhs + 1) * boxes] for piece in (low, pieces[1], high)], axis=0)
        for rhs in range(width)
    ]
    return jnp.concatenate(columns, axis=1).astype(HALF)


def fetch(pairs, signals):
    copies = [
        pltpu.make_async_copy(source, target, signals.at[number])
        for number, (source, target) in enumerate(pairs)
    ]
    for copy in copies:
        copy.start()
    return copies


def near_table(source_ref, chosen_ref):
    boxes, classes = source_ref.shape
    spots = lax.broadcasted_iota(jnp.int32, (boxes, chosen_ref.shape[1]), 1)
    for number in range(classes):
        match = source_ref[:, number : number + 1] == spots
        chosen_ref[number * boxes : (number + 1) * boxes, :] = jnp.where(match, 1.0, 0.0).astype(HALF)


def list_table(order, cap, width, kinds, slot_ref, label_ref, table_ref):
    boxes = slot_ref.shape[1]
    groups, rows, columns = table_ref.shape
    slots, labels = slot_ref[...], label_ref[...]
    places = spot(order, slots // cap) * (cap * width) + slots % cap
    group = kinds // groups
    received = columns // group

    def put(number):
        blocks = []
        for turn in range(group):
            place = jnp.max(jnp.where(labels == number * group + turn, places + 1, 0), axis=0, keepdims=True) - 1
            place = jnp.concatenate([jnp.where(place >= 0, place + rhs * cap, -1) for rhs in range(width)], axis=1)
            spot = lax.broadcasted_iota(jnp.int32, (received, rows), 0)
            blocks.append(jnp.where(place == spot, 1.0, 0.0))
        table_ref[number] = jnp.concatenate(blocks, axis=0).T.astype(HALF)

    each(groups, put)


def first_kernel(
    order,
    width,
    rhs_hbm,
    expand_hbm,
    class_hbm,
    send_hbm,
    near_hbm,
    source_hbm,
    slot_hbm,
    label_hbm,
    out_ref,
    picks_ref,
    expand_ref,
    near_ref,
    chosen_ref,
    table_ref,
    rhs_ref,
    class_ref,
    send_ref,
    wide_ref,
    source_ref,
    slot_ref,
    label_ref,
    signals,
):
    boxes, terms, panels = expand_ref.shape
    core, side = lax.axis_index("core"), lax.axis_index("side")
    step = boxes // 4
    pairs = [
        (send_hbm, send_ref),
        (rhs_hbm.at[pl.ds(core * width, width)], rhs_ref),
        (class_hbm, class_ref),
        (source_hbm, source_ref),
        (slot_hbm, slot_ref),
        (label_hbm, label_ref),
    ]
    for quarter in range(4):
        part = pl.ds(quarter * step, step)
        pairs.append((expand_hbm.at[part], expand_ref.at[part]))
    pairs.append((near_hbm, near_ref))
    copies = fetch(pairs, signals)
    copies[0].wait()
    send_table(order, send_ref, wide_ref, boxes, width, terms // LANES)
    picks_ref[...] = wide_ref[...].astype(HALF)
    band = class_ref.shape[1]
    low = (terms // LANES) * band
    high = low + width * (boxes // 2)
    copies[1].wait()
    copies[2].wait()
    shown = rhs_ref[:, pl.ds(side * (boxes // 2), boxes // 2), :].reshape(high - low, panels).astype(HALF)
    field = rhs_ref[...].reshape(width * boxes, panels).astype(HALF)
    operators = jnp.concatenate(
        [class_ref[0][:, part * LANES : (part + 1) * LANES] for part in range(terms // LANES)], axis=0
    )

    def put(target):
        place = spot(order, target)
        out_ref[place, :low, :] = operators
        out_ref[place, low:high, :] = shown

    each(out_ref.shape[0], put)
    for copy in copies[3:6]:
        copy.wait()
    near_table(source_ref, chosen_ref)
    list_table(order, send_ref.shape[0], width, out_ref.shape[0], slot_ref, label_ref, table_ref)
    result = jnp.zeros((width * boxes, terms), FULL)
    for box in range(boxes):
        if box % step == 0:
            copies[6 + box // step].wait()
        result = own_rows(dot_nt(field, expand_ref[box]), result, box, boxes)
    sent = sent_of(result, picks_ref[...]).astype(HALF)
    out_ref[:, high:, :] = sent.reshape(out_ref.shape[0], -1, LANES)
    copies[10].wait()


def base_of(order, width, low, own_ref, rhs_ref, self_ref, near_ref, chosen_ref):
    boxes, panels = self_ref.shape
    count = own_ref.shape[0]
    core, side, index = lax.axis_index("core"), lax.axis_index("side"), lax.axis_index("box")
    half = boxes // 2
    empty = jnp.zeros((half, panels), FULL)
    pieces = []
    for step in (-1, 0, 1):
        shown = own_ref[spot(order, jnp.clip(index + step, 0, count - 1)), low : low + width * half, :].astype(FULL)
        rows = []
        for rhs in range(width):
            part = shown[rhs * half : (rhs + 1) * half]
            rows += [jnp.where(side == 0, part, empty), jnp.where(side == 0, empty, part)]
        pieces.append(jnp.concatenate(rows, axis=0))
    near = near_of(near_ref, chosen_ref, extended_of(pieces, index, count, boxes), boxes, width)
    field = rhs_ref[pl.ds(core * width, width)]
    diagonal = ((self_ref[...] - SHIFT)[None] * field).reshape(width * boxes, panels)
    return near + jnp.where(side == 0, diagonal, 0.0)


def second_kernel(
    first,
    second,
    width,
    band,
    own_ref,
    other_ref,
    rhs_ref,
    self_ref,
    near_ref,
    chosen_ref,
    expand_ref,
    table_ref,
    send_ref,
    out_ref,
):
    boxes, terms, panels = expand_ref.shape
    count = own_ref.shape[0]
    core, side = lax.axis_index("core"), lax.axis_index("side")
    rows = width * boxes
    high = (terms // LANES) * band + rows // 2
    sources = sources_of(own_ref[:, high:, :].astype(FULL))
    total = local_of(first, (own_ref, other_ref), table_ref, sources, band)
    local = jnp.where(core == 0, total, pltpu.roll(total, band, 1)).astype(HALF)
    base = base_of(first, width, (terms // LANES) * band, own_ref, rhs_ref, self_ref, near_ref, chosen_ref)
    image = far_of(local, expand_ref, side * (terms // 2)) + base
    half = image.astype(HALF)
    sent = sent_of(multipoles_of(half, expand_ref), send_ref[...]).astype(HALF).reshape(count, -1, LANES)

    def put(target):
        for part in range(2):
            place = spot(second, 2 * target + part)
            out_ref[place, :rows, :] = half
            out_ref[place, rows:, :] = sent[spot(first, target)]

    if second is None:
        out_ref[...] = jnp.concatenate(
            [jnp.broadcast_to(half[None, None], (count, 2, rows, LANES)), jnp.stack([sent, sent], axis=1)], axis=2
        ).reshape(out_ref.shape)
    else:
        each(count, put)


def joined(order, parts_ref, place):
    first, second = spot(order, 2 * place), spot(order, 2 * place + 1)
    return parts_ref[first].astype(FULL) + parts_ref[second].astype(FULL)


def field_kernel(order, parts_ref, out_ref):
    out_ref[...] = joined(order, parts_ref, lax.axis_index("box"))[: out_ref.shape[0]]


def rest_of(order, width, parts_ref, self_ref, near_ref, chosen_ref):
    boxes, panels = self_ref.shape
    count = parts_ref.shape[0] // 2
    index = lax.axis_index("box")
    rows = width * boxes
    pieces = [joined(order, parts_ref, jnp.clip(index + step, 0, count - 1))[:rows] for step in (-1, 0, 1)]
    near = near_of(near_ref, chosen_ref, extended_of(pieces, index, count, boxes), boxes, width)
    field = pieces[1]
    diagonal = ((self_ref[...] - SHIFT)[None] * field.reshape(width, boxes, panels)).reshape(rows, panels)
    return near + diagonal


def third_kernel(
    first,
    second,
    width,
    band,
    own_ref,
    other_ref,
    across_ref,
    corner_ref,
    parts_ref,
    expand_ref,
    table_ref,
    self_ref,
    near_ref,
    chosen_ref,
    field_ref,
    rhs_ref,
    out_ref,
):
    boxes, terms, panels = expand_ref.shape
    core, side = lax.axis_index("core"), lax.axis_index("side")
    rows = width * boxes
    count = parts_ref.shape[0] // 2
    if second is None:
        blocks = parts_ref[:, rows:, :].astype(FULL).reshape(count, 2, -1, LANES)
        blocks = blocks[:, 0] + blocks[:, 1]
    else:
        blocks = jnp.stack([joined(second, parts_ref, place)[rows:] for place in first])
    sources = sources_of(blocks)
    bands = (own_ref, other_ref, across_ref, corner_ref)
    total = local_of(first, bands, table_ref, sources, band)
    halves = [total[:, : 2 * band], total[:, 2 * band :]]
    halves = [jnp.where(core == 0, half, pltpu.roll(half, band, 1)) for half in halves]
    local = jnp.concatenate(
        [jnp.where(side == 0, halves[0], halves[1]), jnp.where(side == 0, halves[1], halves[0])], axis=1
    ).astype(HALF)
    last = rest_of(second, width, parts_ref, self_ref, near_ref, chosen_ref) + far_of(local, expand_ref, 0)
    field = field_ref[...]
    right = rhs_ref[pl.ds(core * width, width)].reshape(rows, panels)
    spots = lax.broadcasted_iota(jnp.int32, (8, panels), 0)
    lanes = lax.broadcasted_iota(jnp.int32, (8, panels), 1)
    result = jnp.zeros((8, panels), FULL)
    pairs = ((right, right), (right, field), (field, field), (right, last), (field, last), (last, last))
    for number, (one, two) in enumerate(pairs):
        product = one * two
        for rhs in range(width):
            total = jnp.sum(product[rhs * boxes : (rhs + 1) * boxes])
            mine = (spots == number) & (lanes // (panels // width) == rhs)
            result = jnp.where(mine, total, result)

    def put(target):
        out_ref[target] = result

    each(out_ref.shape[0], put)


def last_kernel(order, width, sums_ref, field_ref, other_ref, rhs_ref, out_ref):
    core = lax.axis_index("core")
    rows, panels = field_ref.shape
    boxes = rows // width
    fields = (field_ref[...], other_ref[...])
    part = panels // width
    lanes = lax.broadcasted_iota(jnp.int32, (1, panels), 1)
    for group in range(2):
        total = fold(
            sums_ref.shape[0] // 2,
            lambda number, state: state + sums_ref[spot(order, 2 * number + group)],
            jnp.zeros(sums_ref.shape[1:], FULL),
        )
        rr, ru, uu, rw, uw, ww = (total[number : number + 1] for number in range(6))
        slope = ru / rr
        norm = uu - slope * ru
        first_row = rw - slope * ru
        scale = lax.rsqrt(rr * norm)
        h11 = slope + SHIFT
        h21 = jnp.sqrt(norm / rr)
        h12 = first_row * scale
        h22 = (uw - slope * uu - slope * first_row) / norm
        image = (ww - 2.0 * slope * uw + slope * slope * uu) / norm
        gram_aa = h11 * h11 + h21 * h21
        gram_ab = h11 * h12 + h21 * (h22 + SHIFT)
        gram_bb = image + 2.0 * SHIFT * h22 + SHIFT * SHIFT
        beta = jnp.sqrt(rr)
        right_a, right_b = beta * h11, beta * h12
        determinant = gram_aa * gram_bb - gram_ab * gram_ab
        coef_a = (gram_bb * right_a - gram_ab * right_b) / determinant
        coef_b = (gram_aa * right_b - gram_ab * right_a) / determinant
        weight = coef_b * lax.rsqrt(norm)
        first = coef_a / beta - weight * slope
        chosen = jnp.where(core == group, fields[0], fields[1])
        for rhs in range(width):
            def wide(value):
                inside = jnp.where(lanes // part == rhs, value, 0.0)
                spread = inside
                for step in range(1, width):
                    spread = spread + pltpu.roll(inside, step * part, 1)
                return spread

            place = group * width + rhs
            out_ref[place] = wide(first) * rhs_ref[place] + wide(weight) * chosen[rhs * boxes : (rhs + 1) * boxes]


def call(kernel, outs, *args, fixed=0, scratch=(), flops=0, limit=16):
    vmem = pl.BlockSpec(memory_space=pltpu.VMEM)
    many = isinstance(outs, list)
    held = len(args) - fixed
    args = [
        value if number < held else pltpu.with_memory_space_constraint(value, pltpu.HBM)
        for number, value in enumerate(args)
    ]
    return pl.pallas_call(
        kernel,
        out_shape=outs,
        in_specs=[vmem] * held + [pl.BlockSpec(memory_space=pltpu.HBM)] * fixed,
        out_specs=[vmem] * len(outs) if many else vmem,
        scratch_shapes=list(scratch),
        compiler_params=pltpu.CompilerParams(vmem_limit_bytes=limit * 1024 * 1024),
        cost_estimate=pl.CostEstimate(flops=flops, bytes_accessed=0, transcendentals=0) if flops else None,
    )(*args)


def per_device(
    rhs_field, self_coef, expand, near_ops, class_ops, near_src, send_rows, list_slot, list_class
):
    count = lax.axis_size("box")
    boxes, terms, panels = expand.shape
    width = rhs_field.shape[0] // 2
    rows = width * boxes
    band = class_ops.shape[1]
    cap = send_rows.shape[2]
    parts = terms // LANES
    area = -(-(cap * width * parts) // 8) * 8
    low = parts * band
    swap = [(0, 1), (1, 0)]
    first, second, third = FIRST.get(count), SECOND.get(2 * count), THIRD.get(2 * count)
    shape = jax.ShapeDtypeStruct
    send = jnp.swapaxes(send_rows, 1, 2)[0]
    slot, label = list_slot.T, list_class.T
    block = shape((rows, panels), FULL)
    kernel = functools.partial(call, limit=16 if count <= 16 else 56)

    slots, picks, kept, near, chosen, table = kernel(
        functools.partial(first_kernel, first, width),
        [
            shape((count, low + rows // 2 + area, LANES), HALF),
            shape((count * area, parts * rows), HALF),
            SLOT(expand.shape, HALF),
            SLOT(near_ops.shape, HALF),
            shape((near_ops.shape[0] * boxes, 3 * boxes), HALF),
            shape((-(-count // 8), rows, min(count, 8) * count * cap * width), HALF),
        ],
        rhs_field, expand, class_ops, send, near_ops, near_src, slot, label,
        fixed=8,
        scratch=[
            pltpu.VMEM((width,) + rhs_field.shape[1:], FULL),
            pltpu.VMEM(class_ops.shape, HALF),
            pltpu.SMEM(send.shape, jnp.int32),
            pltpu.VMEM((count * area, parts * rows), FULL),
            pltpu.VMEM(near_src.shape, jnp.int32),
            pltpu.VMEM(slot.shape, jnp.int32),
            pltpu.VMEM(label.shape, jnp.int32),
            pltpu.SemaphoreType.DMA((11,)),
        ],
    )
    own = exchange(slots, "box", first)
    bands = own[:, :low]
    other = lax.ppermute(bands, "core", swap)
    across = lax.ppermute(bands, "side", swap)
    corner = lax.ppermute(across, "core", swap)
    images = kernel(
        functools.partial(second_kernel, first, second, width, band),
        shape((2 * count, rows + area, LANES), HALF),
        own, other, rhs_field, self_coef, near, chosen, kept, table, picks,
    )
    images = exchange(images, ("box", "side"), second)
    field = kernel(functools.partial(field_kernel, second), block, images)
    field_other = lax.ppermute(field, "core", swap)
    sums = kernel(
        functools.partial(third_kernel, first, second, width, band),
        SLOT((2 * count, 8, panels), FULL),
        bands, other, across, corner, images, kept, table, self_coef, near, chosen, field, rhs_field,
    )
    sums, field_other = lax.optimization_barrier((sums, field_other))
    sums = exchange(sums, ("box", "core"), third)
    return kernel(
        functools.partial(last_kernel, third, width),
        shape(rhs_field.shape, FULL),
        sums, field, field_other, rhs_field,
    )


def solution(mesh):
    count, levels = mesh.devices.shape
    finer = Mesh(mesh.devices.reshape(count, levels // 2, 2), ("box", "side", "core"))
    return jax.shard_map(
        per_device,
        mesh=finer,
        in_specs=(
            P(None, "box", None),
            P("box", None),
            P("box", None, None),
            P(),
            P("box", ("side", "core"), None),
            P("box", None),
            P("box", None, None),
            P("box", None),
            P("box", None),
        ),
        out_specs=P(None, "box", None),
        check_vma=False,
    )
```

```python
import functools

import jax
import jax.numpy as jnp
from jax import lax
from jax.experimental import pallas as pl
from jax.experimental.pallas import tpu as pltpu
from jax.sharding import Mesh, PartitionSpec as P

SHIFT = 3.0
LANES = 128
HALF = jnp.bfloat16
FULL = jnp.float32
SLOT = pltpu.VMEM
FIRST = {8: (5, 7, 0, 4, 6, 3, 1, 2)}
SECOND = {16: (6, 0, 2, 1, 15, 3, 8, 7, 4, 11, 14, 9, 10, 13, 5, 12)}
THIRD = {16: (11, 9, 13, 8, 14, 5, 7, 4, 12, 1, 15, 3, 0, 6, 2, 10)}


def spot(order, member):
    if order is None:
        return member
    if isinstance(member, int):
        return order.index(member)
    result = jnp.zeros_like(member)
    for number, value in enumerate(order):
        result = jnp.where(member == value, number, result)
    return result


def exchange(value, axes, order):
    groups = None if order is None else [list(order)]
    return lax.all_to_all(value, axes, 0, 0, tiled=True, axis_index_groups=groups)


def each(count, body):
    if count <= 32:
        for number in range(count):
            body(number)
    else:
        lax.fori_loop(0, count, lambda number, state: (body(number), state)[1], 0)


def fold(count, body, state):
    if count <= 32:
        for number in range(count):
            state = body(number, state)
        return state
    return lax.fori_loop(0, count, body, state)


def dot_nt(left, right):
    return lax.dot_general(left, right, (((1,), (1,)), ((), ())), preferred_element_type=FULL)


def dot_nn(left, right):
    return lax.dot_general(left, right, (((1,), (0,)), ((), ())), preferred_element_type=FULL)


def own_rows(values, result, box, boxes):
    row = lax.broadcasted_iota(jnp.int32, result.shape, 0)
    return jnp.where(row % boxes == box, values, result)


def multipoles_of(field, expand_ref):
    boxes, terms, _ = expand_ref.shape
    result = jnp.zeros((field.shape[0], terms), FULL)
    for box in range(boxes):
        result = own_rows(dot_nt(field, expand_ref[box]), result, box, boxes)
    return result


def send_table(order, send_ref, out_ref, boxes, width, parts):
    cap, targets = send_ref.shape
    area = out_ref.shape[0] // targets
    row = lax.broadcasted_iota(jnp.int32, (area, out_ref.shape[1]), 0)
    column = lax.broadcasted_iota(jnp.int32, (area, out_ref.shape[1]), 1)
    start = jnp.where(row < cap * width * parts, (row // cap) * boxes, -boxes)

    def put(target):
        place = start
        for turn in range(cap):
            place = jnp.where(row % cap == turn, start + send_ref[turn, target], place)
        begin = spot(order, target) * area
        if not isinstance(target, int):
            begin = pl.multiple_of(begin, area)
        out_ref[pl.ds(begin, area), :] = jnp.where(place == column, 1.0, 0.0)

    each(targets, put)


def sent_of(multipoles, table):
    half = multipoles.astype(HALF)
    parts = half.shape[1] // LANES
    stacked = jnp.concatenate([half[:, part * LANES : (part + 1) * LANES] for part in range(parts)], axis=0)
    return dot_nn(table, stacked)


def far_of(local, expand_ref, offset):
    boxes = expand_ref.shape[0]
    row = lax.broadcasted_iota(jnp.int32, local.shape, 0)
    left = [jnp.where(row % boxes == box, local, jnp.zeros_like(local)) for box in range(boxes)]
    right = [expand_ref[box, pl.ds(offset, local.shape[1]), :] for box in range(boxes)]
    return dot_nn(jnp.concatenate(left, axis=1), jnp.concatenate(right, axis=0))


def near_of(near_ref, chosen_ref, extended, boxes, width):
    picked = dot_nn(chosen_ref[...], extended).astype(HALF)
    classes = near_ref.shape[0]
    result = jnp.zeros((width * boxes, near_ref.shape[1]), FULL)
    for first in range(0, classes, 2):
        group = range(first, min(first + 2, classes))
        left = [
            jnp.concatenate(
                [
                    picked[number * boxes : (number + 1) * boxes, rhs * LANES : (rhs + 1) * LANES]
                    for number in group
                ],
                axis=1,
            )
            for rhs in range(width)
        ]
        right = [near_ref[number] for number in group]
        result = result + dot_nt(jnp.concatenate(left, axis=0), jnp.concatenate(right, axis=1))
    return result


def sources_of(blocks):
    count, area, panels = blocks.shape
    half = area // 2
    pairs = blocks.reshape(count // 2, 2, area, panels)
    low, high = pairs[:, 0], pairs[:, 1]
    row = lax.broadcasted_iota(jnp.int32, low.shape, 1)
    moved_low, moved_high = pltpu.roll(low, half, 1), pltpu.roll(high, half, 1)
    first = jnp.where(row < half, low, moved_high).reshape(-1, panels)
    second = jnp.where(row < half, moved_low, high).reshape(-1, panels)
    return jnp.concatenate([first, second], axis=1).astype(HALF)


def local_of(order, bands, table_ref, sources, band):
    classes = bands[0].shape[0]
    group = classes // table_ref.shape[0]
    parts = sources.shape[1] // LANES

    def add(number, total):
        images = []
        for turn in range(group):
            right = [
                jnp.concatenate(
                    [
                        ref[spot(order, number * group + turn), part * band : (part + 1) * band, :]
                        for part in range(parts)
                    ],
                    axis=1,
                )
                for ref in bands
            ]
            images.append(dot_nt(sources, jnp.concatenate(right, axis=0)))
        images = jnp.concatenate(images, axis=0)
        upper = images.astype(HALF)
        lower = (images - upper.astype(FULL)).astype(HALF)
        table = table_ref[number]
        return total + (dot_nn(table, upper) + dot_nn(table, lower))

    return fold(table_ref.shape[0], add, jnp.zeros((table_ref.shape[1], len(bands) * band), FULL))


def extended_of(pieces, index, count, boxes):
    low = jnp.where(index > 0, pieces[0], jnp.zeros_like(pieces[0]))
    high = jnp.where(index < count - 1, pieces[2], jnp.zeros_like(pieces[2]))
    width = low.shape[0] // boxes
    columns = [
        jnp.concatenate([piece[rhs * boxes : (rhs + 1) * boxes] for piece in (low, pieces[1], high)], axis=0)
        for rhs in range(width)
    ]
    return jnp.concatenate(columns, axis=1).astype(HALF)


def fetch(pairs, signals):
    copies = [
        pltpu.make_async_copy(source, target, signals.at[number])
        for number, (source, target) in enumerate(pairs)
    ]
    for copy in copies:
        copy.start()
    return copies


def near_table(source_ref, chosen_ref):
    boxes, classes = source_ref.shape
    spots = lax.broadcasted_iota(jnp.int32, (boxes, chosen_ref.shape[1]), 1)
    for number in range(classes):
        match = source_ref[:, number : number + 1] == spots
        chosen_ref[number * boxes : (number + 1) * boxes, :] = jnp.where(match, 1.0, 0.0).astype(HALF)


def list_table(order, cap, width, kinds, slot_ref, label_ref, table_ref):
    boxes = slot_ref.shape[1]
    groups, rows, columns = table_ref.shape
    slots, labels = slot_ref[...], label_ref[...]
    places = spot(order, slots // cap) * (cap * width) + slots % cap
    group = kinds // groups
    received = columns // group

    def put(number):
        blocks = []
        for turn in range(group):
            place = jnp.max(jnp.where(labels == number * group + turn, places + 1, 0), axis=0, keepdims=True) - 1
            place = jnp.concatenate([jnp.where(place >= 0, place + rhs * cap, -1) for rhs in range(width)], axis=1)
            spot = lax.broadcasted_iota(jnp.int32, (received, rows), 0)
            blocks.append(jnp.where(place == spot, 1.0, 0.0))
        table_ref[number] = jnp.concatenate(blocks, axis=0).T.astype(HALF)

    each(groups, put)


def first_kernel(
    order,
    width,
    rhs_hbm,
    expand_hbm,
    class_hbm,
    send_hbm,
    near_hbm,
    source_hbm,
    slot_hbm,
    label_hbm,
    out_ref,
    picks_ref,
    expand_ref,
    near_ref,
    chosen_ref,
    table_ref,
    rhs_ref,
    class_ref,
    send_ref,
    wide_ref,
    source_ref,
    slot_ref,
    label_ref,
    signals,
):
    boxes, terms, panels = expand_ref.shape
    core, side = lax.axis_index("core"), lax.axis_index("side")
    step = boxes // 2
    pairs = [
        (send_hbm, send_ref),
        (rhs_hbm.at[pl.ds(core * width, width)], rhs_ref),
        (class_hbm, class_ref),
        (source_hbm, source_ref),
        (slot_hbm, slot_ref),
        (label_hbm, label_ref),
    ]
    for chunk in range(2):
        part = pl.ds(chunk * step, step)
        pairs.append((expand_hbm.at[part], expand_ref.at[part]))
    pairs.append((near_hbm, near_ref))
    copies = fetch(pairs, signals)
    copies[0].wait()
    send_table(order, send_ref, wide_ref, boxes, width, terms // LANES)
    picks_ref[...] = wide_ref[...].astype(HALF)
    band = class_ref.shape[1]
    low = (terms // LANES) * band
    high = low + width * (boxes // 2)
    copies[1].wait()
    copies[2].wait()
    shown = rhs_ref[:, pl.ds(side * (boxes // 2), boxes // 2), :].reshape(high - low, panels).astype(HALF)
    field = rhs_ref[...].reshape(width * boxes, panels).astype(HALF)
    operators = jnp.concatenate(
        [class_ref[0][:, part * LANES : (part + 1) * LANES] for part in range(terms // LANES)], axis=0
    )

    def put(target):
        place = spot(order, target)
        out_ref[place, :low, :] = operators
        out_ref[place, low:high, :] = shown

    each(out_ref.shape[0], put)
    for copy in copies[3:6]:
        copy.wait()
    near_table(source_ref, chosen_ref)
    list_table(order, send_ref.shape[0], width, out_ref.shape[0], slot_ref, label_ref, table_ref)
    result = jnp.zeros((width * boxes, terms), FULL)
    for box in range(boxes):
        if box % step == 0:
            copies[6 + box // step].wait()
        result = own_rows(dot_nt(field, expand_ref[box]), result, box, boxes)
    sent = sent_of(result, picks_ref[...]).astype(HALF)
    out_ref[:, high:, :] = sent.reshape(out_ref.shape[0], -1, LANES)
    copies[8].wait()


def base_of(order, width, low, own_ref, rhs_ref, self_ref, near_ref, chosen_ref):
    boxes, panels = self_ref.shape
    count = own_ref.shape[0]
    core, side, index = lax.axis_index("core"), lax.axis_index("side"), lax.axis_index("box")
    half = boxes // 2
    empty = jnp.zeros((half, panels), FULL)
    pieces = []
    for step in (-1, 0, 1):
        shown = own_ref[spot(order, jnp.clip(index + step, 0, count - 1)), low : low + width * half, :].astype(FULL)
        rows = []
        for rhs in range(width):
            part = shown[rhs * half : (rhs + 1) * half]
            rows += [jnp.where(side == 0, part, empty), jnp.where(side == 0, empty, part)]
        pieces.append(jnp.concatenate(rows, axis=0))
    near = near_of(near_ref, chosen_ref, extended_of(pieces, index, count, boxes), boxes, width)
    field = rhs_ref[pl.ds(core * width, width)]
    diagonal = ((self_ref[...] - SHIFT)[None] * field).reshape(width * boxes, panels)
    return near + jnp.where(side == 0, diagonal, 0.0)


def second_kernel(
    first,
    second,
    width,
    band,
    own_ref,
    other_ref,
    rhs_ref,
    self_ref,
    near_ref,
    chosen_ref,
    expand_ref,
    table_ref,
    send_ref,
    out_ref,
):
    boxes, terms, panels = expand_ref.shape
    count = own_ref.shape[0]
    core, side = lax.axis_index("core"), lax.axis_index("side")
    rows = width * boxes
    high = (terms // LANES) * band + rows // 2
    sources = sources_of(own_ref[:, high:, :].astype(FULL))
    total = local_of(first, (own_ref, other_ref), table_ref, sources, band)
    local = jnp.where(core == 0, total, pltpu.roll(total, band, 1)).astype(HALF)
    base = base_of(first, width, (terms // LANES) * band, own_ref, rhs_ref, self_ref, near_ref, chosen_ref)
    image = far_of(local, expand_ref, side * (terms // 2)) + base
    half = image.astype(HALF)
    sent = sent_of(multipoles_of(half, expand_ref), send_ref[...]).astype(HALF).reshape(count, -1, LANES)

    def put(target):
        for part in range(2):
            place = spot(second, 2 * target + part)
            out_ref[place, :rows, :] = half
            out_ref[place, rows:, :] = sent[spot(first, target)]

    if second is None:
        out_ref[...] = jnp.concatenate(
            [jnp.broadcast_to(half[None, None], (count, 2, rows, LANES)), jnp.stack([sent, sent], axis=1)], axis=2
        ).reshape(out_ref.shape)
    else:
        each(count, put)


def joined(order, parts_ref, place):
    first, second = spot(order, 2 * place), spot(order, 2 * place + 1)
    return parts_ref[first].astype(FULL) + parts_ref[second].astype(FULL)


def field_kernel(order, parts_ref, out_ref):
    out_ref[...] = joined(order, parts_ref, lax.axis_index("box"))[: out_ref.shape[0]]


def rest_of(order, width, parts_ref, self_ref, near_ref, chosen_ref):
    boxes, panels = self_ref.shape
    count = parts_ref.shape[0] // 2
    index = lax.axis_index("box")
    rows = width * boxes
    pieces = [joined(order, parts_ref, jnp.clip(index + step, 0, count - 1))[:rows] for step in (-1, 0, 1)]
    near = near_of(near_ref, chosen_ref, extended_of(pieces, index, count, boxes), boxes, width)
    field = pieces[1]
    diagonal = ((self_ref[...] - SHIFT)[None] * field.reshape(width, boxes, panels)).reshape(rows, panels)
    return near + diagonal


def third_kernel(
    first,
    second,
    width,
    band,
    own_ref,
    other_ref,
    across_ref,
    corner_ref,
    parts_ref,
    expand_ref,
    table_ref,
    self_ref,
    near_ref,
    chosen_ref,
    field_ref,
    rhs_ref,
    out_ref,
):
    boxes, terms, panels = expand_ref.shape
    core, side = lax.axis_index("core"), lax.axis_index("side")
    rows = width * boxes
    count = parts_ref.shape[0] // 2
    if second is None:
        blocks = parts_ref[:, rows:, :].astype(FULL).reshape(count, 2, -1, LANES)
        blocks = blocks[:, 0] + blocks[:, 1]
    else:
        blocks = jnp.stack([joined(second, parts_ref, place)[rows:] for place in first])
    sources = sources_of(blocks)
    bands = (own_ref, other_ref, across_ref, corner_ref)
    total = local_of(first, bands, table_ref, sources, band)
    halves = [total[:, : 2 * band], total[:, 2 * band :]]
    halves = [jnp.where(core == 0, half, pltpu.roll(half, band, 1)) for half in halves]
    local = jnp.concatenate(
        [jnp.where(side == 0, halves[0], halves[1]), jnp.where(side == 0, halves[1], halves[0])], axis=1
    ).astype(HALF)
    last = rest_of(second, width, parts_ref, self_ref, near_ref, chosen_ref) + far_of(local, expand_ref, 0)
    field = field_ref[...]
    right = rhs_ref[pl.ds(core * width, width)].reshape(rows, panels)
    spots = lax.broadcasted_iota(jnp.int32, (8, panels), 0)
    lanes = lax.broadcasted_iota(jnp.int32, (8, panels), 1)
    result = jnp.zeros((8, panels), FULL)
    pairs = ((right, right), (right, field), (field, field), (right, last), (field, last), (last, last))
    for number, (one, two) in enumerate(pairs):
        product = one * two
        for rhs in range(width):
            total = jnp.sum(product[rhs * boxes : (rhs + 1) * boxes])
            mine = (spots == number) & (lanes // (panels // width) == rhs)
            result = jnp.where(mine, total, result)

    def put(target):
        out_ref[target] = result

    each(out_ref.shape[0], put)


def last_kernel(order, width, sums_ref, field_ref, other_ref, rhs_ref, out_ref):
    core = lax.axis_index("core")
    rows, panels = field_ref.shape
    boxes = rows // width
    fields = (field_ref[...], other_ref[...])
    part = panels // width
    lanes = lax.broadcasted_iota(jnp.int32, (1, panels), 1)
    for group in range(2):
        total = fold(
            sums_ref.shape[0] // 2,
            lambda number, state: state + sums_ref[spot(order, 2 * number + group)],
            jnp.zeros(sums_ref.shape[1:], FULL),
        )
        rr, ru, uu, rw, uw, ww = (total[number : number + 1] for number in range(6))
        slope = ru / rr
        norm = uu - slope * ru
        first_row = rw - slope * ru
        scale = lax.rsqrt(rr * norm)
        h11 = slope + SHIFT
        h21 = jnp.sqrt(norm / rr)
        h12 = first_row * scale
        h22 = (uw - slope * uu - slope * first_row) / norm
        image = (ww - 2.0 * slope * uw + slope * slope * uu) / norm
        gram_aa = h11 * h11 + h21 * h21
        gram_ab = h11 * h12 + h21 * (h22 + SHIFT)
        gram_bb = image + 2.0 * SHIFT * h22 + SHIFT * SHIFT
        beta = jnp.sqrt(rr)
        right_a, right_b = beta * h11, beta * h12
        determinant = gram_aa * gram_bb - gram_ab * gram_ab
        coef_a = (gram_bb * right_a - gram_ab * right_b) / determinant
        coef_b = (gram_aa * right_b - gram_ab * right_a) / determinant
        weight = coef_b * lax.rsqrt(norm)
        first = coef_a / beta - weight * slope
        chosen = jnp.where(core == group, fields[0], fields[1])
        for rhs in range(width):
            def wide(value):
                inside = jnp.where(lanes // part == rhs, value, 0.0)
                spread = inside
                for step in range(1, width):
                    spread = spread + pltpu.roll(inside, step * part, 1)
                return spread

            place = group * width + rhs
            out_ref[place] = wide(first) * rhs_ref[place] + wide(weight) * chosen[rhs * boxes : (rhs + 1) * boxes]


def call(kernel, outs, *args, fixed=0, scratch=(), flops=0, limit=16):
    vmem = pl.BlockSpec(memory_space=pltpu.VMEM)
    many = isinstance(outs, list)
    held = len(args) - fixed
    args = [
        value if number < held else pltpu.with_memory_space_constraint(value, pltpu.HBM)
        for number, value in enumerate(args)
    ]
    return pl.pallas_call(
        kernel,
        out_shape=outs,
        in_specs=[vmem] * held + [pl.BlockSpec(memory_space=pltpu.HBM)] * fixed,
        out_specs=[vmem] * len(outs) if many else vmem,
        scratch_shapes=list(scratch),
        compiler_params=pltpu.CompilerParams(vmem_limit_bytes=limit * 1024 * 1024),
        cost_estimate=pl.CostEstimate(flops=flops, bytes_accessed=0, transcendentals=0) if flops else None,
    )(*args)


def per_device(
    rhs_field, self_coef, expand, near_ops, class_ops, near_src, send_rows, list_slot, list_class
):
    count = lax.axis_size("box")
    boxes, terms, panels = expand.shape
    width = rhs_field.shape[0] // 2
    rows = width * boxes
    band = class_ops.shape[1]
    cap = send_rows.shape[2]
    parts = terms // LANES
    area = -(-(cap * width * parts) // 8) * 8
    low = parts * band
    swap = [(0, 1), (1, 0)]
    first, second, third = FIRST.get(count), SECOND.get(2 * count), THIRD.get(2 * count)
    shape = jax.ShapeDtypeStruct
    send = jnp.swapaxes(send_rows, 1, 2)[0]
    slot, label = list_slot.T, list_class.T
    block = shape((rows, panels), FULL)
    kernel = functools.partial(call, limit=16 if count <= 16 else 56)

    slots, picks, kept, near, chosen, table = kernel(
        functools.partial(first_kernel, first, width),
        [
            shape((count, low + rows // 2 + area, LANES), HALF),
            shape((count * area, parts * rows), HALF),
            SLOT(expand.shape, HALF),
            SLOT(near_ops.shape, HALF),
            shape((near_ops.shape[0] * boxes, 3 * boxes), HALF),
            shape((-(-count // 8), rows, min(count, 8) * count * cap * width), HALF),
        ],
        rhs_field, expand, class_ops, send, near_ops, near_src, slot, label,
        fixed=8,
        scratch=[
            pltpu.VMEM((width,) + rhs_field.shape[1:], FULL),
            pltpu.VMEM(class_ops.shape, HALF),
            pltpu.SMEM(send.shape, jnp.int32),
            pltpu.VMEM((count * area, parts * rows), FULL),
            pltpu.VMEM(near_src.shape, jnp.int32),
            pltpu.VMEM(slot.shape, jnp.int32),
            pltpu.VMEM(label.shape, jnp.int32),
            pltpu.SemaphoreType.DMA((9,)),
        ],
    )
    own = exchange(slots, "box", first)
    bands = own[:, :low]
    other = lax.ppermute(bands, "core", swap)
    across = lax.ppermute(bands, "side", swap)
    corner = lax.ppermute(across, "core", swap)
    images = kernel(
        functools.partial(second_kernel, first, second, width, band),
        shape((2 * count, rows + area, LANES), HALF),
        own, other, rhs_field, self_coef, near, chosen, kept, table, picks,
    )
    images = exchange(images, ("box", "side"), second)
    field = kernel(functools.partial(field_kernel, second), block, images)
    field_other = lax.ppermute(field, "core", swap)
    sums = kernel(
        functools.partial(third_kernel, first, second, width, band),
        SLOT((2 * count, 8, panels), FULL),
        bands, other, across, corner, images, kept, table, self_coef, near, chosen, field, rhs_field,
    )
    sums, field_other = lax.optimization_barrier((sums, field_other))
    sums = exchange(sums, ("box", "core"), third)
    return kernel(
        functools.partial(last_kernel, third, width),
        shape(rhs_field.shape, FULL),
        sums, field, field_other, rhs_field,
    )


def solution(mesh):
    count, levels = mesh.devices.shape
    finer = Mesh(mesh.devices.reshape(count, levels // 2, 2), ("box", "side", "core"))
    return jax.shard_map(
        per_device,
        mesh=finer,
        in_specs=(
            P(None, "box", None),
            P("box", None),
            P("box", None, None),
            P(),
            P("box", ("side", "core"), None),
            P("box", None),
            P("box", None, None),
            P("box", None),
            P("box", None),
        ),
        out_specs=P(None, "box", None),
        check_vma=False,
    )
```

```python
import functools

import jax
import jax.numpy as jnp
from jax import lax
from jax.experimental import pallas as pl
from jax.experimental.pallas import tpu as pltpu
from jax.sharding import Mesh, PartitionSpec as P

SHIFT = 3.0
LANES = 128
HALF = jnp.bfloat16
FULL = jnp.float32
SLOT = pltpu.VMEM
FIRST = {8: (5, 7, 0, 4, 6, 3, 1, 2)}
SECOND = {16: (10, 8, 3, 7, 2, 14, 5, 1, 11, 9, 15, 13, 12, 6, 4, 0)}
THIRD = {16: (11, 9, 13, 8, 14, 5, 7, 4, 12, 1, 15, 3, 0, 6, 2, 10)}


def spot(order, member):
    if order is None:
        return member
    if isinstance(member, int):
        return order.index(member)
    result = jnp.zeros_like(member)
    for number, value in enumerate(order):
        result = jnp.where(member == value, number, result)
    return result


def exchange(value, axes, order):
    groups = None if order is None else [list(order)]
    return lax.all_to_all(value, axes, 0, 0, tiled=True, axis_index_groups=groups)


def each(count, body):
    if count <= 32:
        for number in range(count):
            body(number)
    else:
        lax.fori_loop(0, count, lambda number, state: (body(number), state)[1], 0)


def fold(count, body, state):
    if count <= 32:
        for number in range(count):
            state = body(number, state)
        return state
    return lax.fori_loop(0, count, body, state)


def dot_nt(left, right):
    return lax.dot_general(left, right, (((1,), (1,)), ((), ())), preferred_element_type=FULL)


def dot_nn(left, right):
    return lax.dot_general(left, right, (((1,), (0,)), ((), ())), preferred_element_type=FULL)


def own_rows(values, result, box, boxes):
    row = lax.broadcasted_iota(jnp.int32, result.shape, 0)
    return jnp.where(row % boxes == box, values, result)


def multipoles_of(field, expand_ref):
    boxes, terms, _ = expand_ref.shape
    result = jnp.zeros((field.shape[0], terms), FULL)
    for box in range(boxes):
        result = own_rows(dot_nt(field, expand_ref[box]), result, box, boxes)
    return result


def send_table(order, send_ref, out_ref, boxes, width, parts):
    cap, targets = send_ref.shape
    area = out_ref.shape[0] // targets
    row = lax.broadcasted_iota(jnp.int32, (area, out_ref.shape[1]), 0)
    column = lax.broadcasted_iota(jnp.int32, (area, out_ref.shape[1]), 1)
    start = jnp.where(row < cap * width * parts, (row // cap) * boxes, -boxes)

    def put(target):
        place = start
        for turn in range(cap):
            place = jnp.where(row % cap == turn, start + send_ref[turn, target], place)
        begin = spot(order, target) * area
        if not isinstance(target, int):
            begin = pl.multiple_of(begin, area)
        out_ref[pl.ds(begin, area), :] = jnp.where(place == column, 1.0, 0.0)

    each(targets, put)


def sent_of(multipoles, table):
    half = multipoles.astype(HALF)
    parts = half.shape[1] // LANES
    stacked = jnp.concatenate([half[:, part * LANES : (part + 1) * LANES] for part in range(parts)], axis=0)
    return dot_nn(table, stacked)


def far_of(local, expand_ref, offset):
    boxes = expand_ref.shape[0]
    row = lax.broadcasted_iota(jnp.int32, local.shape, 0)
    left = [jnp.where(row % boxes == box, local, jnp.zeros_like(local)) for box in range(boxes)]
    right = [expand_ref[box, pl.ds(offset, local.shape[1]), :] for box in range(boxes)]
    return dot_nn(jnp.concatenate(left, axis=1), jnp.concatenate(right, axis=0))


def near_of(near_ref, chosen_ref, extended, boxes, width):
    picked = dot_nn(chosen_ref[...], extended).astype(HALF)
    classes = near_ref.shape[0]
    result = jnp.zeros((width * boxes, near_ref.shape[1]), FULL)
    for first in range(0, classes, 2):
        group = range(first, min(first + 2, classes))
        left = [
            jnp.concatenate(
                [
                    picked[number * boxes : (number + 1) * boxes, rhs * LANES : (rhs + 1) * LANES]
                    for number in group
                ],
                axis=1,
            )
            for rhs in range(width)
        ]
        right = [near_ref[number] for number in group]
        result = result + dot_nt(jnp.concatenate(left, axis=0), jnp.concatenate(right, axis=1))
    return result


def sources_of(blocks):
    count, area, panels = blocks.shape
    half = area // 2
    pairs = blocks.reshape(count // 2, 2, area, panels)
    low, high = pairs[:, 0], pairs[:, 1]
    row = lax.broadcasted_iota(jnp.int32, low.shape, 1)
    moved_low, moved_high = pltpu.roll(low, half, 1), pltpu.roll(high, half, 1)
    first = jnp.where(row < half, low, moved_high).reshape(-1, panels)
    second = jnp.where(row < half, moved_low, high).reshape(-1, panels)
    return jnp.concatenate([first, second], axis=1).astype(HALF)


def local_of(order, bands, table_ref, sources, band):
    classes = bands[0].shape[0]
    group = classes // table_ref.shape[0]
    parts = sources.shape[1] // LANES

    def add(number, total):
        images = []
        for turn in range(group):
            right = [
                jnp.concatenate(
                    [
                        ref[spot(order, number * group + turn), part * band : (part + 1) * band, :]
                        for part in range(parts)
                    ],
                    axis=1,
                )
                for ref in bands
            ]
            images.append(dot_nt(sources, jnp.concatenate(right, axis=0)))
        images = jnp.concatenate(images, axis=0)
        upper = images.astype(HALF)
        lower = (images - upper.astype(FULL)).astype(HALF)
        table = table_ref[number]
        return total + (dot_nn(table, upper) + dot_nn(table, lower))

    return fold(table_ref.shape[0], add, jnp.zeros((table_ref.shape[1], len(bands) * band), FULL))


def extended_of(pieces, index, count, boxes):
    low = jnp.where(index > 0, pieces[0], jnp.zeros_like(pieces[0]))
    high = jnp.where(index < count - 1, pieces[2], jnp.zeros_like(pieces[2]))
    width = low.shape[0] // boxes
    columns = [
        jnp.concatenate([piece[rhs * boxes : (rhs + 1) * boxes] for piece in (low, pieces[1], high)], axis=0)
        for rhs in range(width)
    ]
    return jnp.concatenate(columns, axis=1).astype(HALF)


def fetch(pairs, signals):
    copies = [
        pltpu.make_async_copy(source, target, signals.at[number])
        for number, (source, target) in enumerate(pairs)
    ]
    for copy in copies:
        copy.start()
    return copies


def near_table(source_ref, chosen_ref):
    boxes, classes = source_ref.shape
    spots = lax.broadcasted_iota(jnp.int32, (boxes, chosen_ref.shape[1]), 1)
    for number in range(classes):
        match = source_ref[:, number : number + 1] == spots
        chosen_ref[number * boxes : (number + 1) * boxes, :] = jnp.where(match, 1.0, 0.0).astype(HALF)


def list_table(order, cap, width, kinds, slot_ref, label_ref, table_ref):
    boxes = slot_ref.shape[1]
    groups, rows, columns = table_ref.shape
    slots, labels = slot_ref[...], label_ref[...]
    places = spot(order, slots // cap) * (cap * width) + slots % cap
    group = kinds // groups
    received = columns // group

    def put(number):
        blocks = []
        for turn in range(group):
            place = jnp.max(jnp.where(labels == number * group + turn, places + 1, 0), axis=0, keepdims=True) - 1
            place = jnp.concatenate([jnp.where(place >= 0, place + rhs * cap, -1) for rhs in range(width)], axis=1)
            spot = lax.broadcasted_iota(jnp.int32, (received, rows), 0)
            blocks.append(jnp.where(place == spot, 1.0, 0.0))
        table_ref[number] = jnp.concatenate(blocks, axis=0).T.astype(HALF)

    each(groups, put)


def first_kernel(
    order,
    width,
    rhs_hbm,
    expand_hbm,
    class_hbm,
    send_hbm,
    near_hbm,
    source_hbm,
    slot_hbm,
    label_hbm,
    out_ref,
    picks_ref,
    expand_ref,
    near_ref,
    chosen_ref,
    table_ref,
    rhs_ref,
    class_ref,
    send_ref,
    wide_ref,
    source_ref,
    slot_ref,
    label_ref,
    signals,
):
    boxes, terms, panels = expand_ref.shape
    core, side = lax.axis_index("core"), lax.axis_index("side")
    step = boxes // 2
    pairs = [
        (send_hbm, send_ref),
        (rhs_hbm.at[pl.ds(core * width, width)], rhs_ref),
        (class_hbm, class_ref),
        (source_hbm, source_ref),
        (slot_hbm, slot_ref),
        (label_hbm, label_ref),
    ]
    for chunk in range(2):
        part = pl.ds(chunk * step, step)
        pairs.append((expand_hbm.at[part], expand_ref.at[part]))
    pairs.append((near_hbm, near_ref))
    copies = fetch(pairs, signals)
    copies[0].wait()
    send_table(order, send_ref, wide_ref, boxes, width, terms // LANES)
    picks_ref[...] = wide_ref[...].astype(HALF)
    band = class_ref.shape[1]
    low = (terms // LANES) * band
    high = low + width * (boxes // 2)
    copies[1].wait()
    copies[2].wait()
    shown = rhs_ref[:, pl.ds(side * (boxes // 2), boxes // 2), :].reshape(high - low, panels).astype(HALF)
    field = rhs_ref[...].reshape(width * boxes, panels).astype(HALF)
    operators = jnp.concatenate(
        [class_ref[0][:, part * LANES : (part + 1) * LANES] for part in range(terms // LANES)], axis=0
    )

    def put(target):
        place = spot(order, target)
        out_ref[place, :low, :] = operators
        out_ref[place, low:high, :] = shown

    each(out_ref.shape[0], put)
    for copy in copies[3:6]:
        copy.wait()
    near_table(source_ref, chosen_ref)
    list_table(order, send_ref.shape[0], width, out_ref.shape[0], slot_ref, label_ref, table_ref)
    result = jnp.zeros((width * boxes, terms), FULL)
    for box in range(boxes):
        if box % step == 0:
            copies[6 + box // step].wait()
        result = own_rows(dot_nt(field, expand_ref[box]), result, box, boxes)
    sent = sent_of(result, picks_ref[...]).astype(HALF)
    out_ref[:, high:, :] = sent.reshape(out_ref.shape[0], -1, LANES)
    copies[8].wait()


def base_of(order, width, low, own_ref, rhs_ref, self_ref, near_ref, chosen_ref):
    boxes, panels = self_ref.shape
    count = own_ref.shape[0]
    core, side, index = lax.axis_index("core"), lax.axis_index("side"), lax.axis_index("box")
    half = boxes // 2
    empty = jnp.zeros((half, panels), FULL)
    pieces = []
    for step in (-1, 0, 1):
        shown = own_ref[spot(order, jnp.clip(index + step, 0, count - 1)), low : low + width * half, :].astype(FULL)
        rows = []
        for rhs in range(width):
            part = shown[rhs * half : (rhs + 1) * half]
            rows += [jnp.where(side == 0, part, empty), jnp.where(side == 0, empty, part)]
        pieces.append(jnp.concatenate(rows, axis=0))
    near = near_of(near_ref, chosen_ref, extended_of(pieces, index, count, boxes), boxes, width)
    field = rhs_ref[pl.ds(core * width, width)]
    diagonal = ((self_ref[...] - SHIFT)[None] * field).reshape(width * boxes, panels)
    return near + jnp.where(side == 0, diagonal, 0.0)


def second_kernel(
    first,
    second,
    width,
    band,
    own_ref,
    other_ref,
    rhs_ref,
    self_ref,
    near_ref,
    chosen_ref,
    expand_ref,
    table_ref,
    send_ref,
    out_ref,
):
    boxes, terms, panels = expand_ref.shape
    count = own_ref.shape[0]
    core, side = lax.axis_index("core"), lax.axis_index("side")
    rows = width * boxes
    high = (terms // LANES) * band + rows // 2
    sources = sources_of(own_ref[:, high:, :].astype(FULL))
    total = local_of(first, (own_ref, other_ref), table_ref, sources, band)
    local = jnp.where(core == 0, total, pltpu.roll(total, band, 1)).astype(HALF)
    base = base_of(first, width, (terms // LANES) * band, own_ref, rhs_ref, self_ref, near_ref, chosen_ref)
    image = far_of(local, expand_ref, side * (terms // 2)) + base
    half = image.astype(HALF)
    sent = sent_of(multipoles_of(half, expand_ref), send_ref[...]).astype(HALF).reshape(count, -1, LANES)

    def put(target):
        for part in range(2):
            place = spot(second, 2 * target + part)
            out_ref[place, :rows, :] = half
            out_ref[place, rows:, :] = sent[spot(first, target)]

    if second is None:
        out_ref[...] = jnp.concatenate(
            [jnp.broadcast_to(half[None, None], (count, 2, rows, LANES)), jnp.stack([sent, sent], axis=1)], axis=2
        ).reshape(out_ref.shape)
    else:
        each(count, put)


def joined(order, parts_ref, place):
    first, second = spot(order, 2 * place), spot(order, 2 * place + 1)
    return parts_ref[first].astype(FULL) + parts_ref[second].astype(FULL)


def field_kernel(order, parts_ref, out_ref):
    out_ref[...] = joined(order, parts_ref, lax.axis_index("box"))[: out_ref.shape[0]]


def rest_of(order, width, parts_ref, self_ref, near_ref, chosen_ref):
    boxes, panels = self_ref.shape
    count = parts_ref.shape[0] // 2
    index = lax.axis_index("box")
    rows = width * boxes
    pieces = [joined(order, parts_ref, jnp.clip(index + step, 0, count - 1))[:rows] for step in (-1, 0, 1)]
    near = near_of(near_ref, chosen_ref, extended_of(pieces, index, count, boxes), boxes, width)
    field = pieces[1]
    diagonal = ((self_ref[...] - SHIFT)[None] * field.reshape(width, boxes, panels)).reshape(rows, panels)
    return near + diagonal


def third_kernel(
    first,
    second,
    width,
    band,
    own_ref,
    other_ref,
    across_ref,
    corner_ref,
    parts_ref,
    expand_ref,
    table_ref,
    self_ref,
    near_ref,
    chosen_ref,
    field_ref,
    rhs_ref,
    out_ref,
):
    boxes, terms, panels = expand_ref.shape
    core, side = lax.axis_index("core"), lax.axis_index("side")
    rows = width * boxes
    count = parts_ref.shape[0] // 2
    if second is None:
        blocks = parts_ref[:, rows:, :].astype(FULL).reshape(count, 2, -1, LANES)
        blocks = blocks[:, 0] + blocks[:, 1]
    else:
        blocks = jnp.stack([joined(second, parts_ref, place)[rows:] for place in first])
    sources = sources_of(blocks)
    bands = (own_ref, other_ref, across_ref, corner_ref)
    total = local_of(first, bands, table_ref, sources, band)
    halves = [total[:, : 2 * band], total[:, 2 * band :]]
    halves = [jnp.where(core == 0, half, pltpu.roll(half, band, 1)) for half in halves]
    local = jnp.concatenate(
        [jnp.where(side == 0, halves[0], halves[1]), jnp.where(side == 0, halves[1], halves[0])], axis=1
    ).astype(HALF)
    last = rest_of(second, width, parts_ref, self_ref, near_ref, chosen_ref) + far_of(local, expand_ref, 0)
    field = field_ref[...]
    right = rhs_ref[pl.ds(core * width, width)].reshape(rows, panels)
    spots = lax.broadcasted_iota(jnp.int32, (8, panels), 0)
    lanes = lax.broadcasted_iota(jnp.int32, (8, panels), 1)
    result = jnp.zeros((8, panels), FULL)
    pairs = ((right, right), (right, field), (field, field), (right, last), (field, last), (last, last))
    for number, (one, two) in enumerate(pairs):
        product = one * two
        for rhs in range(width):
            total = jnp.sum(product[rhs * boxes : (rhs + 1) * boxes])
            mine = (spots == number) & (lanes // (panels // width) == rhs)
            result = jnp.where(mine, total, result)

    def put(target):
        out_ref[target] = result

    each(out_ref.shape[0], put)


def last_kernel(order, width, sums_ref, field_ref, other_ref, rhs_ref, out_ref):
    core = lax.axis_index("core")
    rows, panels = field_ref.shape
    boxes = rows // width
    fields = (field_ref[...], other_ref[...])
    part = panels // width
    lanes = lax.broadcasted_iota(jnp.int32, (1, panels), 1)
    for group in range(2):
        total = fold(
            sums_ref.shape[0] // 2,
            lambda number, state: state + sums_ref[spot(order, 2 * number + group)],
            jnp.zeros(sums_ref.shape[1:], FULL),
        )
        rr, ru, uu, rw, uw, ww = (total[number : number + 1] for number in range(6))
        slope = ru / rr
        norm = uu - slope * ru
        first_row = rw - slope * ru
        scale = lax.rsqrt(rr * norm)
        h11 = slope + SHIFT
        h21 = jnp.sqrt(norm / rr)
        h12 = first_row * scale
        h22 = (uw - slope * uu - slope * first_row) / norm
        image = (ww - 2.0 * slope * uw + slope * slope * uu) / norm
        gram_aa = h11 * h11 + h21 * h21
        gram_ab = h11 * h12 + h21 * (h22 + SHIFT)
        gram_bb = image + 2.0 * SHIFT * h22 + SHIFT * SHIFT
        beta = jnp.sqrt(rr)
        right_a, right_b = beta * h11, beta * h12
        determinant = gram_aa * gram_bb - gram_ab * gram_ab
        coef_a = (gram_bb * right_a - gram_ab * right_b) / determinant
        coef_b = (gram_aa * right_b - gram_ab * right_a) / determinant
        weight = coef_b * lax.rsqrt(norm)
        first = coef_a / beta - weight * slope
        chosen = jnp.where(core == group, fields[0], fields[1])
        for rhs in range(width):
            def wide(value):
                inside = jnp.where(lanes // part == rhs, value, 0.0)
                spread = inside
                for step in range(1, width):
                    spread = spread + pltpu.roll(inside, step * part, 1)
                return spread

            place = group * width + rhs
            out_ref[place] = wide(first) * rhs_ref[place] + wide(weight) * chosen[rhs * boxes : (rhs + 1) * boxes]


def call(kernel, outs, *args, fixed=0, scratch=(), flops=0, limit=16):
    vmem = pl.BlockSpec(memory_space=pltpu.VMEM)
    many = isinstance(outs, list)
    held = len(args) - fixed
    args = [
        value if number < held else pltpu.with_memory_space_constraint(value, pltpu.HBM)
        for number, value in enumerate(args)
    ]
    return pl.pallas_call(
        kernel,
        out_shape=outs,
        in_specs=[vmem] * held + [pl.BlockSpec(memory_space=pltpu.HBM)] * fixed,
        out_specs=[vmem] * len(outs) if many else vmem,
        scratch_shapes=list(scratch),
        compiler_params=pltpu.CompilerParams(vmem_limit_bytes=limit * 1024 * 1024),
        cost_estimate=pl.CostEstimate(flops=flops, bytes_accessed=0, transcendentals=0) if flops else None,
    )(*args)


def per_device(
    rhs_field, self_coef, expand, near_ops, class_ops, near_src, send_rows, list_slot, list_class
):
    count = lax.axis_size("box")
    boxes, terms, panels = expand.shape
    width = rhs_field.shape[0] // 2
    rows = width * boxes
    band = class_ops.shape[1]
    cap = send_rows.shape[2]
    parts = terms // LANES
    area = -(-(cap * width * parts) // 8) * 8
    low = parts * band
    swap = [(0, 1), (1, 0)]
    first, second, third = FIRST.get(count), SECOND.get(2 * count), THIRD.get(2 * count)
    shape = jax.ShapeDtypeStruct
    send = jnp.swapaxes(send_rows, 1, 2)[0]
    slot, label = list_slot.T, list_class.T
    block = shape((rows, panels), FULL)
    kernel = functools.partial(call, limit=16 if count <= 16 else 56)

    slots, picks, kept, near, chosen, table = kernel(
        functools.partial(first_kernel, first, width),
        [
            shape((count, low + rows // 2 + area, LANES), HALF),
            shape((count * area, parts * rows), HALF),
            SLOT(expand.shape, HALF),
            SLOT(near_ops.shape, HALF),
            shape((near_ops.shape[0] * boxes, 3 * boxes), HALF),
            shape((-(-count // 8), rows, min(count, 8) * count * cap * width), HALF),
        ],
        rhs_field, expand, class_ops, send, near_ops, near_src, slot, label,
        fixed=8,
        scratch=[
            pltpu.VMEM((width,) + rhs_field.shape[1:], FULL),
            pltpu.VMEM(class_ops.shape, HALF),
            pltpu.SMEM(send.shape, jnp.int32),
            pltpu.VMEM((count * area, parts * rows), FULL),
            pltpu.VMEM(near_src.shape, jnp.int32),
            pltpu.VMEM(slot.shape, jnp.int32),
            pltpu.VMEM(label.shape, jnp.int32),
            pltpu.SemaphoreType.DMA((9,)),
        ],
    )
    own = exchange(slots, "box", first)
    bands = own[:, :low]
    other = lax.ppermute(bands, "core", swap)
    across = lax.ppermute(bands, "side", swap)
    corner = lax.ppermute(across, "core", swap)
    images = kernel(
        functools.partial(second_kernel, first, second, width, band),
        shape((2 * count, rows + area, LANES), HALF),
        own, other, rhs_field, self_coef, near, chosen, kept, table, picks,
    )
    images = exchange(images, ("box", "side"), second)
    field = kernel(functools.partial(field_kernel, second), block, images)
    field_other = lax.ppermute(field, "core", swap)
    sums = kernel(
        functools.partial(third_kernel, first, second, width, band),
        SLOT((2 * count, 8, panels), FULL),
        bands, other, across, corner, images, kept, table, self_coef, near, chosen, field, rhs_field,
    )
    sums, field_other = lax.optimization_barrier((sums, field_other))
    sums = exchange(sums, ("box", "core"), third)
    return kernel(
        functools.partial(last_kernel, third, width),
        shape(rhs_field.shape, FULL),
        sums, field, field_other, rhs_field,
    )


def solution(mesh):
    count, levels = mesh.devices.shape
    finer = Mesh(mesh.devices.reshape(count, levels // 2, 2), ("box", "side", "core"))
    return jax.shard_map(
        per_device,
        mesh=finer,
        in_specs=(
            P(None, "box", None),
            P("box", None),
            P("box", None, None),
            P(),
            P("box", ("side", "core"), None),
            P("box", None),
            P("box", None, None),
            P("box", None),
            P("box", None),
        ),
        out_specs=P(None, "box", None),
        check_vma=False,
    )
```

```python
import functools

import jax
import jax.numpy as jnp
from jax import lax
from jax.experimental import pallas as pl
from jax.experimental.pallas import tpu as pltpu
from jax.sharding import Mesh, PartitionSpec as P

SHIFT = 3.0
LANES = 128
HALF = jnp.bfloat16
FULL = jnp.float32
SLOT = pltpu.VMEM
FIRST = {8: (5, 7, 0, 4, 6, 3, 1, 2)}
SECOND = {16: (10, 8, 3, 7, 2, 14, 5, 1, 11, 9, 15, 13, 12, 6, 4, 0)}
THIRD = {16: (11, 9, 13, 8, 14, 5, 7, 4, 12, 1, 15, 3, 0, 6, 2, 10)}


def spot(order, member):
    if order is None:
        return member
    if isinstance(member, int):
        return order.index(member)
    result = jnp.zeros_like(member)
    for number, value in enumerate(order):
        result = jnp.where(member == value, number, result)
    return result


def exchange(value, axes, order):
    groups = None if order is None else [list(order)]
    return lax.all_to_all(value, axes, 0, 0, tiled=True, axis_index_groups=groups)


def each(count, body):
    if count <= 32:
        for number in range(count):
            body(number)
    else:
        lax.fori_loop(0, count, lambda number, state: (body(number), state)[1], 0)


def fold(count, body, state):
    if count <= 32:
        for number in range(count):
            state = body(number, state)
        return state
    return lax.fori_loop(0, count, body, state)


def dot_nt(left, right):
    return lax.dot_general(left, right, (((1,), (1,)), ((), ())), preferred_element_type=FULL)


def dot_nn(left, right):
    return lax.dot_general(left, right, (((1,), (0,)), ((), ())), preferred_element_type=FULL)


def own_rows(values, result, box, boxes):
    row = lax.broadcasted_iota(jnp.int32, result.shape, 0)
    return jnp.where(row % boxes == box, values, result)


def multipoles_of(field, expand_ref):
    boxes, terms, _ = expand_ref.shape
    result = jnp.zeros((field.shape[0], terms), FULL)
    for box in range(boxes):
        result = own_rows(dot_nt(field, expand_ref[box]), result, box, boxes)
    return result


def send_table(order, send_ref, out_ref, boxes, width, parts):
    cap, targets = send_ref.shape
    area = out_ref.shape[0] // targets
    row = lax.broadcasted_iota(jnp.int32, (area, out_ref.shape[1]), 0)
    column = lax.broadcasted_iota(jnp.int32, (area, out_ref.shape[1]), 1)
    start = jnp.where(row < cap * width * parts, (row // cap) * boxes, -boxes)

    def put(target):
        place = start
        for turn in range(cap):
            place = jnp.where(row % cap == turn, start + send_ref[turn, target], place)
        begin = spot(order, target) * area
        if not isinstance(target, int):
            begin = pl.multiple_of(begin, area)
        out_ref[pl.ds(begin, area), :] = jnp.where(place == column, 1.0, 0.0)

    each(targets, put)


def sent_of(multipoles, table):
    half = multipoles.astype(HALF)
    parts = half.shape[1] // LANES
    stacked = jnp.concatenate([half[:, part * LANES : (part + 1) * LANES] for part in range(parts)], axis=0)
    return dot_nn(table, stacked)


def far_of(local, expand_ref, offset):
    boxes = expand_ref.shape[0]
    row = lax.broadcasted_iota(jnp.int32, local.shape, 0)
    left = [jnp.where(row % boxes == box, local, jnp.zeros_like(local)) for box in range(boxes)]
    right = [expand_ref[box, pl.ds(offset, local.shape[1]), :] for box in range(boxes)]
    return dot_nn(jnp.concatenate(left, axis=1), jnp.concatenate(right, axis=0))


def near_of(near_ref, chosen_ref, extended, boxes, width):
    picked = dot_nn(chosen_ref[...], extended).astype(HALF)
    classes = near_ref.shape[0]
    result = jnp.zeros((width * boxes, near_ref.shape[1]), FULL)
    for first in range(0, classes, 2):
        group = range(first, min(first + 2, classes))
        left = [
            jnp.concatenate(
                [
                    picked[number * boxes : (number + 1) * boxes, rhs * LANES : (rhs + 1) * LANES]
                    for number in group
                ],
                axis=1,
            )
            for rhs in range(width)
        ]
        right = [near_ref[number] for number in group]
        result = result + dot_nt(jnp.concatenate(left, axis=0), jnp.concatenate(right, axis=1))
    return result


def sources_of(blocks):
    count, area, panels = blocks.shape
    half = area // 2
    pairs = blocks.reshape(count // 2, 2, area, panels)
    low, high = pairs[:, 0], pairs[:, 1]
    row = lax.broadcasted_iota(jnp.int32, low.shape, 1)
    moved_low, moved_high = pltpu.roll(low, half, 1), pltpu.roll(high, half, 1)
    first = jnp.where(row < half, low, moved_high).reshape(-1, panels)
    second = jnp.where(row < half, moved_low, high).reshape(-1, panels)
    return jnp.concatenate([first, second], axis=1).astype(HALF)


def local_of(order, bands, table_ref, sources, band):
    classes = bands[0].shape[0]
    group = classes // table_ref.shape[0]
    parts = sources.shape[1] // LANES

    def add(number, total):
        images = []
        for turn in range(group):
            right = [
                jnp.concatenate(
                    [
                        ref[spot(order, number * group + turn), part * band : (part + 1) * band, :]
                        for part in range(parts)
                    ],
                    axis=1,
                )
                for ref in bands
            ]
            images.append(dot_nt(sources, jnp.concatenate(right, axis=0)))
        images = jnp.concatenate(images, axis=0)
        upper = images.astype(HALF)
        lower = (images - upper.astype(FULL)).astype(HALF)
        table = table_ref[number]
        return total + (dot_nn(table, upper) + dot_nn(table, lower))

    return fold(table_ref.shape[0], add, jnp.zeros((table_ref.shape[1], len(bands) * band), FULL))


def extended_of(pieces, index, count, boxes):
    low = jnp.where(index > 0, pieces[0], jnp.zeros_like(pieces[0]))
    high = jnp.where(index < count - 1, pieces[2], jnp.zeros_like(pieces[2]))
    width = low.shape[0] // boxes
    columns = [
        jnp.concatenate([piece[rhs * boxes : (rhs + 1) * boxes] for piece in (low, pieces[1], high)], axis=0)
        for rhs in range(width)
    ]
    return jnp.concatenate(columns, axis=1).astype(HALF)


def fetch(pairs, signals):
    copies = [
        pltpu.make_async_copy(source, target, signals.at[number])
        for number, (source, target) in enumerate(pairs)
    ]
    for copy in copies:
        copy.start()
    return copies


def near_table(source_ref, chosen_ref):
    boxes, classes = source_ref.shape
    spots = lax.broadcasted_iota(jnp.int32, (boxes, chosen_ref.shape[1]), 1)
    for number in range(classes):
        match = source_ref[:, number : number + 1] == spots
        chosen_ref[number * boxes : (number + 1) * boxes, :] = jnp.where(match, 1.0, 0.0).astype(HALF)


def list_table(order, cap, width, kinds, slot_ref, label_ref, table_ref):
    boxes = slot_ref.shape[1]
    groups, rows, columns = table_ref.shape
    slots, labels = slot_ref[...], label_ref[...]
    places = spot(order, slots // cap) * (cap * width) + slots % cap
    group = kinds // groups
    received = columns // group

    def put(number):
        blocks = []
        for turn in range(group):
            place = jnp.max(jnp.where(labels == number * group + turn, places + 1, 0), axis=0, keepdims=True) - 1
            place = jnp.concatenate([jnp.where(place >= 0, place + rhs * cap, -1) for rhs in range(width)], axis=1)
            spot = lax.broadcasted_iota(jnp.int32, (received, rows), 0)
            blocks.append(jnp.where(place == spot, 1.0, 0.0))
        table_ref[number] = jnp.concatenate(blocks, axis=0).T.astype(HALF)

    each(groups, put)


def first_kernel(
    order,
    width,
    rhs_hbm,
    expand_hbm,
    class_hbm,
    send_hbm,
    near_hbm,
    source_hbm,
    slot_hbm,
    label_hbm,
    out_ref,
    picks_ref,
    expand_ref,
    near_ref,
    chosen_ref,
    table_ref,
    rhs_ref,
    class_ref,
    send_ref,
    wide_ref,
    source_ref,
    slot_ref,
    label_ref,
    signals,
):
    boxes, terms, panels = expand_ref.shape
    core, side = lax.axis_index("core"), lax.axis_index("side")
    step = boxes // 2
    pairs = [
        (send_hbm, send_ref),
        (rhs_hbm.at[pl.ds(core * width, width)], rhs_ref),
        (class_hbm, class_ref),
        (source_hbm, source_ref),
        (slot_hbm, slot_ref),
        (label_hbm, label_ref),
    ]
    for chunk in range(2):
        part = pl.ds(chunk * step, step)
        pairs.append((expand_hbm.at[part], expand_ref.at[part]))
    pairs.append((near_hbm, near_ref))
    copies = fetch(pairs, signals)
    copies[0].wait()
    send_table(order, send_ref, wide_ref, boxes, width, terms // LANES)
    picks_ref[...] = wide_ref[...].astype(HALF)
    band = class_ref.shape[1]
    low = (terms // LANES) * band
    high = low + width * (boxes // 2)
    copies[1].wait()
    copies[2].wait()
    shown = rhs_ref[:, pl.ds(side * (boxes // 2), boxes // 2), :].reshape(high - low, panels).astype(HALF)
    field = rhs_ref[...].reshape(width * boxes, panels).astype(HALF)
    operators = jnp.concatenate(
        [class_ref[0][:, part * LANES : (part + 1) * LANES] for part in range(terms // LANES)], axis=0
    )

    def put(target):
        place = spot(order, target)
        out_ref[place, :low, :] = operators
        out_ref[place, low:high, :] = shown

    each(out_ref.shape[0], put)
    for copy in copies[3:6]:
        copy.wait()
    near_table(source_ref, chosen_ref)
    list_table(order, send_ref.shape[0], width, out_ref.shape[0], slot_ref, label_ref, table_ref)
    result = jnp.zeros((width * boxes, terms), FULL)
    for box in range(boxes):
        if box % step == 0:
            copies[6 + box // step].wait()
        result = own_rows(dot_nt(field, expand_ref[box]), result, box, boxes)
    sent = sent_of(result, picks_ref[...]).astype(HALF)
    out_ref[:, high:, :] = sent.reshape(out_ref.shape[0], -1, LANES)
    copies[8].wait()


def base_of(order, width, low, own_ref, rhs_ref, self_ref, near_ref, chosen_ref):
    boxes, panels = self_ref.shape
    count = own_ref.shape[0]
    core, side, index = lax.axis_index("core"), lax.axis_index("side"), lax.axis_index("box")
    half = boxes // 2
    empty = jnp.zeros((half, panels), FULL)
    pieces = []
    for step in (-1, 0, 1):
        shown = own_ref[spot(order, jnp.clip(index + step, 0, count - 1)), low : low + width * half, :].astype(FULL)
        rows = []
        for rhs in range(width):
            part = shown[rhs * half : (rhs + 1) * half]
            rows += [jnp.where(side == 0, part, empty), jnp.where(side == 0, empty, part)]
        pieces.append(jnp.concatenate(rows, axis=0))
    near = near_of(near_ref, chosen_ref, extended_of(pieces, index, count, boxes), boxes, width)
    field = rhs_ref[pl.ds(core * width, width)]
    diagonal = ((self_ref[...] - SHIFT)[None] * field).reshape(width * boxes, panels)
    return near + jnp.where(side == 0, diagonal, 0.0)


def second_kernel(
    first,
    second,
    width,
    band,
    own_ref,
    other_ref,
    rhs_ref,
    self_ref,
    near_ref,
    chosen_ref,
    expand_ref,
    table_ref,
    send_ref,
    out_ref,
):
    boxes, terms, panels = expand_ref.shape
    count = own_ref.shape[0]
    core, side = lax.axis_index("core"), lax.axis_index("side")
    rows = width * boxes
    high = (terms // LANES) * band + rows // 2
    sources = sources_of(own_ref[:, high:, :].astype(FULL))
    total = local_of(first, (own_ref, other_ref), table_ref, sources, band)
    local = jnp.where(core == 0, total, pltpu.roll(total, band, 1)).astype(HALF)
    base = base_of(first, width, (terms // LANES) * band, own_ref, rhs_ref, self_ref, near_ref, chosen_ref)
    image = far_of(local, expand_ref, side * (terms // 2)) + base
    half = image.astype(HALF)
    sent = sent_of(multipoles_of(half, expand_ref), send_ref[...]).astype(HALF).reshape(count, -1, LANES)

    def put(target):
        for part in range(2):
            place = spot(second, 2 * target + part)
            out_ref[place, :rows, :] = half
            out_ref[place, rows:, :] = sent[spot(first, target)]

    if second is None:
        out_ref[...] = jnp.concatenate(
            [jnp.broadcast_to(half[None, None], (count, 2, rows, LANES)), jnp.stack([sent, sent], axis=1)], axis=2
        ).reshape(out_ref.shape)
    else:
        each(count, put)


def joined(order, parts_ref, place):
    first, second = spot(order, 2 * place), spot(order, 2 * place + 1)
    return parts_ref[first].astype(FULL) + parts_ref[second].astype(FULL)


def field_kernel(order, parts_ref, out_ref):
    out_ref[...] = joined(order, parts_ref, lax.axis_index("box"))[: out_ref.shape[0]]


def rest_of(order, width, parts_ref, self_ref, near_ref, chosen_ref):
    boxes, panels = self_ref.shape
    count = parts_ref.shape[0] // 2
    index = lax.axis_index("box")
    rows = width * boxes
    pieces = [joined(order, parts_ref, jnp.clip(index + step, 0, count - 1))[:rows] for step in (-1, 0, 1)]
    near = near_of(near_ref, chosen_ref, extended_of(pieces, index, count, boxes), boxes, width)
    field = pieces[1]
    diagonal = ((self_ref[...] - SHIFT)[None] * field.reshape(width, boxes, panels)).reshape(rows, panels)
    return near + diagonal


def third_kernel(
    first,
    second,
    width,
    band,
    own_ref,
    other_ref,
    across_ref,
    corner_ref,
    parts_ref,
    expand_ref,
    table_ref,
    self_ref,
    near_ref,
    chosen_ref,
    field_ref,
    rhs_ref,
    out_ref,
):
    boxes, terms, panels = expand_ref.shape
    core, side = lax.axis_index("core"), lax.axis_index("side")
    rows = width * boxes
    count = parts_ref.shape[0] // 2
    if second is None:
        blocks = parts_ref[:, rows:, :].astype(FULL).reshape(count, 2, -1, LANES)
        blocks = blocks[:, 0] + blocks[:, 1]
    else:
        blocks = jnp.stack([joined(second, parts_ref, place)[rows:] for place in first])
    sources = sources_of(blocks)
    bands = (own_ref, other_ref, across_ref, corner_ref)
    total = local_of(first, bands, table_ref, sources, band)
    halves = [total[:, : 2 * band], total[:, 2 * band :]]
    halves = [jnp.where(core == 0, half, pltpu.roll(half, band, 1)) for half in halves]
    local = jnp.concatenate(
        [jnp.where(side == 0, halves[0], halves[1]), jnp.where(side == 0, halves[1], halves[0])], axis=1
    ).astype(HALF)
    last = rest_of(second, width, parts_ref, self_ref, near_ref, chosen_ref) + far_of(local, expand_ref, 0)
    field = field_ref[...]
    right = rhs_ref[pl.ds(core * width, width)].reshape(rows, panels)
    spots = lax.broadcasted_iota(jnp.int32, (8, panels), 0)
    lanes = lax.broadcasted_iota(jnp.int32, (8, panels), 1)
    result = jnp.zeros((8, panels), FULL)
    pairs = ((right, right), (right, field), (field, field), (right, last), (field, last), (last, last))
    for number, (one, two) in enumerate(pairs):
        product = one * two
        for rhs in range(width):
            total = jnp.sum(product[rhs * boxes : (rhs + 1) * boxes])
            mine = (spots == number) & (lanes // (panels // width) == rhs)
            result = jnp.where(mine, total, result)

    def put(target):
        out_ref[target] = result

    each(out_ref.shape[0], put)


def last_kernel(order, width, sums_ref, field_ref, other_ref, rhs_ref, out_ref):
    core = lax.axis_index("core")
    rows, panels = field_ref.shape
    boxes = rows // width
    fields = (field_ref[...], other_ref[...])
    part = panels // width
    lanes = lax.broadcasted_iota(jnp.int32, (1, panels), 1)
    for group in range(2):
        total = fold(
            sums_ref.shape[0] // 2,
            lambda number, state: state + sums_ref[spot(order, 2 * number + group)],
            jnp.zeros(sums_ref.shape[1:], FULL),
        )
        rr, ru, uu, rw, uw, ww = (total[number : number + 1] for number in range(6))
        slope = ru / rr
        norm = uu - slope * ru
        first_row = rw - slope * ru
        scale = lax.rsqrt(rr) * lax.rsqrt(norm)
        h11 = slope + SHIFT
        h21 = jnp.sqrt(norm / rr)
        h12 = first_row * scale
        h22 = (uw - slope * uu - slope * first_row) / norm
        image = (ww - 2.0 * slope * uw + slope * slope * uu) / norm
        gram_aa = h11 * h11 + h21 * h21
        gram_ab = h11 * h12 + h21 * (h22 + SHIFT)
        gram_bb = image + 2.0 * SHIFT * h22 + SHIFT * SHIFT
        beta = jnp.sqrt(rr)
        right_a, right_b = beta * h11, beta * h12
        determinant = gram_aa * gram_bb - gram_ab * gram_ab
        coef_a = (gram_bb * right_a - gram_ab * right_b) / determinant
        coef_b = (gram_aa * right_b - gram_ab * right_a) / determinant
        weight = coef_b * lax.rsqrt(norm)
        first = coef_a / beta - weight * slope
        chosen = jnp.where(core == group, fields[0], fields[1])
        for rhs in range(width):
            def wide(value):
                inside = jnp.where(lanes // part == rhs, value, 0.0)
                spread = inside
                for step in range(1, width):
                    spread = spread + pltpu.roll(inside, step * part, 1)
                return spread

            place = group * width + rhs
            out_ref[place] = wide(first) * rhs_ref[place] + wide(weight) * chosen[rhs * boxes : (rhs + 1) * boxes]


def call(kernel, outs, *args, fixed=0, scratch=(), flops=0, limit=16):
    vmem = pl.BlockSpec(memory_space=pltpu.VMEM)
    many = isinstance(outs, list)
    held = len(args) - fixed
    args = [
        value if number < held else pltpu.with_memory_space_constraint(value, pltpu.HBM)
        for number, value in enumerate(args)
    ]
    return pl.pallas_call(
        kernel,
        out_shape=outs,
        in_specs=[vmem] * held + [pl.BlockSpec(memory_space=pltpu.HBM)] * fixed,
        out_specs=[vmem] * len(outs) if many else vmem,
        scratch_shapes=list(scratch),
        compiler_params=pltpu.CompilerParams(vmem_limit_bytes=limit * 1024 * 1024),
        cost_estimate=pl.CostEstimate(flops=flops, bytes_accessed=0, transcendentals=0) if flops else None,
    )(*args)


def per_device(
    rhs_field, self_coef, expand, near_ops, class_ops, near_src, send_rows, list_slot, list_class
):
    count = lax.axis_size("box")
    boxes, terms, panels = expand.shape
    width = rhs_field.shape[0] // 2
    rows = width * boxes
    band = class_ops.shape[1]
    cap = send_rows.shape[2]
    parts = terms // LANES
    area = -(-(cap * width * parts) // 8) * 8
    low = parts * band
    swap = [(0, 1), (1, 0)]
    first, second, third = FIRST.get(count), SECOND.get(2 * count), THIRD.get(2 * count)
    shape = jax.ShapeDtypeStruct
    send = jnp.swapaxes(send_rows, 1, 2)[0]
    slot, label = list_slot.T, list_class.T
    block = shape((rows, panels), FULL)
    kernel = functools.partial(call, limit=16 if count <= 16 else 56)

    slots, picks, kept, near, chosen, table = kernel(
        functools.partial(first_kernel, first, width),
        [
            shape((count, low + rows // 2 + area, LANES), HALF),
            shape((count * area, parts * rows), HALF),
            SLOT(expand.shape, HALF),
            SLOT(near_ops.shape, HALF),
            shape((near_ops.shape[0] * boxes, 3 * boxes), HALF),
            shape((-(-count // 8), rows, min(count, 8) * count * cap * width), HALF),
        ],
        rhs_field, expand, class_ops, send, near_ops, near_src, slot, label,
        fixed=8,
        scratch=[
            pltpu.VMEM((width,) + rhs_field.shape[1:], FULL),
            pltpu.VMEM(class_ops.shape, HALF),
            pltpu.SMEM(send.shape, jnp.int32),
            pltpu.VMEM((count * area, parts * rows), FULL),
            pltpu.VMEM(near_src.shape, jnp.int32),
            pltpu.VMEM(slot.shape, jnp.int32),
            pltpu.VMEM(label.shape, jnp.int32),
            pltpu.SemaphoreType.DMA((9,)),
        ],
    )
    own = exchange(slots, "box", first)
    bands = own[:, :low]
    other = lax.ppermute(bands, "core", swap)
    across = lax.ppermute(bands, "side", swap)
    corner = lax.ppermute(across, "core", swap)
    images = kernel(
        functools.partial(second_kernel, first, second, width, band),
        shape((2 * count, rows + area, LANES), HALF),
        own, other, rhs_field, self_coef, near, chosen, kept, table, picks,
    )
    images = exchange(images, ("box", "side"), second)
    field = kernel(functools.partial(field_kernel, second), block, images)
    field_other = lax.ppermute(field, "core", swap)
    sums = kernel(
        functools.partial(third_kernel, first, second, width, band),
        SLOT((2 * count, 8, panels), FULL),
        bands, other, across, corner, images, kept, table, self_coef, near, chosen, field, rhs_field,
    )
    sums, field_other = lax.optimization_barrier((sums, field_other))
    sums = exchange(sums, ("box", "core"), third)
    return kernel(
        functools.partial(last_kernel, third, width),
        shape(rhs_field.shape, FULL),
        sums, field, field_other, rhs_field,
    )


def solution(mesh):
    count, levels = mesh.devices.shape
    finer = Mesh(mesh.devices.reshape(count, levels // 2, 2), ("box", "side", "core"))
    return jax.shard_map(
        per_device,
        mesh=finer,
        in_specs=(
            P(None, "box", None),
            P("box", None),
            P("box", None, None),
            P(),
            P("box", ("side", "core"), None),
            P("box", None),
            P("box", None, None),
            P("box", None),
            P("box", None),
        ),
        out_specs=P(None, "box", None),
        check_vma=False,
    )
```

```python
import functools

import jax
import jax.numpy as jnp
from jax import lax
from jax.experimental import pallas as pl
from jax.experimental.pallas import tpu as pltpu
from jax.sharding import Mesh, PartitionSpec as P

SHIFT = 3.0
LANES = 128
HALF = jnp.bfloat16
FULL = jnp.float32
SLOT = pltpu.VMEM
FIRST = {8: (5, 7, 0, 4, 6, 3, 1, 2)}
SECOND = {16: (10, 8, 3, 1, 2, 14, 5, 7, 11, 9, 15, 13, 12, 6, 4, 0)}
THIRD = {16: (11, 9, 13, 8, 14, 5, 7, 4, 12, 1, 15, 3, 0, 6, 2, 10)}


def spot(order, member):
    if order is None:
        return member
    if isinstance(member, int):
        return order.index(member)
    result = jnp.zeros_like(member)
    for number, value in enumerate(order):
        result = jnp.where(member == value, number, result)
    return result


def exchange(value, axes, order):
    groups = None if order is None else [list(order)]
    return lax.all_to_all(value, axes, 0, 0, tiled=True, axis_index_groups=groups)


def each(count, body):
    if count <= 32:
        for number in range(count):
            body(number)
    else:
        lax.fori_loop(0, count, lambda number, state: (body(number), state)[1], 0)


def fold(count, body, state):
    if count <= 32:
        for number in range(count):
            state = body(number, state)
        return state
    return lax.fori_loop(0, count, body, state)


def dot_nt(left, right):
    return lax.dot_general(left, right, (((1,), (1,)), ((), ())), preferred_element_type=FULL)


def dot_nn(left, right):
    return lax.dot_general(left, right, (((1,), (0,)), ((), ())), preferred_element_type=FULL)


def own_rows(values, result, box, boxes):
    row = lax.broadcasted_iota(jnp.int32, result.shape, 0)
    return jnp.where(row % boxes == box, values, result)


def multipoles_of(field, expand_ref):
    boxes, terms, _ = expand_ref.shape
    result = jnp.zeros((field.shape[0], terms), FULL)
    for box in range(boxes):
        result = own_rows(dot_nt(field, expand_ref[box]), result, box, boxes)
    return result


def send_table(order, send_ref, out_ref, boxes, width, parts):
    cap, targets = send_ref.shape
    area = out_ref.shape[0] // targets
    row = lax.broadcasted_iota(jnp.int32, (area, out_ref.shape[1]), 0)
    column = lax.broadcasted_iota(jnp.int32, (area, out_ref.shape[1]), 1)
    start = jnp.where(row < cap * width * parts, (row // cap) * boxes, -boxes)

    def put(target):
        place = start
        for turn in range(cap):
            place = jnp.where(row % cap == turn, start + send_ref[turn, target], place)
        begin = spot(order, target) * area
        if not isinstance(target, int):
            begin = pl.multiple_of(begin, area)
        out_ref[pl.ds(begin, area), :] = jnp.where(place == column, 1.0, 0.0)

    each(targets, put)


def sent_of(multipoles, table):
    half = multipoles.astype(HALF)
    parts = half.shape[1] // LANES
    stacked = jnp.concatenate([half[:, part * LANES : (part + 1) * LANES] for part in range(parts)], axis=0)
    return dot_nn(table, stacked)


def far_of(local, expand_ref, offset):
    boxes = expand_ref.shape[0]
    row = lax.broadcasted_iota(jnp.int32, local.shape, 0)
    left = [jnp.where(row % boxes == box, local, jnp.zeros_like(local)) for box in range(boxes)]
    right = [expand_ref[box, pl.ds(offset, local.shape[1]), :] for box in range(boxes)]
    return dot_nn(jnp.concatenate(left, axis=1), jnp.concatenate(right, axis=0))


def near_of(near_ref, chosen_ref, extended, boxes, width):
    picked = dot_nn(chosen_ref[...], extended).astype(HALF)
    classes = near_ref.shape[0]
    result = jnp.zeros((width * boxes, near_ref.shape[1]), FULL)
    for first in range(0, classes, 2):
        group = range(first, min(first + 2, classes))
        left = [
            jnp.concatenate(
                [
                    picked[number * boxes : (number + 1) * boxes, rhs * LANES : (rhs + 1) * LANES]
                    for number in group
                ],
                axis=1,
            )
            for rhs in range(width)
        ]
        right = [near_ref[number] for number in group]
        result = result + dot_nt(jnp.concatenate(left, axis=0), jnp.concatenate(right, axis=1))
    return result


def sources_of(blocks):
    count, area, panels = blocks.shape
    half = area // 2
    pairs = blocks.reshape(count // 2, 2, area, panels)
    low, high = pairs[:, 0], pairs[:, 1]
    row = lax.broadcasted_iota(jnp.int32, low.shape, 1)
    moved_low, moved_high = pltpu.roll(low, half, 1), pltpu.roll(high, half, 1)
    first = jnp.where(row < half, low, moved_high).reshape(-1, panels)
    second = jnp.where(row < half, moved_low, high).reshape(-1, panels)
    return jnp.concatenate([first, second], axis=1).astype(HALF)


def local_of(order, bands, table_ref, sources, band):
    classes = bands[0].shape[0]
    group = classes // table_ref.shape[0]
    parts = sources.shape[1] // LANES

    def add(number, total):
        images = []
        for turn in range(group):
            right = [
                jnp.concatenate(
                    [
                        ref[spot(order, number * group + turn), part * band : (part + 1) * band, :]
                        for part in range(parts)
                    ],
                    axis=1,
                )
                for ref in bands
            ]
            images.append(dot_nt(sources, jnp.concatenate(right, axis=0)))
        images = jnp.concatenate(images, axis=0).astype(HALF)
        return total + dot_nn(table_ref[number], images)

    return fold(table_ref.shape[0], add, jnp.zeros((table_ref.shape[1], len(bands) * band), FULL))


def extended_of(pieces, index, count, boxes):
    low = jnp.where(index > 0, pieces[0], jnp.zeros_like(pieces[0]))
    high = jnp.where(index < count - 1, pieces[2], jnp.zeros_like(pieces[2]))
    width = low.shape[0] // boxes
    columns = [
        jnp.concatenate([piece[rhs * boxes : (rhs + 1) * boxes] for piece in (low, pieces[1], high)], axis=0)
        for rhs in range(width)
    ]
    return jnp.concatenate(columns, axis=1).astype(HALF)


def fetch(pairs, signals):
    copies = [
        pltpu.make_async_copy(source, target, signals.at[number])
        for number, (source, target) in enumerate(pairs)
    ]
    for copy in copies:
        copy.start()
    return copies


def near_table(source_ref, chosen_ref):
    boxes, classes = source_ref.shape
    spots = lax.broadcasted_iota(jnp.int32, (boxes, chosen_ref.shape[1]), 1)
    for number in range(classes):
        match = source_ref[:, number : number + 1] == spots
        chosen_ref[number * boxes : (number + 1) * boxes, :] = jnp.where(match, 1.0, 0.0).astype(HALF)


def list_table(order, cap, width, kinds, slot_ref, label_ref, table_ref):
    boxes = slot_ref.shape[1]
    groups, rows, columns = table_ref.shape
    slots, labels = slot_ref[...], label_ref[...]
    places = spot(order, slots // cap) * (cap * width) + slots % cap
    group = kinds // groups
    received = columns // group

    def put(number):
        blocks = []
        for turn in range(group):
            place = jnp.max(jnp.where(labels == number * group + turn, places + 1, 0), axis=0, keepdims=True) - 1
            place = jnp.concatenate([jnp.where(place >= 0, place + rhs * cap, -1) for rhs in range(width)], axis=1)
            spot = lax.broadcasted_iota(jnp.int32, (received, rows), 0)
            blocks.append(jnp.where(place == spot, 1.0, 0.0))
        table_ref[number] = jnp.concatenate(blocks, axis=0).T.astype(HALF)

    each(groups, put)


def first_kernel(
    order,
    width,
    rhs_hbm,
    expand_hbm,
    class_hbm,
    send_hbm,
    near_hbm,
    source_hbm,
    slot_hbm,
    label_hbm,
    out_ref,
    picks_ref,
    expand_ref,
    near_ref,
    chosen_ref,
    table_ref,
    rhs_ref,
    class_ref,
    send_ref,
    wide_ref,
    source_ref,
    slot_ref,
    label_ref,
    signals,
):
    boxes, terms, panels = expand_ref.shape
    core, side = lax.axis_index("core"), lax.axis_index("side")
    step = boxes // 2
    pairs = [
        (send_hbm, send_ref),
        (rhs_hbm.at[pl.ds(core * width, width)], rhs_ref),
        (class_hbm, class_ref),
        (source_hbm, source_ref),
        (slot_hbm, slot_ref),
        (label_hbm, label_ref),
    ]
    for chunk in range(2):
        part = pl.ds(chunk * step, step)
        pairs.append((expand_hbm.at[part], expand_ref.at[part]))
    pairs.append((near_hbm, near_ref))
    copies = fetch(pairs, signals)
    copies[0].wait()
    send_table(order, send_ref, wide_ref, boxes, width, terms // LANES)
    picks_ref[...] = wide_ref[...].astype(HALF)
    band = class_ref.shape[1]
    low = (terms // LANES) * band
    high = low + width * (boxes // 2)
    copies[1].wait()
    copies[2].wait()
    shown = rhs_ref[:, pl.ds(side * (boxes // 2), boxes // 2), :].reshape(high - low, panels).astype(HALF)
    field = rhs_ref[...].reshape(width * boxes, panels).astype(HALF)
    operators = jnp.concatenate(
        [class_ref[0][:, part * LANES : (part + 1) * LANES] for part in range(terms // LANES)], axis=0
    )

    def put(target):
        place = spot(order, target)
        out_ref[place, :low, :] = operators
        out_ref[place, low:high, :] = shown

    each(out_ref.shape[0], put)
    for copy in copies[3:6]:
        copy.wait()
    near_table(source_ref, chosen_ref)
    list_table(order, send_ref.shape[0], width, out_ref.shape[0], slot_ref, label_ref, table_ref)
    result = jnp.zeros((width * boxes, terms), FULL)
    for box in range(boxes):
        if box % step == 0:
            copies[6 + box // step].wait()
        result = own_rows(dot_nt(field, expand_ref[box]), result, box, boxes)
    sent = sent_of(result, picks_ref[...]).astype(HALF)
    out_ref[:, high:, :] = sent.reshape(out_ref.shape[0], -1, LANES)
    copies[8].wait()


def base_of(order, width, low, own_ref, rhs_ref, self_ref, near_ref, chosen_ref):
    boxes, panels = self_ref.shape
    count = own_ref.shape[0]
    core, side, index = lax.axis_index("core"), lax.axis_index("side"), lax.axis_index("box")
    half = boxes // 2
    empty = jnp.zeros((half, panels), FULL)
    pieces = []
    for step in (-1, 0, 1):
        shown = own_ref[spot(order, jnp.clip(index + step, 0, count - 1)), low : low + width * half, :].astype(FULL)
        rows = []
        for rhs in range(width):
            part = shown[rhs * half : (rhs + 1) * half]
            rows += [jnp.where(side == 0, part, empty), jnp.where(side == 0, empty, part)]
        pieces.append(jnp.concatenate(rows, axis=0))
    near = near_of(near_ref, chosen_ref, extended_of(pieces, index, count, boxes), boxes, width)
    field = rhs_ref[pl.ds(core * width, width)]
    diagonal = ((self_ref[...] - SHIFT)[None] * field).reshape(width * boxes, panels)
    return near + jnp.where(side == 0, diagonal, 0.0)


def second_kernel(
    first,
    second,
    width,
    band,
    own_ref,
    other_ref,
    rhs_ref,
    self_ref,
    near_ref,
    chosen_ref,
    expand_ref,
    table_ref,
    send_ref,
    out_ref,
):
    boxes, terms, panels = expand_ref.shape
    count = own_ref.shape[0]
    core, side = lax.axis_index("core"), lax.axis_index("side")
    rows = width * boxes
    high = (terms // LANES) * band + rows // 2
    sources = sources_of(own_ref[:, high:, :].astype(FULL))
    total = local_of(first, (own_ref, other_ref), table_ref, sources, band)
    local = jnp.where(core == 0, total, pltpu.roll(total, band, 1)).astype(HALF)
    base = base_of(first, width, (terms // LANES) * band, own_ref, rhs_ref, self_ref, near_ref, chosen_ref)
    image = far_of(local, expand_ref, side * (terms // 2)) + base
    half = image.astype(HALF)
    sent = sent_of(multipoles_of(half, expand_ref), send_ref[...]).astype(HALF).reshape(count, -1, LANES)

    def put(target):
        for part in range(2):
            place = spot(second, 2 * target + part)
            out_ref[place, :rows, :] = half
            out_ref[place, rows:, :] = sent[spot(first, target)]

    if second is None:
        out_ref[...] = jnp.concatenate(
            [jnp.broadcast_to(half[None, None], (count, 2, rows, LANES)), jnp.stack([sent, sent], axis=1)], axis=2
        ).reshape(out_ref.shape)
    else:
        each(count, put)


def joined(order, parts_ref, place):
    first, second = spot(order, 2 * place), spot(order, 2 * place + 1)
    return parts_ref[first].astype(FULL) + parts_ref[second].astype(FULL)


def field_kernel(order, parts_ref, out_ref):
    out_ref[...] = joined(order, parts_ref, lax.axis_index("box"))[: out_ref.shape[0]]


def rest_of(order, width, parts_ref, self_ref, near_ref, chosen_ref):
    boxes, panels = self_ref.shape
    count = parts_ref.shape[0] // 2
    index = lax.axis_index("box")
    rows = width * boxes
    pieces = [joined(order, parts_ref, jnp.clip(index + step, 0, count - 1))[:rows] for step in (-1, 0, 1)]
    near = near_of(near_ref, chosen_ref, extended_of(pieces, index, count, boxes), boxes, width)
    field = pieces[1]
    diagonal = ((self_ref[...] - SHIFT)[None] * field.reshape(width, boxes, panels)).reshape(rows, panels)
    return near + diagonal


def third_kernel(
    first,
    second,
    width,
    band,
    own_ref,
    other_ref,
    across_ref,
    corner_ref,
    parts_ref,
    expand_ref,
    table_ref,
    self_ref,
    near_ref,
    chosen_ref,
    field_ref,
    rhs_ref,
    out_ref,
):
    boxes, terms, panels = expand_ref.shape
    core, side = lax.axis_index("core"), lax.axis_index("side")
    rows = width * boxes
    count = parts_ref.shape[0] // 2
    if second is None:
        blocks = parts_ref[:, rows:, :].astype(FULL).reshape(count, 2, -1, LANES)
        blocks = blocks[:, 0] + blocks[:, 1]
    else:
        blocks = jnp.stack([joined(second, parts_ref, place)[rows:] for place in first])
    sources = sources_of(blocks)
    bands = (own_ref, other_ref, across_ref, corner_ref)
    total = local_of(first, bands, table_ref, sources, band)
    halves = [total[:, : 2 * band], total[:, 2 * band :]]
    halves = [jnp.where(core == 0, half, pltpu.roll(half, band, 1)) for half in halves]
    local = jnp.concatenate(
        [jnp.where(side == 0, halves[0], halves[1]), jnp.where(side == 0, halves[1], halves[0])], axis=1
    ).astype(HALF)
    last = rest_of(second, width, parts_ref, self_ref, near_ref, chosen_ref) + far_of(local, expand_ref, 0)
    field = field_ref[...]
    right = rhs_ref[pl.ds(core * width, width)].reshape(rows, panels)
    spots = lax.broadcasted_iota(jnp.int32, (8, panels), 0)
    lanes = lax.broadcasted_iota(jnp.int32, (8, panels), 1)
    result = jnp.zeros((8, panels), FULL)
    pairs = ((right, right), (right, field), (field, field), (right, last), (field, last), (last, last))
    for number, (one, two) in enumerate(pairs):
        product = one * two
        for rhs in range(width):
            total = jnp.sum(product[rhs * boxes : (rhs + 1) * boxes])
            mine = (spots == number) & (lanes // (panels // width) == rhs)
            result = jnp.where(mine, total, result)

    def put(target):
        out_ref[target] = result

    each(out_ref.shape[0], put)


def last_kernel(order, width, sums_ref, field_ref, other_ref, rhs_ref, out_ref):
    core = lax.axis_index("core")
    rows, panels = field_ref.shape
    boxes = rows // width
    fields = (field_ref[...], other_ref[...])
    part = panels // width
    lanes = lax.broadcasted_iota(jnp.int32, (1, panels), 1)
    for group in range(2):
        total = fold(
            sums_ref.shape[0] // 2,
            lambda number, state: state + sums_ref[spot(order, 2 * number + group)],
            jnp.zeros(sums_ref.shape[1:], FULL),
        )
        rr, ru, uu, rw, uw, ww = (total[number : number + 1] for number in range(6))
        slope = ru / rr
        norm = uu - slope * ru
        first_row = rw - slope * ru
        scale = lax.rsqrt(rr) * lax.rsqrt(norm)
        h11 = slope + SHIFT
        h21 = jnp.sqrt(norm / rr)
        h12 = first_row * scale
        h22 = (uw - slope * uu - slope * first_row) / norm
        image = (ww - 2.0 * slope * uw + slope * slope * uu) / norm
        gram_aa = h11 * h11 + h21 * h21
        gram_ab = h11 * h12 + h21 * (h22 + SHIFT)
        gram_bb = image + 2.0 * SHIFT * h22 + SHIFT * SHIFT
        beta = jnp.sqrt(rr)
        right_a, right_b = beta * h11, beta * h12
        determinant = gram_aa * gram_bb - gram_ab * gram_ab
        coef_a = (gram_bb * right_a - gram_ab * right_b) / determinant
        coef_b = (gram_aa * right_b - gram_ab * right_a) / determinant
        weight = coef_b * lax.rsqrt(norm)
        first = coef_a / beta - weight * slope
        chosen = jnp.where(core == group, fields[0], fields[1])
        for rhs in range(width):
            def wide(value):
                inside = jnp.where(lanes // part == rhs, value, 0.0)
                spread = inside
                for step in range(1, width):
                    spread = spread + pltpu.roll(inside, step * part, 1)
                return spread

            place = group * width + rhs
            out_ref[place] = wide(first) * rhs_ref[place] + wide(weight) * chosen[rhs * boxes : (rhs + 1) * boxes]


def call(kernel, outs, *args, fixed=0, scratch=(), flops=0, limit=16):
    vmem = pl.BlockSpec(memory_space=pltpu.VMEM)
    many = isinstance(outs, list)
    held = len(args) - fixed
    args = [
        value if number < held else pltpu.with_memory_space_constraint(value, pltpu.HBM)
        for number, value in enumerate(args)
    ]
    return pl.pallas_call(
        kernel,
        out_shape=outs,
        in_specs=[vmem] * held + [pl.BlockSpec(memory_space=pltpu.HBM)] * fixed,
        out_specs=[vmem] * len(outs) if many else vmem,
        scratch_shapes=list(scratch),
        compiler_params=pltpu.CompilerParams(vmem_limit_bytes=limit * 1024 * 1024),
        cost_estimate=pl.CostEstimate(flops=flops, bytes_accessed=0, transcendentals=0) if flops else None,
    )(*args)


def per_device(
    rhs_field, self_coef, expand, near_ops, class_ops, near_src, send_rows, list_slot, list_class
):
    count = lax.axis_size("box")
    boxes, terms, panels = expand.shape
    width = rhs_field.shape[0] // 2
    rows = width * boxes
    band = class_ops.shape[1]
    cap = send_rows.shape[2]
    parts = terms // LANES
    area = -(-(cap * width * parts) // 8) * 8
    low = parts * band
    swap = [(0, 1), (1, 0)]
    first, second, third = FIRST.get(count), SECOND.get(2 * count), THIRD.get(2 * count)
    shape = jax.ShapeDtypeStruct
    send = jnp.swapaxes(send_rows, 1, 2)[0]
    slot, label = list_slot.T, list_class.T
    block = shape((rows, panels), FULL)
    kernel = functools.partial(call, limit=16 if count <= 16 else 56)

    slots, picks, kept, near, chosen, table = kernel(
        functools.partial(first_kernel, first, width),
        [
            shape((count, low + rows // 2 + area, LANES), HALF),
            shape((count * area, parts * rows), HALF),
            SLOT(expand.shape, HALF),
            SLOT(near_ops.shape, HALF),
            shape((near_ops.shape[0] * boxes, 3 * boxes), HALF),
            shape((-(-count // 8), rows, min(count, 8) * count * cap * width), HALF),
        ],
        rhs_field, expand, class_ops, send, near_ops, near_src, slot, label,
        fixed=8,
        scratch=[
            pltpu.VMEM((width,) + rhs_field.shape[1:], FULL),
            pltpu.VMEM(class_ops.shape, HALF),
            pltpu.SMEM(send.shape, jnp.int32),
            pltpu.VMEM((count * area, parts * rows), FULL),
            pltpu.VMEM(near_src.shape, jnp.int32),
            pltpu.VMEM(slot.shape, jnp.int32),
            pltpu.VMEM(label.shape, jnp.int32),
            pltpu.SemaphoreType.DMA((9,)),
        ],
    )
    own = exchange(slots, "box", first)
    bands = own[:, :low]
    other = lax.ppermute(bands, "core", swap)
    across = lax.ppermute(bands, "side", swap)
    corner = lax.ppermute(across, "core", swap)
    images = kernel(
        functools.partial(second_kernel, first, second, width, band),
        shape((2 * count, rows + area, LANES), HALF),
        own, other, rhs_field, self_coef, near, chosen, kept, table, picks,
    )
    images = exchange(images, ("box", "side"), second)
    field = kernel(functools.partial(field_kernel, second), block, images)
    field_other = lax.ppermute(field, "core", swap)
    sums = kernel(
        functools.partial(third_kernel, first, second, width, band),
        SLOT((2 * count, 8, panels), FULL),
        bands, other, across, corner, images, kept, table, self_coef, near, chosen, field, rhs_field,
    )
    sums, field_other = lax.optimization_barrier((sums, field_other))
    sums = exchange(sums, ("box", "core"), third)
    return kernel(
        functools.partial(last_kernel, third, width),
        shape(rhs_field.shape, FULL),
        sums, field, field_other, rhs_field,
    )


def solution(mesh):
    count, levels = mesh.devices.shape
    finer = Mesh(mesh.devices.reshape(count, levels // 2, 2), ("box", "side", "core"))
    return jax.shard_map(
        per_device,
        mesh=finer,
        in_specs=(
            P(None, "box", None),
            P("box", None),
            P("box", None, None),
            P(),
            P("box", ("side", "core"), None),
            P("box", None),
            P("box", None, None),
            P("box", None),
            P("box", None),
        ),
        out_specs=P(None, "box", None),
        check_vma=False,
    )
```

```python
import functools

import jax
import jax.numpy as jnp
from jax import lax
from jax.experimental import pallas as pl
from jax.experimental.pallas import tpu as pltpu
from jax.sharding import Mesh, PartitionSpec as P

SHIFT = 3.0
LANES = 128
HALF = jnp.bfloat16
FULL = jnp.float32
SLOT = pltpu.VMEM
FIRST = {8: (5, 7, 0, 4, 6, 3, 1, 2)}
SECOND = {16: (10, 8, 3, 7, 2, 14, 5, 1, 11, 9, 15, 13, 12, 6, 4, 0)}
THIRD = {16: (11, 9, 13, 8, 14, 5, 7, 4, 12, 1, 15, 3, 0, 6, 2, 10)}


def spot(order, member):
    if order is None:
        return member
    if isinstance(member, int):
        return order.index(member)
    result = jnp.zeros_like(member)
    for number, value in enumerate(order):
        result = jnp.where(member == value, number, result)
    return result


def exchange(value, axes, order):
    groups = None if order is None else [list(order)]
    return lax.all_to_all(value, axes, 0, 0, tiled=True, axis_index_groups=groups)


def each(count, body):
    if count <= 32:
        for number in range(count):
            body(number)
    else:
        lax.fori_loop(0, count, lambda number, state: (body(number), state)[1], 0)


def fold(count, body, state):
    if count <= 32:
        for number in range(count):
            state = body(number, state)
        return state
    return lax.fori_loop(0, count, body, state)


def dot_nt(left, right):
    return lax.dot_general(left, right, (((1,), (1,)), ((), ())), preferred_element_type=FULL)


def dot_nn(left, right):
    return lax.dot_general(left, right, (((1,), (0,)), ((), ())), preferred_element_type=FULL)


def own_rows(values, result, box, boxes):
    row = lax.broadcasted_iota(jnp.int32, result.shape, 0)
    return jnp.where(row % boxes == box, values, result)


def multipoles_of(field, expand_ref):
    boxes, terms, _ = expand_ref.shape
    result = jnp.zeros((field.shape[0], terms), FULL)
    for box in range(boxes):
        result = own_rows(dot_nt(field, expand_ref[box]), result, box, boxes)
    return result


def send_table(order, send_ref, out_ref, boxes, width, parts):
    cap, targets = send_ref.shape
    area = out_ref.shape[0] // targets
    row = lax.broadcasted_iota(jnp.int32, (area, out_ref.shape[1]), 0)
    column = lax.broadcasted_iota(jnp.int32, (area, out_ref.shape[1]), 1)
    start = jnp.where(row < cap * width * parts, (row // cap) * boxes, -boxes)

    def put(target):
        place = start
        for turn in range(cap):
            place = jnp.where(row % cap == turn, start + send_ref[turn, target], place)
        begin = spot(order, target) * area
        if not isinstance(target, int):
            begin = pl.multiple_of(begin, area)
        out_ref[pl.ds(begin, area), :] = jnp.where(place == column, 1.0, 0.0)

    each(targets, put)


def sent_of(multipoles, table):
    half = multipoles.astype(HALF)
    parts = half.shape[1] // LANES
    stacked = jnp.concatenate([half[:, part * LANES : (part + 1) * LANES] for part in range(parts)], axis=0)
    return dot_nn(table, stacked)


def far_of(local, expand_ref, offset):
    boxes = expand_ref.shape[0]
    row = lax.broadcasted_iota(jnp.int32, local.shape, 0)
    left = [jnp.where(row % boxes == box, local, jnp.zeros_like(local)) for box in range(boxes)]
    right = [expand_ref[box, pl.ds(offset, local.shape[1]), :] for box in range(boxes)]
    return dot_nn(jnp.concatenate(left, axis=1), jnp.concatenate(right, axis=0))


def near_of(near_ref, chosen_ref, extended, boxes, width):
    picked = dot_nn(chosen_ref[...], extended).astype(HALF)
    classes = near_ref.shape[0]
    result = jnp.zeros((width * boxes, near_ref.shape[1]), FULL)
    for first in range(0, classes, 2):
        group = range(first, min(first + 2, classes))
        left = [
            jnp.concatenate(
                [
                    picked[number * boxes : (number + 1) * boxes, rhs * LANES : (rhs + 1) * LANES]
                    for number in group
                ],
                axis=1,
            )
            for rhs in range(width)
        ]
        right = [near_ref[number] for number in group]
        result = result + dot_nt(jnp.concatenate(left, axis=0), jnp.concatenate(right, axis=1))
    return result


def sources_of(blocks):
    count, area, panels = blocks.shape
    half = area // 2
    pairs = blocks.reshape(count // 2, 2, area, panels)
    low, high = pairs[:, 0], pairs[:, 1]
    row = lax.broadcasted_iota(jnp.int32, low.shape, 1)
    moved_low, moved_high = pltpu.roll(low, half, 1), pltpu.roll(high, half, 1)
    first = jnp.where(row < half, low, moved_high).reshape(-1, panels)
    second = jnp.where(row < half, moved_low, high).reshape(-1, panels)
    return jnp.concatenate([first, second], axis=1).astype(HALF)


def local_of(order, bands, table_ref, sources, band):
    classes = bands[0].shape[0]
    group = classes // table_ref.shape[0]
    parts = sources.shape[1] // LANES

    def add(number, total):
        images = []
        for turn in range(group):
            right = [
                jnp.concatenate(
                    [
                        ref[spot(order, number * group + turn), part * band : (part + 1) * band, :]
                        for part in range(parts)
                    ],
                    axis=1,
                )
                for ref in bands
            ]
            images.append(dot_nt(sources, jnp.concatenate(right, axis=0)))
        images = jnp.concatenate(images, axis=0)
        upper = images.astype(HALF)
        lower = (images - upper.astype(FULL)).astype(HALF)
        table = table_ref[number]
        return total + (dot_nn(table, upper) + dot_nn(table, lower))

    return fold(table_ref.shape[0], add, jnp.zeros((table_ref.shape[1], len(bands) * band), FULL))


def extended_of(pieces, index, count, boxes):
    low = jnp.where(index > 0, pieces[0], jnp.zeros_like(pieces[0]))
    high = jnp.where(index < count - 1, pieces[2], jnp.zeros_like(pieces[2]))
    width = low.shape[0] // boxes
    columns = [
        jnp.concatenate([piece[rhs * boxes : (rhs + 1) * boxes] for piece in (low, pieces[1], high)], axis=0)
        for rhs in range(width)
    ]
    return jnp.concatenate(columns, axis=1).astype(HALF)


def fetch(pairs, signals):
    copies = [
        pltpu.make_async_copy(source, target, signals.at[number])
        for number, (source, target) in enumerate(pairs)
    ]
    for copy in copies:
        copy.start()
    return copies


def near_table(source_ref, chosen_ref):
    boxes, classes = source_ref.shape
    spots = lax.broadcasted_iota(jnp.int32, (boxes, chosen_ref.shape[1]), 1)
    for number in range(classes):
        match = source_ref[:, number : number + 1] == spots
        chosen_ref[number * boxes : (number + 1) * boxes, :] = jnp.where(match, 1.0, 0.0).astype(HALF)


def list_table(order, cap, width, kinds, slot_ref, label_ref, table_ref):
    boxes = slot_ref.shape[1]
    groups, rows, columns = table_ref.shape
    slots, labels = slot_ref[...], label_ref[...]
    places = spot(order, slots // cap) * (cap * width) + slots % cap
    group = kinds // groups
    received = columns // group

    def put(number):
        blocks = []
        for turn in range(group):
            place = jnp.max(jnp.where(labels == number * group + turn, places + 1, 0), axis=0, keepdims=True) - 1
            place = jnp.concatenate([jnp.where(place >= 0, place + rhs * cap, -1) for rhs in range(width)], axis=1)
            spot = lax.broadcasted_iota(jnp.int32, (received, rows), 0)
            blocks.append(jnp.where(place == spot, 1.0, 0.0))
        table_ref[number] = jnp.concatenate(blocks, axis=0).T.astype(HALF)

    each(groups, put)


def first_kernel(
    order,
    width,
    rhs_hbm,
    expand_hbm,
    class_hbm,
    send_hbm,
    near_hbm,
    source_hbm,
    slot_hbm,
    label_hbm,
    out_ref,
    picks_ref,
    expand_ref,
    near_ref,
    chosen_ref,
    table_ref,
    rhs_ref,
    class_ref,
    send_ref,
    wide_ref,
    source_ref,
    slot_ref,
    label_ref,
    signals,
):
    boxes, terms, panels = expand_ref.shape
    core, side = lax.axis_index("core"), lax.axis_index("side")
    step = boxes // 2
    pairs = [
        (send_hbm, send_ref),
        (rhs_hbm.at[pl.ds(core * width, width)], rhs_ref),
        (class_hbm, class_ref),
        (source_hbm, source_ref),
        (slot_hbm, slot_ref),
        (label_hbm, label_ref),
    ]
    for chunk in range(2):
        part = pl.ds(chunk * step, step)
        pairs.append((expand_hbm.at[part], expand_ref.at[part]))
    pairs.append((near_hbm, near_ref))
    copies = fetch(pairs, signals)
    copies[0].wait()
    send_table(order, send_ref, wide_ref, boxes, width, terms // LANES)
    picks_ref[...] = wide_ref[...].astype(HALF)
    band = class_ref.shape[1]
    low = (terms // LANES) * band
    high = low + width * (boxes // 2)
    copies[1].wait()
    copies[2].wait()
    shown = rhs_ref[:, pl.ds(side * (boxes // 2), boxes // 2), :].reshape(high - low, panels).astype(HALF)
    field = rhs_ref[...].reshape(width * boxes, panels).astype(HALF)
    operators = jnp.concatenate(
        [class_ref[0][:, part * LANES : (part + 1) * LANES] for part in range(terms // LANES)], axis=0
    )

    def put(target):
        place = spot(order, target)
        out_ref[place, :low, :] = operators
        out_ref[place, low:high, :] = shown

    each(out_ref.shape[0], put)
    for copy in copies[3:6]:
        copy.wait()
    near_table(source_ref, chosen_ref)
    list_table(order, send_ref.shape[0], width, out_ref.shape[0], slot_ref, label_ref, table_ref)
    result = jnp.zeros((width * boxes, terms), FULL)
    for box in range(boxes):
        if box % step == 0:
            copies[6 + box // step].wait()
        result = own_rows(dot_nt(field, expand_ref[box]), result, box, boxes)
    sent = sent_of(result, picks_ref[...]).astype(HALF)
    out_ref[:, high:, :] = sent.reshape(out_ref.shape[0], -1, LANES)
    copies[8].wait()


def base_of(order, width, low, own_ref, rhs_ref, self_ref, near_ref, chosen_ref):
    boxes, panels = self_ref.shape
    count = own_ref.shape[0]
    core, side, index = lax.axis_index("core"), lax.axis_index("side"), lax.axis_index("box")
    half = boxes // 2
    empty = jnp.zeros((half, panels), FULL)
    pieces = []
    for step in (-1, 0, 1):
        shown = own_ref[spot(order, jnp.clip(index + step, 0, count - 1)), low : low + width * half, :].astype(FULL)
        rows = []
        for rhs in range(width):
            part = shown[rhs * half : (rhs + 1) * half]
            rows += [jnp.where(side == 0, part, empty), jnp.where(side == 0, empty, part)]
        pieces.append(jnp.concatenate(rows, axis=0))
    near = near_of(near_ref, chosen_ref, extended_of(pieces, index, count, boxes), boxes, width)
    field = rhs_ref[pl.ds(core * width, width)]
    diagonal = ((self_ref[...] - SHIFT)[None] * field).reshape(width * boxes, panels)
    return near + jnp.where(side == 0, diagonal, 0.0)


def second_kernel(
    first,
    second,
    width,
    band,
    own_ref,
    other_ref,
    rhs_ref,
    self_ref,
    near_ref,
    chosen_ref,
    expand_ref,
    table_ref,
    send_ref,
    out_ref,
):
    boxes, terms, panels = expand_ref.shape
    count = own_ref.shape[0]
    core, side = lax.axis_index("core"), lax.axis_index("side")
    rows = width * boxes
    high = (terms // LANES) * band + rows // 2
    sources = sources_of(own_ref[:, high:, :].astype(FULL))
    total = local_of(first, (own_ref, other_ref), table_ref, sources, band)
    local = jnp.where(core == 0, total, pltpu.roll(total, band, 1)).astype(HALF)
    base = base_of(first, width, (terms // LANES) * band, own_ref, rhs_ref, self_ref, near_ref, chosen_ref)
    image = far_of(local, expand_ref, side * (terms // 2)) + base
    half = image.astype(HALF)
    sent = sent_of(multipoles_of(half, expand_ref), send_ref[...]).astype(HALF).reshape(count, -1, LANES)

    def put(target):
        for part in range(2):
            place = spot(second, 2 * target + part)
            out_ref[place, :rows, :] = half
            out_ref[place, rows:, :] = sent[spot(first, target)]

    if second is None:
        out_ref[...] = jnp.concatenate(
            [jnp.broadcast_to(half[None, None], (count, 2, rows, LANES)), jnp.stack([sent, sent], axis=1)], axis=2
        ).reshape(out_ref.shape)
    else:
        each(count, put)


def joined(order, parts_ref, place):
    first, second = spot(order, 2 * place), spot(order, 2 * place + 1)
    return parts_ref[first].astype(FULL) + parts_ref[second].astype(FULL)


def field_kernel(order, parts_ref, out_ref):
    out_ref[...] = joined(order, parts_ref, lax.axis_index("box"))[: out_ref.shape[0]]


def rest_of(order, width, parts_ref, self_ref, near_ref, chosen_ref):
    boxes, panels = self_ref.shape
    count = parts_ref.shape[0] // 2
    index = lax.axis_index("box")
    rows = width * boxes
    pieces = [joined(order, parts_ref, jnp.clip(index + step, 0, count - 1))[:rows] for step in (-1, 0, 1)]
    near = near_of(near_ref, chosen_ref, extended_of(pieces, index, count, boxes), boxes, width)
    field = pieces[1]
    diagonal = ((self_ref[...] - SHIFT)[None] * field.reshape(width, boxes, panels)).reshape(rows, panels)
    return near + diagonal


def third_kernel(
    first,
    second,
    width,
    band,
    own_ref,
    other_ref,
    across_ref,
    corner_ref,
    parts_ref,
    expand_ref,
    table_ref,
    self_ref,
    near_ref,
    chosen_ref,
    field_ref,
    rhs_ref,
    out_ref,
):
    boxes, terms, panels = expand_ref.shape
    core, side = lax.axis_index("core"), lax.axis_index("side")
    rows = width * boxes
    count = parts_ref.shape[0] // 2
    if second is None:
        blocks = parts_ref[:, rows:, :].astype(FULL).reshape(count, 2, -1, LANES)
        blocks = blocks[:, 0] + blocks[:, 1]
    else:
        blocks = jnp.stack([joined(second, parts_ref, place)[rows:] for place in first])
    sources = sources_of(blocks)
    bands = (own_ref, other_ref, across_ref, corner_ref)
    total = local_of(first, bands, table_ref, sources, band)
    halves = [total[:, : 2 * band], total[:, 2 * band :]]
    halves = [jnp.where(core == 0, half, pltpu.roll(half, band, 1)) for half in halves]
    local = jnp.concatenate(
        [jnp.where(side == 0, halves[0], halves[1]), jnp.where(side == 0, halves[1], halves[0])], axis=1
    ).astype(HALF)
    last = rest_of(second, width, parts_ref, self_ref, near_ref, chosen_ref) + far_of(local, expand_ref, 0)
    field = field_ref[...]
    right = rhs_ref[pl.ds(core * width, width)].reshape(rows, panels)
    spots = lax.broadcasted_iota(jnp.int32, (8, panels), 0)
    lanes = lax.broadcasted_iota(jnp.int32, (8, panels), 1)
    rows_of = [jnp.zeros((8, panels), FULL) for _ in range(width)]
    pairs = ((right, right), (right, field), (field, field), (right, last), (field, last), (last, last))
    for number, (one, two) in enumerate(pairs):
        product = one * two
        for rhs in range(width):
            row = jnp.sum(product[rhs * boxes : (rhs + 1) * boxes], axis=0, keepdims=True)
            rows_of[rhs] = jnp.where(spots == number, row, rows_of[rhs])
    result = jnp.zeros((8, panels), FULL)
    for rhs in range(width):
        total = jnp.sum(rows_of[rhs], axis=1, keepdims=True)
        result = jnp.where(lanes // (panels // width) == rhs, total, result)

    def put(target):
        out_ref[target] = result

    each(out_ref.shape[0], put)


def last_kernel(order, width, sums_ref, field_ref, other_ref, rhs_ref, out_ref):
    core = lax.axis_index("core")
    rows, panels = field_ref.shape
    boxes = rows // width
    fields = (field_ref[...], other_ref[...])
    part = panels // width
    lanes = lax.broadcasted_iota(jnp.int32, (1, panels), 1)
    for group in range(2):
        total = fold(
            sums_ref.shape[0] // 2,
            lambda number, state: state + sums_ref[spot(order, 2 * number + group)],
            jnp.zeros(sums_ref.shape[1:], FULL),
        )
        rr, ru, uu, rw, uw, ww = (total[number : number + 1] for number in range(6))
        slope = ru / rr
        norm = uu - slope * ru
        first_row = rw - slope * ru
        scale = lax.rsqrt(rr) * lax.rsqrt(norm)
        h11 = slope + SHIFT
        h21 = jnp.sqrt(norm / rr)
        h12 = first_row * scale
        h22 = (uw - slope * uu - slope * first_row) / norm
        image = (ww - 2.0 * slope * uw + slope * slope * uu) / norm
        gram_aa = h11 * h11 + h21 * h21
        gram_ab = h11 * h12 + h21 * (h22 + SHIFT)
        gram_bb = image + 2.0 * SHIFT * h22 + SHIFT * SHIFT
        beta = jnp.sqrt(rr)
        right_a, right_b = beta * h11, beta * h12
        determinant = gram_aa * gram_bb - gram_ab * gram_ab
        coef_a = (gram_bb * right_a - gram_ab * right_b) / determinant
        coef_b = (gram_aa * right_b - gram_ab * right_a) / determinant
        weight = coef_b * lax.rsqrt(norm)
        first = coef_a / beta - weight * slope
        chosen = jnp.where(core == group, fields[0], fields[1])
        for rhs in range(width):
            def wide(value):
                inside = jnp.where(lanes // part == rhs, value, 0.0)
                spread = inside
                for step in range(1, width):
                    spread = spread + pltpu.roll(inside, step * part, 1)
                return spread

            place = group * width + rhs
            out_ref[place] = wide(first) * rhs_ref[place] + wide(weight) * chosen[rhs * boxes : (rhs + 1) * boxes]


def call(kernel, outs, *args, fixed=0, scratch=(), flops=0, limit=16):
    vmem = pl.BlockSpec(memory_space=pltpu.VMEM)
    many = isinstance(outs, list)
    held = len(args) - fixed
    args = [
        value if number < held else pltpu.with_memory_space_constraint(value, pltpu.HBM)
        for number, value in enumerate(args)
    ]
    return pl.pallas_call(
        kernel,
        out_shape=outs,
        in_specs=[vmem] * held + [pl.BlockSpec(memory_space=pltpu.HBM)] * fixed,
        out_specs=[vmem] * len(outs) if many else vmem,
        scratch_shapes=list(scratch),
        compiler_params=pltpu.CompilerParams(vmem_limit_bytes=limit * 1024 * 1024),
        cost_estimate=pl.CostEstimate(flops=flops, bytes_accessed=0, transcendentals=0) if flops else None,
    )(*args)


def per_device(
    rhs_field, self_coef, expand, near_ops, class_ops, near_src, send_rows, list_slot, list_class
):
    count = lax.axis_size("box")
    boxes, terms, panels = expand.shape
    width = rhs_field.shape[0] // 2
    rows = width * boxes
    band = class_ops.shape[1]
    cap = send_rows.shape[2]
    parts = terms // LANES
    area = -(-(cap * width * parts) // 8) * 8
    low = parts * band
    swap = [(0, 1), (1, 0)]
    first, second, third = FIRST.get(count), SECOND.get(2 * count), THIRD.get(2 * count)
    shape = jax.ShapeDtypeStruct
    send = jnp.swapaxes(send_rows, 1, 2)[0]
    slot, label = list_slot.T, list_class.T
    block = shape((rows, panels), FULL)
    kernel = functools.partial(call, limit=16 if count <= 16 else 56)

    slots, picks, kept, near, chosen, table = kernel(
        functools.partial(first_kernel, first, width),
        [
            shape((count, low + rows // 2 + area, LANES), HALF),
            shape((count * area, parts * rows), HALF),
            SLOT(expand.shape, HALF),
            SLOT(near_ops.shape, HALF),
            shape((near_ops.shape[0] * boxes, 3 * boxes), HALF),
            shape((-(-count // 8), rows, min(count, 8) * count * cap * width), HALF),
        ],
        rhs_field, expand, class_ops, send, near_ops, near_src, slot, label,
        fixed=8,
        scratch=[
            pltpu.VMEM((width,) + rhs_field.shape[1:], FULL),
            pltpu.VMEM(class_ops.shape, HALF),
            pltpu.SMEM(send.shape, jnp.int32),
            pltpu.VMEM((count * area, parts * rows), FULL),
            pltpu.VMEM(near_src.shape, jnp.int32),
            pltpu.VMEM(slot.shape, jnp.int32),
            pltpu.VMEM(label.shape, jnp.int32),
            pltpu.SemaphoreType.DMA((9,)),
        ],
    )
    own = exchange(slots, "box", first)
    bands = own[:, :low]
    other = lax.ppermute(bands, "core", swap)
    across = lax.ppermute(bands, "side", swap)
    corner = lax.ppermute(across, "core", swap)
    images = kernel(
        functools.partial(second_kernel, first, second, width, band),
        shape((2 * count, rows + area, LANES), HALF),
        own, other, rhs_field, self_coef, near, chosen, kept, table, picks,
    )
    images = exchange(images, ("box", "side"), second)
    field = kernel(functools.partial(field_kernel, second), block, images)
    field_other = lax.ppermute(field, "core", swap)
    sums = kernel(
        functools.partial(third_kernel, first, second, width, band),
        SLOT((2 * count, 8, panels), FULL),
        bands, other, across, corner, images, kept, table, self_coef, near, chosen, field, rhs_field,
    )
    sums, field_other = lax.optimization_barrier((sums, field_other))
    sums = exchange(sums, ("box", "core"), third)
    return kernel(
        functools.partial(last_kernel, third, width),
        shape(rhs_field.shape, FULL),
        sums, field, field_other, rhs_field,
    )


def solution(mesh):
    count, levels = mesh.devices.shape
    finer = Mesh(mesh.devices.reshape(count, levels // 2, 2), ("box", "side", "core"))
    return jax.shard_map(
        per_device,
        mesh=finer,
        in_specs=(
            P(None, "box", None),
            P("box", None),
            P("box", None, None),
            P(),
            P("box", ("side", "core"), None),
            P("box", None),
            P("box", None, None),
            P("box", None),
            P("box", None),
        ),
        out_specs=P(None, "box", None),
        check_vma=False,
    )
```
